256 devices in a mesh: seq: 32 (over x, z), head: 8 (over y, core).
Axes of the slice: x: 4, y: 4, z: 8, core: 2. Of those that a mesh axis runs over, the one named last changes fastest.
Arguments:
- queries: bfloat16 [14336, 4096], P('seq', 'head'), may hold values from -9 to 9
- cache_keys: bfloat16 [128, 128, 4096], P('seq', None, 'head'), may hold values from -9 to 9
- cache_values: bfloat16 [128, 128, 4096], P('seq', None, 'head'), may hold values from -5 to 5
- owners: int32 [224, 2], P('seq'), may hold values from 0 to 31, all different within a row; in each aligned block of 7 rows (0 to 6, 7 to 13, ...) at most 2 rows name the same one
- slots: int32 [224, 2], P('seq'), may hold values from 0 to 3
- out_weight: bfloat16 [4096, 4096], P(None, 'head'), may hold values from -0.09375 to 0.09375
- cotangent: bfloat16 [14336, 4096], P('seq', 'head'), may hold values from -6 to 6
Outputs:
- mixed: bfloat16 [14336, 4096], P('seq', 'head')
- grad_weight: bfloat16 [4096, 4096], P('seq', 'head')
- grad_keys: bfloat16 [128, 128, 4096], P('seq', None, 'head')
- grad_values: bfloat16 [128, 128, 4096], P('seq', None, 'head')
The draws below stay inside these ranges and needn't reach their ends.
Inputs may be any that keep to these rules, and one draw needn't show every extreme that they name: The 2 neighbours of a span lie on different owners; among the 7 spans of one device at most 2 neighbours name one owner, and some device names one owner exactly 2 times.
All inputs are finite; a program needn't handle non-finite values.
Results may differ from the reference program's by a relative error of at most 0.033.
Values may be sent and summed in bfloat16 or wider, within the bound.
A program may use at most 192 MiB of HBM per device.

```python
import math
import jax
import jax.numpy as jnp
import numpy as np
from jax import lax

D = 4096
HEADS = 32
HEAD_DIM = 128
SPAN = 64
NEIGH_LEN = 128
TOP = 2
TOK_DEV = 448
E_DEV = 4
HD = 4096
SPANS_DEV = 7
CAP = 2
TOKENS = 14336
SPANS = 224
ENTRIES = 128
N_SEQ = 32
N_HEAD = 8


def draw_queries(key, part):
    key = jax.random.fold_in(key, 3)
    first = jax.random.fold_in(key, 0)
    return jnp.clip(jax.random.normal(first, (TOKENS, HEADS * HEAD_DIM), jnp.float32), -4.5, 4.5).astype(jnp.bfloat16)


def draw_cache_keys(key, part):
    key = jax.random.fold_in(key, 5)
    return jnp.clip(jax.random.normal(key, (ENTRIES, NEIGH_LEN, HEADS * HEAD_DIM), jnp.float32), -4.5, 4.5).astype(jnp.bfloat16)


def with_ends(array, key, least, top_value):
    spot = [jax.random.randint(jax.random.fold_in(key, axis), (), 0, length) for axis, length in enumerate(array.shape)]
    widest = array.shape.index(max(array.shape))
    next_to = spot[:widest] + [(spot[widest] + 1) % array.shape[widest]] + spot[widest + 1:]
    return array.at[tuple(spot)].set(least).at[tuple(next_to)].set(top_value)


def steps_of(rng, extent, cuts, low, top_value):
    factor_of, own = 1.0, jax.random.fold_in(rng, 6)
    for axis_at, blocks in cuts:
        heights = jnp.exp(jax.random.uniform(jax.random.fold_in(own, axis_at), (blocks,), jnp.float32, low / len(cuts), top_value / len(cuts)))
        factor_of = factor_of * jnp.repeat(heights, extent[axis_at] // blocks).reshape([-1 if axis == axis_at else 1 for axis in range(len(extent))])
    return factor_of


def routed_block(stream_key, own, number, rows, number_of, top, limit, lean):
    order = jax.random.permutation(stream_key, number_of)
    packed, ordinary = load_shares(number_of, rows * top, limit, lean, True), load_shares(number_of, rows * top, limit, lean, False)
    places = jnp.arange(number_of)

    def named(lengths, rotation):
        used = int((lengths > 0).sum())
        fixed = max(1, used // 4)
        shifted = fixed + (places - fixed + rotation * (used - fixed)) % max(1, number_of - fixed)
        return jnp.zeros((number_of,), jnp.int32).at[order[jnp.where(places < fixed, places, shifted)]].set(jnp.asarray(lengths, jnp.int32))

    lengths = jnp.where(number % 4 == 0, named(packed, number // 4), named(ordinary, number - number // 4 - 1))
    mixed = jax.random.permutation(jax.random.fold_in(own, 3), number_of)
    donor, taker = mixed[0:number_of // 2 * 2:2], mixed[1:number_of // 2 * 2:2]
    margin = jnp.minimum(lengths[donor] - 1, limit - lengths[taker]) // 2
    margin = jnp.where((donor == order[0]) | (taker == order[0]) | (lengths[taker] == 0), 0, jnp.maximum(margin, 0))
    shifted = jax.random.randint(jax.random.fold_in(own, 4), (number_of // 2,), 0, 1 << 20) % (margin + 1)
    lengths = lengths.at[donor].add(-shifted).at[taker].add(shifted)
    items = jnp.searchsorted(jnp.cumsum(lengths), jnp.arange(rows * top), side="right").astype(jnp.int32)
    listing = items.reshape(top, rows).T
    listing = listing[jax.random.permutation(jax.random.fold_in(own, 1), rows)]
    rotation = jax.random.randint(jax.random.fold_in(own, 2), (rows, 1), 0, top)
    return jnp.take_along_axis(listing, (jnp.arange(top)[None, :] + rotation) % top, axis=1)


def load_shares(amount, total, limit, lean, full):
    loads = [(1 << 20) // math.isqrt(rank ** lean) + 1 for rank in range(1, amount + 1)]
    largest = limit if full else min(limit, max(-(-total // amount), total * loads[0] // sum(loads)))
    least = 1 if total - largest >= amount - 1 else 0
    holding, surplus = [largest] + [least] * (amount - 1), total - largest - least * (amount - 1)
    while surplus > 0:
        movable = [i for i in range(1, amount) if holding[i] < largest] or [i for i in range(1, amount) if holding[i] < limit]
        pool, left = sum([loads[i] for i in movable]), surplus
        for i in movable:
            addition = min(limit - holding[i], max(1, left * loads[i] // pool), surplus)
            holding[i] = holding[i] + addition
            surplus = surplus - addition
    return np.array(holding)


def centred(key, extent, spread, bound, cuts=(), kind=jnp.bfloat16):
    array = spread * jax.random.normal(key, extent, jnp.float32)
    if cuts:
        array = array * steps_of(key, extent, cuts, -0.22, 0.18)
    return jnp.clip(array, -bound, bound).astype(kind)


def setup_inputs(seed: int = 0) -> dict:
    seeds = jax.random.split(jax.random.key(seed), 8)
    queries = draw_queries(jax.random.fold_in(seeds[7], 71), 0)
    cache_keys = draw_cache_keys(jax.random.fold_in(seeds[7], 71), 0)
    cache_values = centred(seeds[2], (ENTRIES, NEIGH_LEN, HD), 1.0, 5.0, ((0, 32), (2, 8)))
    owners_keys = jax.random.split(jax.random.fold_in(seeds[3], 1), SPANS // SPANS_DEV)
    owners_turns = jax.random.permutation(jax.random.fold_in(seeds[3], 3), SPANS // SPANS_DEV)
    owners = jax.vmap(lambda own, number: routed_block(jax.random.fold_in(seeds[3], 2), own, number, SPANS_DEV, N_SEQ, TOP, CAP, 2))(owners_keys, owners_turns).reshape((SPANS, TOP))
    slots = with_ends(jax.random.randint(seeds[4], (SPANS, TOP), 0, E_DEV), jax.random.fold_in(seeds[4], 1), 0, E_DEV - 1).astype(jnp.int32)
    out_weight = centred(seeds[5], (HD, D), HD ** -0.5, 0.09375, ((1, 8),))
    cotangent = centred(seeds[6], (TOKENS, D), 1.0, 6.0, ((0, 32), (1, 8)))
    return dict(queries=queries, cache_keys=cache_keys, cache_values=cache_values, owners=owners, slots=slots, out_weight=out_weight, cotangent=cotangent)


def rounded(value):
    return lax.optimization_barrier(value.astype(jnp.bfloat16)).astype(jnp.float32)

def reference(queries, cache_keys, cache_values, owners, slots, out_weight, cotangent):
    scale = 1.0 / math.sqrt(HEAD_DIM)
    lead = SPAN - 1
    width = HEADS * HEAD_DIM
    span_queries = jnp.concatenate([queries[lead:], jnp.zeros((lead, width), queries.dtype)], 0)
    span_queries = span_queries.reshape(SPANS, SPAN, HEADS, HEAD_DIM)
    entry = (owners * E_DEV + slots).astype(jnp.int32)

    def neighbour_scores(block, keys):
        return jnp.einsum('qhd,khd->hqk', block.astype(jnp.float32), keys.astype(jnp.float32)) * scale

    def forward_span(inputs):
        block, ids = inputs
        keys = cache_keys[ids].reshape(TOP, NEIGH_LEN, HEADS, HEAD_DIM)
        values = cache_values[ids].reshape(TOP, NEIGH_LEN, HEADS, HEAD_DIM)
        parts = []
        sums = []
        for index in range(TOP):
            scores = neighbour_scores(block, keys[index])
            part_lse = jax.nn.logsumexp(scores, axis=-1)
            weights = rounded(jnp.exp(scores - part_lse[..., None]))
            partial_value = jnp.einsum('hqk,khd->qhd', weights, values[index].astype(jnp.float32))
            parts.append(rounded(partial_value))
            sums.append(part_lse)
        stacked = jnp.stack(sums, 0)
        total_lse = jax.nn.logsumexp(stacked, axis=0)
        merged = jnp.zeros((SPAN, HEADS, HEAD_DIM), jnp.float32)
        for index in range(TOP):
            share = jnp.exp(stacked[index] - total_lse).T[..., None]
            merged = merged + share * parts[index]
        return (merged.astype(jnp.bfloat16), total_lse)
    span_out, total_lse = lax.map(forward_span, (span_queries, entry))
    flat_out = span_out.reshape(TOKENS, width)
    attended = jnp.concatenate([jnp.zeros((lead, width), jnp.bfloat16), flat_out[:TOKENS - lead]], 0)
    mixed = jnp.dot(attended, out_weight, preferred_element_type=jnp.float32).astype(jnp.bfloat16)
    group_width = D // N_HEAD

    def group_term(total, group):
        start = (group * group_width).astype(jnp.int32)
        cot_part = lax.dynamic_slice_in_dim(cotangent, start, group_width, 1)
        weight_part = lax.dynamic_slice_in_dim(out_weight, start, group_width, 1)
        term = lax.dot_general(cot_part, weight_part, (((1,), (1,)), ((), ())), preferred_element_type=jnp.float32)
        return (total + rounded(term), None)
    out_total, _ = lax.scan(group_term, jnp.zeros((TOKENS, width), jnp.float32), jnp.arange(N_HEAD, dtype=jnp.int32))
    out_grad = out_total.astype(jnp.bfloat16)
    span_grad = jnp.concatenate([out_grad[lead:], jnp.zeros((lead, width), jnp.bfloat16)], 0)
    span_grad = span_grad.reshape(SPANS, SPAN, HEADS, HEAD_DIM)
    delta = lax.optimization_barrier(jnp.sum(span_grad.astype(jnp.float32) * span_out.astype(jnp.float32), axis=-1))
    delta = jnp.transpose(delta, (0, 2, 1))

    def backward_span(carry, inputs):
        key_total, value_total = carry
        block, ids, lse_row, delta_row, grad_block = inputs
        keys = cache_keys[ids].reshape(TOP, NEIGH_LEN, HEADS, HEAD_DIM)
        values = cache_values[ids].reshape(TOP, NEIGH_LEN, HEADS, HEAD_DIM)
        grads = grad_block.astype(jnp.float32)
        for index in range(TOP):
            scores = neighbour_scores(block, keys[index])
            probs = jnp.exp(scores - lse_row[..., None])
            value_terms = jnp.einsum('hqk,qhd->khd', rounded(probs), grads)
            prob_grad = jnp.einsum('qhd,khd->hqk', grads, values[index].astype(jnp.float32))
            score_grad = rounded(probs * (prob_grad - delta_row[..., None]))
            key_terms = jnp.einsum('hqk,qhd->khd', score_grad, block.astype(jnp.float32)) * scale
            key_total = key_total.at[ids[index]].add(key_terms)
            value_total = value_total.at[ids[index]].add(value_terms)
        return ((key_total, value_total), None)
    empty = jnp.zeros((ENTRIES, NEIGH_LEN, HEADS, HEAD_DIM), jnp.float32)
    (key_total, value_total), _ = lax.scan(backward_span, (empty, empty), (span_queries, entry, total_lse, delta, span_grad))
    grad_keys = key_total.reshape(ENTRIES, NEIGH_LEN, width).astype(jnp.bfloat16)
    grad_values = value_total.reshape(ENTRIES, NEIGH_LEN, width).astype(jnp.bfloat16)

    def weight_group(total, group):
        start = (group * TOK_DEV).astype(jnp.int32)
        att_part = lax.dynamic_slice_in_dim(attended, start, TOK_DEV, 0)
        cot_part = lax.dynamic_slice_in_dim(cotangent, start, TOK_DEV, 0)
        term = lax.dot_general(att_part, cot_part, (((0,), (0,)), ((), ())), preferred_element_type=jnp.float32)
        return (total + rounded(term), None)
    weight_total, _ = lax.scan(weight_group, jnp.zeros((width, D), jnp.float32), jnp.arange(N_SEQ, dtype=jnp.int32))
    return (mixed, weight_total.astype(jnp.bfloat16), grad_keys, grad_values)
```

```python
import functools
import math

import jax
import jax.numpy as jnp
from jax import lax
from jax.experimental import pallas as pl
from jax.experimental.pallas import tpu as pltpu
from jax.sharding import PartitionSpec as P

HEAD_DIM = 128
SPAN = 64
TOP = 2
NX, NZ, NY = 4, 8, 4
ROWS, WIDTH = 448, 512
SPANS_HERE = 7
PAIRS = SPANS_HERE * TOP
ENTRIES_HERE = 4
KEYS = 128
HALF = ROWS // 2
SCALE = 1.0 / math.sqrt(HEAD_DIM)
NEVER = -1e30
VMEM_BYTES = 56 * 1024 * 1024
MESH_ID = pl.DeviceIdType.MESH
BF, F32 = jnp.bfloat16, jnp.float32


def place():
    seq, head = lax.axis_index("seq"), lax.axis_index("head")
    return seq, head, seq // NZ, lax.rem(seq, NZ), head // 2, lax.rem(head, 2)


def remote(src, dst, sems, index, device):
    return pltpu.make_async_remote_copy(
        src_ref=src,
        dst_ref=dst,
        send_sem=sems.at[0, index],
        recv_sem=sems.at[1, index],
        device_id=device,
        device_id_type=MESH_ID,
    )


def meet(devices):
    sem = pltpu.get_barrier_semaphore()
    for device in devices:
        pl.semaphore_signal(sem, inc=1, device_id=device, device_id_type=MESH_ID)
    pl.semaphore_wait(sem, len(devices))


def selector(step):
    row = lax.broadcasted_iota(jnp.int32, (SPAN, 2 * SPAN), 0)
    column = lax.broadcasted_iota(jnp.int32, (SPAN, 2 * SPAN), 1)
    return (column == row + step).astype(F32).astype(BF)


def shift_rows(raw, step, write):
    pick = selector(step)

    def one(block, carry):
        window = raw[pl.ds(pl.multiple_of(block * SPAN, SPAN), 2 * SPAN), :]
        write(block, jnp.dot(pick, window, preferred_element_type=F32).astype(BF))
        return carry

    lax.fori_loop(0, SPANS_HERE, one, 0)


def add_blocks(write, *terms):
    def one(block, carry):
        rows = pl.ds(pl.multiple_of(block * SPAN, SPAN), SPAN)
        total = terms[0](rows).astype(F32)
        for term in terms[1:]:
            total = total + term(rows).astype(F32)
        write(rows, total)
        return carry

    return one


class Ring:
    def __init__(self, first, out, sems):
        seq, head, x, z, _, _ = place()
        self.first, self.out, self.sems, self.z = first, out, sems, z
        self.right = (x * NZ + lax.rem(z + 1, NZ), head)
        self.left = (x * NZ + lax.rem(z + NZ - 1, NZ), head)

    def copy(self, step, way):
        slot = lax.rem(self.z + (NZ - step if way == 0 else step), NZ)
        src = self.out.at[slot] if step else self.first
        dst = self.out.at[slot]
        if step == 3:
            src, dst = (self.out.at[slot, pl.ds(way * HALF, HALF)],) * 2
        to = self.left if way else self.right
        return remote(src, dst, self.sems, 4 * way + step, to)

    def start(self, step):
        for way in range(2):
            if step:
                self.copy(step - 1, way).wait_recv()
            self.copy(step, way).start()

    def finish(self):
        for way in range(2):
            self.copy(3, way).wait_recv()
            for step in range(4):
                self.copy(step, way).wait_send()


def gather_kernel(
    q, k, v, codes, cot, w,
    q_all, g_all, k_all, v_all, codes_all,
    q_raw, q_sh, g_raw, g_sh, cot_v, w_v, part, pair_got, y_send, y_got, g_acc,
    local, q_sems, g_sems, kv_sems, code_sems, edge_sems, pair_sems, y_sems,
):
    seq, head, x, z, y, c = place()
    n_seq = NX * NZ
    before = (lax.rem(seq + n_seq - 1, n_seq), head)
    after = (lax.rem(seq + 1, n_seq), head)
    z_peers = [(x * NZ + lax.rem(z + d, NZ), head) for d in range(1, NZ)]
    x_peers = [(lax.rem(x + d, NX) * NZ + z, head) for d in range(1, NX)]
    y_peers = [(seq, 2 * lax.rem(y + d, NY) + c) for d in range(1, NY)]
    sibling = (seq, 2 * y + 1 - c)

    own_q = pltpu.make_async_copy(q, q_raw.at[pl.ds(0, ROWS)], local.at[0])
    own_cot = pltpu.make_async_copy(cot, cot_v, local.at[1])
    own_w = pltpu.make_async_copy(w, w_v, local.at[2])
    own_q.start()
    own_cot.start()
    own_w.start()
    meet(z_peers + x_peers + y_peers + [sibling, before, after])
    q_edge = remote(q.at[pl.ds(0, SPAN)], q_raw.at[pl.ds(ROWS, SPAN)], edge_sems, 0, before)
    q_edge.start()
    code_copies = [
        remote(codes, codes_all.at[z], code_sems, d, z_peers[d]) for d in range(NZ - 1)
    ]
    for copy in code_copies:
        copy.start()
    own_k = pltpu.make_async_copy(k, k_all.at[x], local.at[3])
    own_v = pltpu.make_async_copy(v, v_all.at[x], local.at[4])
    own_codes = pltpu.make_async_copy(codes, codes_all.at[z], local.at[5])
    own_k.start()
    own_v.start()
    own_codes.start()
    own_q.wait()
    q_edge.wait()
    last = seq == n_seq - 1
    tail = q_raw[pl.ds(ROWS, SPAN), :]
    q_raw[pl.ds(ROWS, SPAN), :] = jnp.where(last, jnp.zeros_like(tail), tail)

    def put_q(block, value):
        q_sh[pl.ds(pl.multiple_of(block * SPAN, SPAN), SPAN), :] = value

    shift_rows(q_raw, SPAN - 1, put_q)
    q_ring = Ring(q_sh, q_all, q_sems)
    q_ring.start(0)
    keep_q = pltpu.make_async_copy(q_sh, q_all.at[z], local.at[6])
    keep_q.start()
    kv_copies = []
    for d in range(NX - 1):
        kv_copies.append(remote(k, k_all.at[x], kv_sems, 2 * d, x_peers[d]))
        kv_copies.append(remote(v, v_all.at[x], kv_sems, 2 * d + 1, x_peers[d]))
    for copy in kv_copies:
        copy.start()

    own_cot.wait()
    own_w.wait()

    def product(to_head):
        rows = pl.ds(pl.multiple_of(to_head * WIDTH, WIDTH), WIDTH)
        return lax.dot_general(
            cot_v[...], w_v[rows, :], (((1,), (1,)), ((), ())), preferred_element_type=F32
        )

    def pair_copy(j):
        return remote(part.at[j], pair_got.at[j], pair_sems, j, sibling)

    def for_sibling(j, carry):
        part[j] = product(2 * lax.rem(y + j, NY) + 1 - c).astype(BF)
        pair_copy(j).start()
        return carry

    lax.fori_loop(0, NY, for_sibling, 0)

    def y_copy(j):
        to = (seq, 2 * lax.rem(y + j, NY) + c)
        return remote(y_send.at[j - 1], y_got.at[j - 1], y_sems, j - 1, to)

    def for_row(j, carry):
        value = product(2 * lax.rem(y + j, NY) + c)
        pair_copy(j).wait_recv()
        y_send[j - 1] = (value + pair_got[j].astype(F32)).astype(BF)
        y_copy(j).start()
        return carry

    lax.fori_loop(1, NY, for_row, 0)
    q_ring.start(1)
    mine = product(2 * y + c)
    pair_copy(0).wait_recv()
    g_acc[...] = mine + pair_got[0].astype(F32)
    q_ring.start(2)
    for j in range(1, NY):
        y_copy(j).wait_recv()
    q_ring.start(3)

    def put_g(rows, total):
        g_raw[rows, :] = total.astype(BF)

    lax.fori_loop(
        0,
        SPANS_HERE,
        add_blocks(
            put_g,
            lambda rows: g_acc[rows, :],
            lambda rows: y_got[0, rows, :],
            lambda rows: y_got[1, rows, :],
            lambda rows: y_got[2, rows, :],
        ),
        0,
    )
    g_edge = remote(
        g_raw.at[pl.ds(0, SPAN)], g_raw.at[pl.ds(ROWS, SPAN)], edge_sems, 1, before
    )
    g_edge.start()
    g_edge.wait()
    tail = g_raw[pl.ds(ROWS, SPAN), :]
    g_raw[pl.ds(ROWS, SPAN), :] = jnp.where(last, jnp.zeros_like(tail), tail)

    def put_gs(block, value):
        g_sh[pl.ds(pl.multiple_of(block * SPAN, SPAN), SPAN), :] = value

    shift_rows(g_raw, SPAN - 1, put_gs)
    g_ring = Ring(g_sh, g_all, g_sems)
    g_ring.start(0)
    keep_g = pltpu.make_async_copy(g_sh, g_all.at[z], local.at[7])
    keep_g.start()
    q_ring.finish()
    for step in range(1, 4):
        g_ring.start(step)
    for copy in kv_copies + code_copies:
        copy.wait()
    for j in range(NY):
        pair_copy(j).wait_send()
    for j in range(1, NY):
        y_copy(j).wait_send()
    own_k.wait()
    own_v.wait()
    own_codes.wait()
    keep_q.wait()
    keep_g.wait()
    g_ring.finish()


def gather_all(q, k, v, codes, cot, w):
    def vm(*shape):
        return pltpu.VMEM(shape, BF)

    def sems(n):
        return pltpu.SemaphoreType.DMA((2, n))

    any_spec = pl.BlockSpec(memory_space=pl.ANY)
    entries = (NX, ENTRIES_HERE, KEYS, WIDTH)
    return pl.pallas_call(
        gather_kernel,
        out_shape=(
            jax.ShapeDtypeStruct((NZ, ROWS, WIDTH), BF),
            jax.ShapeDtypeStruct((NZ, ROWS, WIDTH), BF),
            jax.ShapeDtypeStruct(entries, BF),
            jax.ShapeDtypeStruct(entries, BF),
            jax.ShapeDtypeStruct((NZ, 8, 128), jnp.int32),
        ),
        in_specs=[any_spec] * 6,
        out_specs=(any_spec,) * 5,
        scratch_shapes=[
            vm(ROWS + SPAN, WIDTH), vm(ROWS, WIDTH), vm(ROWS + SPAN, WIDTH), vm(ROWS, WIDTH),
            vm(ROWS, WIDTH), vm(8 * WIDTH, WIDTH), vm(NY, ROWS, WIDTH), vm(NY, ROWS, WIDTH),
            vm(NY - 1, ROWS, WIDTH), vm(NY - 1, ROWS, WIDTH), pltpu.VMEM((ROWS, WIDTH), F32),
            pltpu.SemaphoreType.DMA((8,)), sems(8), sems(8), sems(6), sems(7), sems(2),
            sems(4), sems(3),
        ],
        compiler_params=pltpu.CompilerParams(
            collective_id=0, has_side_effects=True, vmem_limit_bytes=VMEM_BYTES
        ),
        name="gather_all",
    )(q, k, v, codes, cot, w)


def two_heads(block):
    lane = lax.broadcasted_iota(jnp.int32, block.shape, 1)
    zero = jnp.zeros_like(block)
    upper = jnp.where(lane < HEAD_DIM, block, zero)
    lower = jnp.where(lane < HEAD_DIM, zero, block)
    return jnp.concatenate([upper, lower], axis=0)


def dot_t(a, b):
    return lax.dot_general(a, b, (((1,), (1,)), ((), ())), preferred_element_type=F32)


def each_live(codes, visit):
    z = lax.rem(lax.axis_index("seq"), NZ)

    def source(src, carry):
        def pair(j, inner):
            code = codes[src, 0, j]
            owner = code // ENTRIES_HERE

            @pl.when(lax.rem(owner, NZ) == z)
            def _():
                entry = (owner // NZ) * ENTRIES_HERE + lax.rem(code, ENTRIES_HERE)
                visit(src, j // TOP, entry)

            return inner

        return lax.fori_loop(0, PAIRS, pair, carry)

    lax.fori_loop(0, NZ, source, 0)


def stats_kernel(codes, q, g, k, v, stats):
    lanes = NZ * SPAN // 2
    stats[:, :, :lanes] = jnp.full((NZ, 8, lanes), NEVER, F32)
    stats[:, :, lanes:] = jnp.zeros((NZ, 8, lanes), F32)

    def visit(src, span, entry):
        row = src * SPANS_HERE + span
        for pair in range(2):
            columns = pl.ds(pair * 256, 256)
            q2 = two_heads(q[row, :, columns])
            g2 = two_heads(g[row, :, columns])
            scores = dot_t(k[entry, :, columns], q2) * SCALE
            prob_grad = dot_t(v[entry, :, columns], g2)
            top = jnp.max(scores, axis=0, keepdims=True)
            probs = jnp.exp(scores - top)
            total = jnp.sum(probs, axis=0, keepdims=True)
            lse = top + jnp.log(total)
            delta = jnp.sum(probs * prob_grad, axis=0, keepdims=True) / total
            at_lse, at_delta = pl.ds(pair * 128, 128), pl.ds(lanes + pair * 128, 128)
            here = lax.broadcasted_iota(jnp.int32, (8, 128), 0) == span
            old_lse, old_delta = stats[src, :, at_lse], stats[src, :, at_delta]
            high = jnp.maximum(old_lse, lse)
            old_part, new_part = jnp.exp(old_lse - high), jnp.exp(lse - high)
            both = old_part + new_part
            stats[src, :, at_lse] = jnp.where(here, high + jnp.log(both), old_lse)
            stats[src, :, at_delta] = jnp.where(
                here, (old_part * old_delta + new_part * delta) / both, old_delta
            )

    each_live(codes, visit)


def local_stats(codes, q, g, k, v):
    return pl.pallas_call(
        stats_kernel,
        out_shape=jax.ShapeDtypeStruct((NZ, 8, 512), F32),
        in_specs=[pl.BlockSpec(memory_space=pltpu.SMEM)]
        + [pl.BlockSpec(memory_space=pltpu.VMEM)] * 4,
        out_specs=pl.BlockSpec(memory_space=pltpu.VMEM),
        compiler_params=pltpu.CompilerParams(vmem_limit_bytes=VMEM_BYTES),
        name="local_stats",
    )(codes, q, g, k, v)


def totals_kernel(stats, out, got, summed, there, sems, back_sems):
    seq, head, x, z, _, _ = place()
    peers = [(x * NZ + lax.rem(z + d, NZ), head) for d in range(1, NZ)]
    meet(peers)
    copies = [
        remote(stats.at[lax.rem(z + d + 1, NZ)], got.at[d], sems, d, peers[d])
        for d in range(NZ - 1)
    ]
    for copy in copies:
        copy.start()
    for copy in copies:
        copy.wait_recv()
    terms = [stats[z]] + [got[d] for d in range(NZ - 1)]
    high = terms[0][:, :256]
    for term in terms[1:]:
        high = jnp.maximum(high, term[:, :256])
    both = jnp.zeros_like(high)
    delta = jnp.zeros_like(high)
    for term in terms:
        part = jnp.exp(term[:, :256] - high)
        both = both + part
        delta = delta + part * term[:, 256:]
    summed[:, :256] = high + jnp.log(both)
    summed[:, 256:] = delta / both
    returns = [remote(summed, there.at[d], back_sems, d, peers[d]) for d in range(NZ - 1)]
    for copy in returns:
        copy.start()
    out[z] = summed[...]
    for d in range(NZ - 1):
        returns[d].wait_recv()
        out[lax.rem(z + NZ - d - 1, NZ)] = there[d]
    for copy in copies + returns:
        copy.wait_send()


def all_totals(stats):
    shape = (NZ, 8, 512)
    vmem = pl.BlockSpec(memory_space=pltpu.VMEM)
    return pl.pallas_call(
        totals_kernel,
        out_shape=jax.ShapeDtypeStruct(shape, F32),
        in_specs=[vmem],
        out_specs=vmem,
        scratch_shapes=[
            pltpu.VMEM((NZ - 1, 8, 512), F32),
            pltpu.VMEM((8, 512), F32),
            pltpu.VMEM((NZ - 1, 8, 512), F32),
            pltpu.SemaphoreType.DMA((2, NZ - 1)),
            pltpu.SemaphoreType.DMA((2, NZ - 1)),
        ],
        compiler_params=pltpu.CompilerParams(collective_id=1, has_side_effects=True),
        name="all_totals",
    )(stats)


def grads_kernel(codes, q, g, k, v, totals, out, key_out, value_out, key_acc, value_acc):
    def clear(i, carry):
        out[i] = jnp.zeros((SPAN, WIDTH), BF)
        return carry

    lax.fori_loop(0, NZ * SPANS_HERE, clear, 0)

    def clear_acc(i, carry):
        key_acc[i] = jnp.zeros((KEYS, WIDTH), F32)
        value_acc[i] = jnp.zeros((KEYS, WIDTH), F32)
        return carry

    lax.fori_loop(0, NX * ENTRIES_HERE, clear_acc, 0)

    def visit(src, span, entry):
        row = src * SPANS_HERE + span
        for pair in range(2):
            columns = pl.ds(pair * 256, 256)
            q2 = two_heads(q[row, :, columns])
            g2 = two_heads(g[row, :, columns])
            values = v[entry, :, columns]
            scores = dot_t(k[entry, :, columns], q2) * SCALE
            prob_grad = dot_t(values, g2)
            here = lax.broadcasted_iota(jnp.int32, (8, 128), 0) == span
            lse, delta = (
                jnp.sum(
                    jnp.where(here, totals[src, :, pl.ds(start + pair * 128, 128)], 0.0),
                    axis=0,
                    keepdims=True,
                )
                for start in (0, 256)
            )
            probs = jnp.exp(scores - lse)
            low = probs.astype(BF)
            score_grad = (probs * (prob_grad - delta)).astype(BF)
            key_acc[entry, :, columns] += jnp.dot(score_grad, q2, preferred_element_type=F32)
            value_acc[entry, :, columns] += jnp.dot(low, g2, preferred_element_type=F32)
            mixed = lax.dot_general(
                low, values, (((0,), (0,)), ((), ())), preferred_element_type=F32
            )
            for head in range(2):
                at = pl.ds(pair * 256 + head * 128, 128)
                term = mixed[head * SPAN : (head + 1) * SPAN, head * 128 : (head + 1) * 128]
                out[row, :, at] = (out[row, :, at].astype(F32) + term).astype(BF)

    each_live(codes, visit)

    def close(i, carry):
        key_out[i] = (key_acc[i] * SCALE).astype(BF)
        value_out[i] = value_acc[i].astype(BF)
        return carry

    lax.fori_loop(0, NX * ENTRIES_HERE, close, 0)


def local_grads(codes, q, g, k, v, totals):
    entries = (NX * ENTRIES_HERE, KEYS, WIDTH)
    vmem = pl.BlockSpec(memory_space=pltpu.VMEM)
    return pl.pallas_call(
        grads_kernel,
        out_shape=(
            jax.ShapeDtypeStruct((NZ * SPANS_HERE, SPAN, WIDTH), BF),
            jax.ShapeDtypeStruct(entries, BF),
            jax.ShapeDtypeStruct(entries, BF),
        ),
        in_specs=[pl.BlockSpec(memory_space=pltpu.SMEM)] + [vmem] * 5,
        out_specs=(vmem,) * 3,
        scratch_shapes=[pltpu.VMEM(entries, F32), pltpu.VMEM(entries, F32)],
        compiler_params=pltpu.CompilerParams(vmem_limit_bytes=VMEM_BYTES),
        name="local_grads",
    )(codes, q, g, k, v, totals)


class RingSum:
    def __init__(self, blocks, rows, got, sums, sems):
        seq, head, x, z, _, _ = place()
        self.blocks, self.rows, self.got, self.sums, self.sems, self.z = (
            blocks, rows, got, sums, sems, z,
        )
        self.right = (x * NZ + lax.rem(z + 1, NZ), head)
        self.left = (x * NZ + lax.rem(z + NZ - 1, NZ), head)

    def copy(self, step, way):
        half = self.rows // 2
        if step == 0:
            far, rows = lax.rem(self.z + 4, NZ), pl.ds(way * half, half)
            src, dst = self.blocks.at[far, rows], self.got.at[way, 0, rows]
        else:
            src, dst = self.sums.at[way, step - 1], self.got.at[way, step]
        to = self.left if way else self.right
        return remote(src, dst, self.sems, 4 * way + step, to)

    def start(self, step):
        half, piece = self.rows // 2, 32
        for way in range(2):
            if step:
                self.copy(step - 1, way).wait_recv()
                block = lax.rem(self.z + (4 + step if way else 4 - step), NZ)

                def add(i, carry):
                    rows = pl.ds(pl.multiple_of(i * piece, piece), piece)
                    self.sums[way, step - 1, rows, :] = (
                        self.blocks[block, rows, :].astype(F32)
                        + self.got[way, step - 1, rows, :].astype(F32)
                    ).astype(BF)
                    return carry

                def move(i, carry):
                    rows = pl.ds(pl.multiple_of(i * piece, piece), piece)
                    self.sums[way, step - 1, rows, :] = self.blocks[block, rows, :]
                    return carry

                upper, lower = (0, half // piece), (half // piece, self.rows // piece)
                if step > 1:
                    lax.fori_loop(0, self.rows // piece, add, 0)
                else:
                    lax.fori_loop(*(lower if way else upper), add, 0)
                    lax.fori_loop(*(upper if way else lower), move, 0)
            self.copy(step, way).start()

    def wait_last(self):
        for way in range(2):
            self.copy(3, way).wait_recv()

    def wait_sends(self):
        for way in range(2):
            for step in range(4):
                self.copy(step, way).wait_send()


def finish_kernel(
    o, keys, values, cot, w,
    mixed, weight_grad, key_grad, value_grad,
    w_v, own_kv, kv_got, o_got, o_sums, att_raw, att, acc,
    wide, tall, wide_got, wide_sum, wide_z, tall_got, tall_sums, tall_sum, tall_x,
    local, kv_sems, o_sems, edge_sems, pair_sems, y_sems, forward_sems,
    wide_sems, wide_z_sems, tall_sems, tall_x_sems,
):
    seq, head, x, z, y, c = place()
    n_seq = NX * NZ
    before = (lax.rem(seq + n_seq - 1, n_seq), head)
    after = (lax.rem(seq + 1, n_seq), head)
    z_peers = [(x * NZ + lax.rem(z + d, NZ), head) for d in range(1, NZ)]
    x_peers = [(lax.rem(x + d, NX) * NZ + z, head) for d in range(1, NX)]
    y_peers = [(seq, 2 * lax.rem(y + d, NY) + c) for d in range(1, NY)]
    sibling = (seq, 2 * y + 1 - c)
    own_w = pltpu.make_async_copy(w, w_v, local.at[0])
    own_k = pltpu.make_async_copy(keys.at[x], own_kv.at[0], local.at[1])
    own_v = pltpu.make_async_copy(values.at[x], own_kv.at[1], local.at[2])
    own_w.start()
    own_k.start()
    own_v.start()
    meet(z_peers + x_peers + y_peers + [sibling, before, after])
    o_ring = RingSum(o, ROWS, o_got, o_sums, o_sems)
    o_ring.start(0)
    kv_copies = []
    for d in range(NX - 1):
        to = lax.rem(x + d + 1, NX)
        kv_copies.append(remote(keys.at[to], kv_got.at[0, d], kv_sems, 2 * d, x_peers[d]))
        kv_copies.append(remote(values.at[to], kv_got.at[1, d], kv_sems, 2 * d + 1, x_peers[d]))
    for copy in kv_copies:
        copy.start()
    for step in range(1, 4):
        o_ring.start(step)
    o_ring.wait_last()

    def put_out(rows, total):
        att_raw[pl.ds(pl.multiple_of(rows.start + SPAN, SPAN), SPAN), :] = total.astype(BF)

    lax.fori_loop(
        0,
        SPANS_HERE,
        add_blocks(
            put_out,
            lambda rows: o[z, rows, :],
            lambda rows: o_got[0, 3, rows, :],
            lambda rows: o_got[1, 3, rows, :],
        ),
        0,
    )
    edge = remote(
        att_raw.at[pl.ds(ROWS, SPAN)], att_raw.at[pl.ds(0, SPAN)], edge_sems, 0, after
    )
    edge.start()
    edge.wait()
    lead = att_raw[pl.ds(0, SPAN), :]
    att_raw[pl.ds(0, SPAN), :] = jnp.where(seq == 0, jnp.zeros_like(lead), lead)

    def put_att(block, value):
        att[head, pl.ds(pl.multiple_of(block * SPAN, SPAN), SPAN), :] = value

    shift_rows(att_raw, 1, put_att)
    own_block = att.at[head]
    y_copies = [remote(own_block, own_block, y_sems, j, y_peers[j]) for j in range(NY - 1)]
    pair_copy = remote(own_block, own_block, pair_sems, 0, sibling)
    for j in (1, 0, 2):
        y_copies[j].start()
    pair_copy.start()
    own_w.wait()

    def use(block, first=False):
        rows = pl.ds(pl.multiple_of(block * WIDTH, WIDTH), WIDTH)
        term = jnp.dot(att[block], w_v[rows, :], preferred_element_type=F32)
        acc[...] = term if first else acc[...] + term
        terms = lax.dot_general(
            att[block], cot[...], (((0,), (0,)), ((), ())), preferred_element_type=F32
        ).astype(BF)
        to_x, part = block // 2, lax.rem(block, 2)
        wide[to_x, pl.ds(pl.multiple_of(part * WIDTH, WIDTH), WIDTH), :] = terms[:, :256]
        for i in range(4):
            tall[part * 4 + i, pl.ds(pl.multiple_of(to_x * 128, 128), 128), :] = terms[
                i * 128 : (i + 1) * 128, 256:
            ]

    use(head, True)
    pair_copy.wait_recv()
    use(2 * y + 1 - c)
    forwards = []
    for j in (0, 2, 1):
        y_copies[j].wait_recv()
        came = 2 * lax.rem(y + NY - j - 1, NY) + c
        forward = remote(att.at[came], att.at[came], forward_sems, j, sibling)
        forward.start()
        forwards.append(forward)
        use(came)
        forward.wait_recv()
        use(2 * lax.rem(y + NY - j - 1, NY) + 1 - c)

    tall_ring = RingSum(tall, 512, tall_got, tall_sums, tall_sems)
    tall_ring.start(0)
    wide_copies = [
        remote(wide.at[lax.rem(x + d + 1, NX)], wide_got.at[d], wide_sems, d, x_peers[d])
        for d in range(NX - 1)
    ]
    for copy in wide_copies:
        copy.start()
    mixed[...] = acc[...].astype(BF)

    for copy in kv_copies:
        copy.wait_recv()
    own_k.wait()
    own_v.wait()
    for which, out in enumerate((key_grad, value_grad)):

        def add(i, carry, which=which, out=out):
            total = own_kv[which, i].astype(F32)
            for d in range(NX - 1):
                total = total + kv_got[which, d, i].astype(F32)
            out[i] = total.astype(BF)
            return carry

        lax.fori_loop(0, ENTRIES_HERE, add, 0)
    for step in range(1, 4):
        tall_ring.start(step)
    for copy in wide_copies:
        copy.wait_recv()

    def add_wide(i, carry):
        rows = pl.ds(pl.multiple_of(i * 128, 128), 128)
        total = wide[x, rows, :].astype(F32)
        for d in range(NX - 1):
            total = total + wide_got[d, rows, :].astype(F32)
        wide_sum[i] = total.astype(BF)
        return carry

    lax.fori_loop(0, NZ, add_wide, 0)
    wide_z_copies = [
        remote(wide_sum.at[lax.rem(z + d + 1, NZ)], wide_z.at[d], wide_z_sems, d, z_peers[d])
        for d in range(NZ - 1)
    ]
    for copy in wide_z_copies:
        copy.start()
    tall_ring.wait_last()

    def add_tall(i, carry):
        rows = pl.ds(pl.multiple_of(i * 128, 128), 128)
        tall_sum[i] = (
            tall[z, rows, :].astype(F32)
            + tall_got[0, 3, rows, :].astype(F32)
            + tall_got[1, 3, rows, :].astype(F32)
        ).astype(BF)
        return carry

    lax.fori_loop(0, NX, add_tall, 0)
    tall_x_copies = [
        remote(tall_sum.at[lax.rem(x + d + 1, NX)], tall_x.at[d], tall_x_sems, d, x_peers[d])
        for d in range(NX - 1)
    ]
    for copy in tall_x_copies:
        copy.start()
    for copy in tall_x_copies:
        copy.wait_recv()
    total = tall_sum[x].astype(F32)
    for d in range(NX - 1):
        total = total + tall_x[d].astype(F32)
    weight_grad[:, 256:] = total.astype(BF)
    for copy in wide_z_copies:
        copy.wait_recv()
    total = wide_sum[z].astype(F32)
    for d in range(NZ - 1):
        total = total + wide_z[d].astype(F32)
    weight_grad[:, :256] = total.astype(BF)

    o_ring.wait_sends()
    tall_ring.wait_sends()
    for copy in kv_copies + y_copies + forwards + wide_copies + wide_z_copies + tall_x_copies:
        copy.wait_send()
    pair_copy.wait_send()


def finish(o, keys, values, cot, w):
    def vm(*shape):
        return pltpu.VMEM(shape, BF)

    def sems(n):
        return pltpu.SemaphoreType.DMA((2, n))

    any_spec = pl.BlockSpec(memory_space=pl.ANY)
    vmem = pl.BlockSpec(memory_space=pltpu.VMEM)
    entry = (ENTRIES_HERE, KEYS, WIDTH)
    return pl.pallas_call(
        finish_kernel,
        out_shape=(
            jax.ShapeDtypeStruct((ROWS, WIDTH), BF),
            jax.ShapeDtypeStruct((128, WIDTH), BF),
            jax.ShapeDtypeStruct(entry, BF),
            jax.ShapeDtypeStruct(entry, BF),
        ),
        in_specs=[vmem, any_spec, any_spec, vmem, any_spec],
        out_specs=(vmem,) * 4,
        scratch_shapes=[
            vm(8 * WIDTH, WIDTH), vm(2, *entry), vm(2, NX - 1, *entry),
            vm(2, 4, ROWS, WIDTH), vm(2, 3, ROWS, WIDTH),
            vm(ROWS + SPAN, WIDTH), vm(8, ROWS, WIDTH), pltpu.VMEM((ROWS, WIDTH), F32),
            vm(NX, 1024, 256), vm(NZ, 512, 256), vm(NX - 1, 1024, 256), vm(NZ, 128, 256),
            vm(NZ - 1, 128, 256), vm(2, 4, 512, 256), vm(2, 3, 512, 256), vm(NX, 128, 256),
            vm(NX - 1, 128, 256),
            pltpu.SemaphoreType.DMA((3,)), sems(6), sems(8), sems(1), sems(1), sems(3), sems(3),
            sems(3), sems(7), sems(8), sems(3),
        ],
        compiler_params=pltpu.CompilerParams(
            collective_id=2, has_side_effects=True, vmem_limit_bytes=VMEM_BYTES
        ),
        name="finish",
    )(o, keys, values, cot, w)


def body(queries, cache_keys, cache_values, owners, slots, out_weight, cotangent):
    codes = (owners * ENTRIES_HERE + slots).reshape(1, PAIRS)
    codes = jnp.pad(codes, ((0, 7), (0, 128 - PAIRS)))
    q, g, k, v, codes = gather_all(
        queries, cache_keys, cache_values, codes, cotangent, out_weight
    )
    q = q.reshape(NZ * SPANS_HERE, SPAN, WIDTH)
    g = g.reshape(NZ * SPANS_HERE, SPAN, WIDTH)
    k = k.reshape(NX * ENTRIES_HERE, KEYS, WIDTH)
    v = v.reshape(NX * ENTRIES_HERE, KEYS, WIDTH)
    totals = all_totals(local_stats(codes, q, g, k, v))
    out, key_terms, value_terms = local_grads(codes, q, g, k, v, totals)
    entries = (NX, ENTRIES_HERE, KEYS, WIDTH)
    return finish(
        out.reshape(NZ, ROWS, WIDTH),
        key_terms.reshape(entries),
        value_terms.reshape(entries),
        cotangent,
        out_weight,
    )


def solution(mesh):
    placed = (
        P("seq", "head"),
        P("seq", None, "head"),
        P("seq", None, "head"),
        P("seq", None),
        P("seq", None),
        P(None, "head"),
        P("seq", "head"),
    )
    return jax.shard_map(
        body,
        mesh=mesh,
        in_specs=placed,
        out_specs=(
            P("seq", "head"),
            P("seq", "head"),
            P("seq", None, "head"),
            P("seq", None, "head"),
        ),
        check_vma=False,
    )
```

```python
import functools
import math

import jax
import jax.numpy as jnp
from jax import lax
from jax.experimental import pallas as pl
from jax.experimental.pallas import tpu as pltpu
from jax.sharding import PartitionSpec as P

HEAD_DIM = 128
SPAN = 64
TOP = 2
NX, NZ, NY = 4, 8, 4
ROWS, WIDTH = 448, 512
SPANS_HERE = 7
PAIRS = SPANS_HERE * TOP
ENTRIES_HERE = 4
KEYS = 128
HALF = ROWS // 2
SCALE = 1.0 / math.sqrt(HEAD_DIM)
NEVER = -1e30
VMEM_BYTES = 56 * 1024 * 1024
MESH_ID = pl.DeviceIdType.MESH
BF, F32 = jnp.bfloat16, jnp.float32


def place():
    seq, head = lax.axis_index("seq"), lax.axis_index("head")
    return seq, head, seq // NZ, lax.rem(seq, NZ), head // 2, lax.rem(head, 2)


def remote(src, dst, sems, index, device):
    return pltpu.make_async_remote_copy(
        src_ref=src,
        dst_ref=dst,
        send_sem=sems.at[0, index],
        recv_sem=sems.at[1, index],
        device_id=device,
        device_id_type=MESH_ID,
    )


def meet(devices):
    sem = pltpu.get_barrier_semaphore()
    for device in devices:
        pl.semaphore_signal(sem, inc=1, device_id=device, device_id_type=MESH_ID)
    pl.semaphore_wait(sem, len(devices))


def selector(step):
    row = lax.broadcasted_iota(jnp.int32, (SPAN, 2 * SPAN), 0)
    column = lax.broadcasted_iota(jnp.int32, (SPAN, 2 * SPAN), 1)
    return (column == row + step).astype(F32).astype(BF)


def shift_rows(raw, step, write):
    pick = selector(step)

    def one(block, carry):
        window = raw[pl.ds(pl.multiple_of(block * SPAN, SPAN), 2 * SPAN), :]
        write(block, jnp.dot(pick, window, preferred_element_type=F32).astype(BF))
        return carry

    lax.fori_loop(0, SPANS_HERE, one, 0)


class Line:
    def __init__(self, axis):
        seq, head, x, z, y, c = place()
        if axis == "z":
            self.n, self.at, to = NZ, z, lambda i: (x * NZ + i, head)
        elif axis == "x":
            self.n, self.at, to = NX, x, lambda i: (i * NZ + z, head)
        else:
            self.n, self.at, to = NY, y, lambda i: (seq, 2 * i + c)
        self.half = self.n // 2
        self.beside = (to(self.off(1)), to(self.off(-1)))

    def off(self, steps):
        return lax.rem(self.at + steps + self.n, self.n)


class Ring:
    def __init__(self, axis, first, out, rows, sems, slot=lambda place: place):
        self.line, self.first, self.out, self.sems, self.slot = (
            Line(axis), first, out, sems, slot,
        )
        self.rows = rows // 2

    def copy(self, way, main, step):
        slot = self.slot(self.line.off(step if way else -step))
        half = way if main else 1 - way
        rows = pl.ds(half * self.rows, self.rows)
        dst = self.out.at[slot, rows]
        src = dst if step else self.first.at[rows]
        index = way * (self.line.n - 1) + (0 if main else self.line.half) + step
        return remote(src, dst, self.sems, index, self.line.beside[way])

    def start(self, step):
        for main in (True, False):
            if main or step < self.line.half - 1:
                for way in range(2):
                    if step:
                        self.copy(way, main, step - 1).wait_recv()
                    self.copy(way, main, step).start()

    def wait_others(self):
        for way in range(2):
            self.copy(way, False, self.line.half - 2).wait_recv()

    def wait_mains(self):
        for way in range(2):
            self.copy(way, True, self.line.half - 1).wait_recv()

    def wait_sends(self):
        for way in range(2):
            for step in range(self.line.half):
                self.copy(way, True, step).wait_send()
            for step in range(self.line.half - 1):
                self.copy(way, False, step).wait_send()

    def finish(self):
        self.wait_others()
        self.wait_mains()
        self.wait_sends()


class RingSum:
    def __init__(self, axis, blocks, rows, got, sums, sems):
        self.line = Line(axis)
        self.blocks, self.got, self.sums, self.sems = blocks, got, sums, sems
        self.rows = rows // 2

    def copy(self, way, main, step):
        half = way if main else 1 - way
        if step == (0 if main else 1):
            far = self.line.half - step
            block = self.line.off(-far if way else far)
            src = self.blocks.at[block, pl.ds(half * self.rows, self.rows)]
        else:
            src = self.sums.at[way, half, step]
        index = way * self.line.n + (0 if main else self.line.half) + step
        dst = self.got.at[way, half, step]
        return remote(src, dst, self.sems, index, self.line.beside[way])

    def send(self, way, main, step):
        half = way if main else 1 - way
        if step > (0 if main else 1):
            self.copy(way, main, step - 1).wait_recv()
            far = self.line.half - step
            block = self.line.off(-far if way else far)
            piece = 32

            def add(i, carry):
                rows = pl.ds(pl.multiple_of(i * piece, piece), piece)
                from_rows = pl.ds(pl.multiple_of(half * self.rows + i * piece, piece), piece)
                self.sums[way, half, step, rows, :] = (
                    self.blocks[block, from_rows, :].astype(F32)
                    + self.got[way, half, step - 1, rows, :].astype(F32)
                ).astype(BF)
                return carry

            lax.fori_loop(0, self.rows // piece, add, 0)
        self.copy(way, main, step).start()

    def start(self, step):
        for way in range(2):
            self.send(way, True, step)
        if step + 1 < self.line.half:
            for way in range(2):
                self.send(way, False, step + 1)

    def wait_last(self):
        for main in (False, True):
            for way in range(2):
                self.copy(way, main, self.line.half - 1).wait_recv()

    def wait_sends(self):
        for way in range(2):
            for step in range(self.line.half):
                self.copy(way, True, step).wait_send()
            for step in range(1, self.line.half):
                self.copy(way, False, step).wait_send()

    def total(self, write, mine, piece):
        for half in range(2):

            def one(i, carry):
                rows = pl.ds(pl.multiple_of(i * piece, piece), piece)
                at = pl.ds(pl.multiple_of(half * self.rows + i * piece, piece), piece)
                term = mine(at).astype(F32)
                for way in range(2):
                    term = term + self.got[way, half, self.line.half - 1, rows, :].astype(F32)
                write(at, term)
                return carry

            lax.fori_loop(0, self.rows // piece, one, 0)


def gather_kernel(
    q, k, v, codes, cot, w,
    q_all, g_all, k_all, v_all, codes_all,
    q_raw, q_sh, g_raw, g_sh, cot_v, w_v, part, pair_got, y_blocks, y_got, y_sums, g_acc,
    local, q_sems, g_sems, k_sems, v_sems, code_sems, edge_sems, pair_sems, y_sems,
):
    seq, head, x, z, y, c = place()
    n_seq = NX * NZ
    before = (lax.rem(seq + n_seq - 1, n_seq), head)
    after = (lax.rem(seq + 1, n_seq), head)
    z_peers = [(x * NZ + lax.rem(z + d, NZ), head) for d in range(1, NZ)]
    sibling = (seq, 2 * y + 1 - c)
    own_q = pltpu.make_async_copy(q, q_raw.at[pl.ds(0, ROWS)], local.at[0])
    own_cot = pltpu.make_async_copy(cot, cot_v, local.at[1])
    own_w = pltpu.make_async_copy(w, w_v, local.at[2])
    own_q.start()
    own_cot.start()
    own_w.start()
    meet(
        z_peers + list(Line("x").beside) + list(Line("y").beside) + [sibling, before, after]
    )
    q_edge = remote(q.at[pl.ds(0, SPAN)], q_raw.at[pl.ds(ROWS, SPAN)], edge_sems, 0, before)
    q_edge.start()
    k_ring = Ring("x", k, k_all, ENTRIES_HERE, k_sems)
    v_ring = Ring("x", v, v_all, ENTRIES_HERE, v_sems)
    k_ring.start(0)
    v_ring.start(0)
    code_copies = [
        remote(codes, codes_all.at[z], code_sems, d, z_peers[d]) for d in range(NZ - 1)
    ]
    for copy in code_copies:
        copy.start()
    own_k = pltpu.make_async_copy(k, k_all.at[x], local.at[3])
    own_v = pltpu.make_async_copy(v, v_all.at[x], local.at[4])
    own_codes = pltpu.make_async_copy(codes, codes_all.at[z], local.at[5])
    own_k.start()
    own_v.start()
    own_codes.start()
    own_q.wait()
    q_edge.wait()
    last = seq == n_seq - 1
    tail = q_raw[pl.ds(ROWS, SPAN), :]
    q_raw[pl.ds(ROWS, SPAN), :] = jnp.where(last, jnp.zeros_like(tail), tail)

    def put_q(block, value):
        q_sh[pl.ds(pl.multiple_of(block * SPAN, SPAN), SPAN), :] = value

    shift_rows(q_raw, SPAN - 1, put_q)
    q_ring = Ring("z", q_sh, q_all, ROWS, q_sems)
    q_ring.start(0)
    keep_q = pltpu.make_async_copy(q_sh, q_all.at[z], local.at[6])
    keep_q.start()

    own_cot.wait()
    own_w.wait()

    def product(to_head):
        rows = pl.ds(pl.multiple_of(to_head * WIDTH, WIDTH), WIDTH)
        return lax.dot_general(
            cot_v[...], w_v[rows, :], (((1,), (1,)), ((), ())), preferred_element_type=F32
        )

    def pair_copy(j):
        return remote(part.at[j], pair_got.at[j], pair_sems, j, sibling)

    def for_sibling(i, carry):
        j = NY - 1 - i
        part[j] = product(2 * lax.rem(y + j, NY) + 1 - c).astype(BF)
        pair_copy(j).start()
        return carry

    lax.fori_loop(0, NY, for_sibling, 0)

    def for_row(i, carry):
        j = NY - 1 - i
        to = lax.rem(y + j, NY)
        value = product(2 * to + c)
        pair_copy(j).wait_recv()
        y_blocks[to] = (value + pair_got[j].astype(F32)).astype(BF)
        return carry

    lax.fori_loop(0, NY - 1, for_row, 0)
    y_ring = RingSum("y", y_blocks, ROWS, y_got, y_sums, y_sems)
    y_ring.start(0)
    mine = product(2 * y + c)
    pair_copy(0).wait_recv()
    g_acc[...] = mine + pair_got[0].astype(F32)
    q_ring.start(1)
    y_ring.start(1)
    q_ring.start(2)
    y_ring.wait_last()

    def put_g(rows, total):
        g_raw[rows, :] = total.astype(BF)

    y_ring.total(put_g, lambda rows: g_acc[rows, :], 32)
    g_edge = remote(
        g_raw.at[pl.ds(0, SPAN)], g_raw.at[pl.ds(ROWS, SPAN)], edge_sems, 1, before
    )
    g_edge.start()
    q_ring.start(3)
    g_edge.wait()
    tail = g_raw[pl.ds(ROWS, SPAN), :]
    g_raw[pl.ds(ROWS, SPAN), :] = jnp.where(last, jnp.zeros_like(tail), tail)

    def put_gs(block, value):
        g_sh[pl.ds(pl.multiple_of(block * SPAN, SPAN), SPAN), :] = value

    shift_rows(g_raw, SPAN - 1, put_gs)
    g_ring = Ring("z", g_sh, g_all, ROWS, g_sems)
    g_ring.start(0)
    keep_g = pltpu.make_async_copy(g_sh, g_all.at[z], local.at[7])
    keep_g.start()
    k_ring.start(1)
    v_ring.start(1)
    for step in range(1, 4):
        g_ring.start(step)
    q_ring.finish()
    k_ring.finish()
    v_ring.finish()
    for copy in code_copies:
        copy.wait()
    for j in range(NY):
        pair_copy(j).wait_send()
    y_ring.wait_sends()
    own_k.wait()
    own_v.wait()
    own_codes.wait()
    keep_q.wait()
    keep_g.wait()
    g_ring.finish()


def gather_all(q, k, v, codes, cot, w):
    def vm(*shape):
        return pltpu.VMEM(shape, BF)

    def sems(n):
        return pltpu.SemaphoreType.DMA((2, n))

    any_spec = pl.BlockSpec(memory_space=pl.ANY)
    entries = (NX, ENTRIES_HERE, KEYS, WIDTH)
    return pl.pallas_call(
        gather_kernel,
        out_shape=(
            jax.ShapeDtypeStruct((NZ, ROWS, WIDTH), BF),
            jax.ShapeDtypeStruct((NZ, ROWS, WIDTH), BF),
            jax.ShapeDtypeStruct(entries, BF),
            jax.ShapeDtypeStruct(entries, BF),
            jax.ShapeDtypeStruct((NZ, 8, 128), jnp.int32),
        ),
        in_specs=[any_spec] * 6,
        out_specs=(any_spec,) * 5,
        scratch_shapes=[
            vm(ROWS + SPAN, WIDTH), vm(ROWS, WIDTH), vm(ROWS + SPAN, WIDTH), vm(ROWS, WIDTH),
            vm(ROWS, WIDTH), vm(8 * WIDTH, WIDTH), vm(NY, ROWS, WIDTH), vm(NY, ROWS, WIDTH),
            vm(NY, ROWS, WIDTH), vm(2, 2, 2, HALF, WIDTH), vm(2, 2, 2, HALF, WIDTH),
            pltpu.VMEM((ROWS, WIDTH), F32),
            pltpu.SemaphoreType.DMA((8,)), sems(14), sems(14), sems(6), sems(6), sems(7),
            sems(2), sems(4), sems(8),
        ],
        compiler_params=pltpu.CompilerParams(
            collective_id=0, has_side_effects=True, vmem_limit_bytes=VMEM_BYTES
        ),
        name="gather_all",
    )(q, k, v, codes, cot, w)


def two_heads(block):
    lane = lax.broadcasted_iota(jnp.int32, block.shape, 1)
    zero = jnp.zeros_like(block)
    upper = jnp.where(lane < HEAD_DIM, block, zero)
    lower = jnp.where(lane < HEAD_DIM, zero, block)
    return jnp.concatenate([upper, lower], axis=0)


def dot_t(a, b):
    return lax.dot_general(a, b, (((1,), (1,)), ((), ())), preferred_element_type=F32)


def each_live(codes, visit):
    z = lax.rem(lax.axis_index("seq"), NZ)

    def source(src, carry):
        def pair(j, inner):
            code = codes[src, 0, j]

            @pl.when(((code >> 2) & (NZ - 1)) == z)
            def _():
                visit(src, j >> 1, ((code >> 5) << 2) + (code & 3))

            return inner

        return lax.fori_loop(0, PAIRS, pair, carry)

    lax.fori_loop(0, NZ, source, 0)


def stats_kernel(codes, q, g, k, v, stats):
    lanes = NZ * SPAN // 2
    stats[:, :, :lanes] = jnp.full((NZ, 8, lanes), NEVER, F32)
    stats[:, :, lanes:] = jnp.zeros((NZ, 8, lanes), F32)

    def visit(src, span, entry):
        row = src * SPANS_HERE + span
        for pair in range(2):
            columns = pl.ds(pair * 256, 256)
            q2 = two_heads(q[row, :, columns])
            g2 = two_heads(g[row, :, columns])
            scores = dot_t(k[entry, :, columns], q2) * SCALE
            prob_grad = dot_t(v[entry, :, columns], g2)
            top = jnp.max(scores, axis=0, keepdims=True)
            probs = jnp.exp(scores - top)
            total = jnp.sum(probs, axis=0, keepdims=True)
            lse = top + jnp.log(total)
            delta = jnp.sum(probs * prob_grad, axis=0, keepdims=True) / total
            at_lse, at_delta = pl.ds(pair * 128, 128), pl.ds(lanes + pair * 128, 128)
            here = lax.broadcasted_iota(jnp.int32, (8, 128), 0) == span
            old_lse, old_delta = stats[src, :, at_lse], stats[src, :, at_delta]
            high = jnp.maximum(old_lse, lse)
            old_part, new_part = jnp.exp(old_lse - high), jnp.exp(lse - high)
            both = old_part + new_part
            stats[src, :, at_lse] = jnp.where(here, high + jnp.log(both), old_lse)
            stats[src, :, at_delta] = jnp.where(
                here, (old_part * old_delta + new_part * delta) / both, old_delta
            )

    each_live(codes, visit)


def local_stats(codes, q, g, k, v):
    return pl.pallas_call(
        stats_kernel,
        out_shape=jax.ShapeDtypeStruct((NZ, 8, 512), F32),
        in_specs=[pl.BlockSpec(memory_space=pltpu.SMEM)]
        + [pl.BlockSpec(memory_space=pltpu.VMEM)] * 4,
        out_specs=pl.BlockSpec(memory_space=pltpu.VMEM),
        compiler_params=pltpu.CompilerParams(vmem_limit_bytes=VMEM_BYTES),
        name="local_stats",
    )(codes, q, g, k, v)


def totals_kernel(stats, out, got, summed, there, sems, back_sems):
    seq, head, x, z, _, _ = place()
    peers = [(x * NZ + lax.rem(z + d, NZ), head) for d in range(1, NZ)]
    meet(peers)
    copies = [
        remote(stats.at[lax.rem(z + d + 1, NZ)], got.at[d], sems, d, peers[d])
        for d in range(NZ - 1)
    ]
    for copy in copies:
        copy.start()
    for copy in copies:
        copy.wait_recv()
    terms = [stats[z]] + [got[d] for d in range(NZ - 1)]
    high = terms[0][:, :256]
    for term in terms[1:]:
        high = jnp.maximum(high, term[:, :256])
    both = jnp.zeros_like(high)
    delta = jnp.zeros_like(high)
    for term in terms:
        part = jnp.exp(term[:, :256] - high)
        both = both + part
        delta = delta + part * term[:, 256:]
    summed[:, :256] = high + jnp.log(both)
    summed[:, 256:] = delta / both
    returns = [remote(summed, there.at[d], back_sems, d, peers[d]) for d in range(NZ - 1)]
    for copy in returns:
        copy.start()
    out[z] = summed[...]
    for d in range(NZ - 1):
        returns[d].wait_recv()
        out[lax.rem(z + NZ - d - 1, NZ)] = there[d]
    for copy in copies + returns:
        copy.wait_send()


def all_totals(stats):
    shape = (NZ, 8, 512)
    vmem = pl.BlockSpec(memory_space=pltpu.VMEM)
    return pl.pallas_call(
        totals_kernel,
        out_shape=jax.ShapeDtypeStruct(shape, F32),
        in_specs=[vmem],
        out_specs=vmem,
        scratch_shapes=[
            pltpu.VMEM((NZ - 1, 8, 512), F32),
            pltpu.VMEM((8, 512), F32),
            pltpu.VMEM((NZ - 1, 8, 512), F32),
            pltpu.SemaphoreType.DMA((2, NZ - 1)),
            pltpu.SemaphoreType.DMA((2, NZ - 1)),
        ],
        compiler_params=pltpu.CompilerParams(collective_id=1, has_side_effects=True),
        name="all_totals",
    )(stats)


def grads_kernel(
    codes, q_in, g_in, k_in, v_in, totals, out, key_out, value_out,
    q, g, k, v, key_acc, value_acc, o, key_low, value_low, loads, stores,
):
    copies = [
        pltpu.make_async_copy(src, dst, loads.at[i])
        for i, (src, dst) in enumerate(((q_in, q), (k_in, k), (g_in, g), (v_in, v)))
    ]
    for copy in copies:
        copy.start()

    def clear(i, carry):
        o[i] = jnp.zeros((SPAN, WIDTH), BF)
        return carry

    lax.fori_loop(0, NZ * SPANS_HERE, clear, 0)

    def clear_acc(i, carry):
        key_acc[i] = jnp.zeros((KEYS, WIDTH), F32)
        value_acc[i] = jnp.zeros((KEYS, WIDTH), F32)
        return carry

    lax.fori_loop(0, NX * ENTRIES_HERE, clear_acc, 0)
    for copy in copies:
        copy.wait()

    def visit(src, span, entry):
        row = src * SPANS_HERE + span
        for pair in range(2):
            columns = pl.ds(pair * 256, 256)
            q2 = two_heads(q[row, :, columns])
            g2 = two_heads(g[row, :, columns])
            values = v[entry, :, columns]
            scores = dot_t(k[entry, :, columns], q2) * SCALE
            prob_grad = dot_t(values, g2)
            here = lax.broadcasted_iota(jnp.int32, (8, 128), 0) == span
            lse, delta = (
                jnp.sum(
                    jnp.where(here, totals[src, :, pl.ds(start + pair * 128, 128)], 0.0),
                    axis=0,
                    keepdims=True,
                )
                for start in (0, 256)
            )
            probs = jnp.exp(scores - lse)
            low = probs.astype(BF)
            score_grad = (probs * (prob_grad - delta)).astype(BF)
            key_acc[entry, :, columns] += jnp.dot(score_grad, q2, preferred_element_type=F32)
            value_acc[entry, :, columns] += jnp.dot(low, g2, preferred_element_type=F32)
            mixed = lax.dot_general(
                low, values, (((0,), (0,)), ((), ())), preferred_element_type=F32
            )
            for head in range(2):
                at = pl.ds(pair * 256 + head * 128, 128)
                term = mixed[head * SPAN : (head + 1) * SPAN, head * 128 : (head + 1) * 128]
                o[row, :, at] = (o[row, :, at].astype(F32) + term).astype(BF)

    each_live(codes, visit)

    out_copy = pltpu.make_async_copy(o, out, loads.at[0])
    out_copy.start()

    def store(i, which):
        low, to = ((key_low, key_out), (value_low, value_out))[which]
        return pltpu.make_async_copy(low.at[i], to.at[i], stores.at[which, i])

    def close(i, carry):
        key_low[i] = (key_acc[i] * SCALE).astype(BF)
        store(i, 0).start()
        value_low[i] = value_acc[i].astype(BF)
        store(i, 1).start()
        return carry

    def wait(i, carry):
        store(i, 0).wait()
        store(i, 1).wait()
        return carry

    lax.fori_loop(0, NX * ENTRIES_HERE, close, 0)
    out_copy.wait()
    lax.fori_loop(0, NX * ENTRIES_HERE, wait, 0)


def local_grads(codes, q, g, k, v, totals):
    entries = (NX * ENTRIES_HERE, KEYS, WIDTH)
    spans = (NZ * SPANS_HERE, SPAN, WIDTH)
    any_spec = pl.BlockSpec(memory_space=pl.ANY)
    return pl.pallas_call(
        grads_kernel,
        out_shape=(
            jax.ShapeDtypeStruct(spans, BF),
            jax.ShapeDtypeStruct(entries, BF),
            jax.ShapeDtypeStruct(entries, BF),
        ),
        in_specs=[pl.BlockSpec(memory_space=pltpu.SMEM)]
        + [any_spec] * 4
        + [pl.BlockSpec(memory_space=pltpu.VMEM)],
        out_specs=(any_spec,) * 3,
        scratch_shapes=[
            pltpu.VMEM(spans, BF), pltpu.VMEM(spans, BF),
            pltpu.VMEM(entries, BF), pltpu.VMEM(entries, BF),
            pltpu.VMEM(entries, F32), pltpu.VMEM(entries, F32),
            pltpu.VMEM(spans, BF), pltpu.VMEM(entries, BF), pltpu.VMEM(entries, BF),
            pltpu.SemaphoreType.DMA((4,)), pltpu.SemaphoreType.DMA((2, NX * ENTRIES_HERE)),
        ],
        compiler_params=pltpu.CompilerParams(vmem_limit_bytes=VMEM_BYTES),
        name="local_grads",
    )(codes, q, g, k, v, totals)


def finish_kernel(
    o, keys, values, cot, w,
    mixed, weight_grad, key_grad, value_grad,
    w_v, k_v, v_v, k_got, k_sums, v_got, v_sums, o_got, o_sums, att_raw, att, acc,
    wide, tall, wide_got, wide_sum, wide_z, tall_got, tall_sums, tall_sum, tall_x,
    local, k_sems, v_sems, o_sems, edge_sems, pair_sems, y_sems,
    wide_sems, wide_z_sems, tall_sems, tall_x_sems,
):
    seq, head, x, z, y, c = place()
    n_seq = NX * NZ
    before = (lax.rem(seq + n_seq - 1, n_seq), head)
    after = (lax.rem(seq + 1, n_seq), head)
    z_peers = [(x * NZ + lax.rem(z + d, NZ), head) for d in range(1, NZ)]
    x_peers = [(lax.rem(x + d, NX) * NZ + z, head) for d in range(1, NX)]
    sibling = (seq, 2 * y + 1 - c)
    own_k = pltpu.make_async_copy(keys, k_v, local.at[0])
    own_v = pltpu.make_async_copy(values, v_v, local.at[1])
    own_w = pltpu.make_async_copy(w, w_v, local.at[2])
    own_k.start()
    own_v.start()
    own_w.start()
    meet(z_peers + x_peers + list(Line("y").beside) + [sibling, before, after])
    o_ring = RingSum("z", o, ROWS, o_got, o_sums, o_sems)
    o_ring.start(0)
    own_k.wait()
    own_v.wait()
    k_ring = RingSum("x", k_v, 512, k_got, k_sums, k_sems)
    v_ring = RingSum("x", v_v, 512, v_got, v_sums, v_sems)
    k_ring.start(0)
    v_ring.start(0)
    o_ring.start(1)
    o_ring.start(2)
    k_ring.start(1)
    v_ring.start(1)
    o_ring.start(3)
    o_ring.wait_last()

    def put_out(rows, total):
        att_raw[pl.ds(pl.multiple_of(rows.start + SPAN, 32), 32), :] = total.astype(BF)

    o_ring.total(put_out, lambda rows: o[z, rows, :], 32)
    edge = remote(
        att_raw.at[pl.ds(ROWS, SPAN)], att_raw.at[pl.ds(0, SPAN)], edge_sems, 0, after
    )
    edge.start()
    edge.wait()
    lead = att_raw[pl.ds(0, SPAN), :]
    att_raw[pl.ds(0, SPAN), :] = jnp.where(seq == 0, jnp.zeros_like(lead), lead)

    def put_att(block, value):
        att[head, pl.ds(pl.multiple_of(block * SPAN, SPAN), SPAN), :] = value

    shift_rows(att_raw, 1, put_att)
    y_ring = Ring("y", att.at[head], att, ROWS, y_sems, lambda place: 2 * place + c)

    def pair_copy(j):
        block = att.at[2 * y_ring.line.off(j) + c]
        return remote(block, block, pair_sems, j, sibling)

    y_ring.start(0)
    pair_copy(0).start()
    own_w.wait()

    def use(block, first=False):
        rows = pl.ds(pl.multiple_of(block * WIDTH, WIDTH), WIDTH)
        term = jnp.dot(att[block], w_v[rows, :], preferred_element_type=F32)
        acc[...] = term if first else acc[...] + term
        terms = lax.dot_general(
            att[block], cot[...], (((0,), (0,)), ((), ())), preferred_element_type=F32
        ).astype(BF)
        to_x, part = block // 2, lax.rem(block, 2)
        wide[to_x, pl.ds(pl.multiple_of(part * WIDTH, WIDTH), WIDTH), :] = terms[:, :256]
        for i in range(4):
            tall[part * 4 + i, pl.ds(pl.multiple_of(to_x * 128, 128), 128), :] = terms[
                i * 128 : (i + 1) * 128, 256:
            ]

    def wide_copy(apart):
        to = lax.rem(x + apart, NX)
        return remote(
            wide.at[to], wide_got.at[apart - 1], wide_sems, apart - 1, (to * NZ + z, head)
        )

    def send_wide(to):
        apart = lax.rem(to - x + NX, NX)

        @pl.when(apart != 0)
        def _():
            wide_copy(apart).start()

    use(head, True)
    pair_copy(0).wait_recv()
    use(2 * y + 1 - c)
    send_wide(y)
    y_ring.start(1)
    y_ring.wait_others()
    pair_copy(1).start()
    pair_copy(3).start()
    for j in (1, 3, 2):
        if j == 2:
            y_ring.wait_mains()
            pair_copy(2).start()
        came = y_ring.line.off(j)
        use(2 * came + c)
        pair_copy(j).wait_recv()
        use(2 * came + 1 - c)
        send_wide(came)

    tall_ring = RingSum("z", tall, 512, tall_got, tall_sums, tall_sems)
    tall_ring.start(0)
    mixed[...] = acc[...].astype(BF)
    for ring, mine, out in ((k_ring, k_v, key_grad), (v_ring, v_v, value_grad)):
        ring.wait_last()

        def put(rows, total, out=out):
            out[rows, :] = total.astype(BF)

        ring.total(put, lambda rows, mine=mine: mine[x, rows, :], 32)
    tall_ring.start(1)
    tall_ring.start(2)
    for apart in range(1, NX):
        wide_copy(apart).wait_recv()

    def add_wide(i, carry):
        rows = pl.ds(pl.multiple_of(i * 128, 128), 128)
        total = wide[x, rows, :].astype(F32)
        for d in range(NX - 1):
            total = total + wide_got[d, rows, :].astype(F32)
        wide_sum[i] = total.astype(BF)
        return carry

    lax.fori_loop(0, NZ, add_wide, 0)
    wide_z_copies = [
        remote(wide_sum.at[lax.rem(z + d + 1, NZ)], wide_z.at[d], wide_z_sems, d, z_peers[d])
        for d in range(NZ - 1)
    ]
    for copy in wide_z_copies:
        copy.start()
    tall_ring.start(3)
    tall_ring.wait_last()

    def put_tall(rows, total):
        tall_sum[rows, :] = total.astype(BF)

    tall_ring.total(put_tall, lambda rows: tall[z, rows, :], 32)

    def x_rows(to):
        return pl.ds(pl.multiple_of(to * 128, 128), 128)

    tall_x_copies = [
        remote(
            tall_sum.at[x_rows(lax.rem(x + d + 1, NX))],
            tall_x.at[d], tall_x_sems, d, x_peers[d],
        )
        for d in range(NX - 1)
    ]
    for copy in tall_x_copies:
        copy.start()
    for copy in wide_z_copies:
        copy.wait_recv()
    total = wide_sum[z].astype(F32)
    for d in range(NZ - 1):
        total = total + wide_z[d].astype(F32)
    weight_grad[:, :256] = total.astype(BF)
    for copy in tall_x_copies:
        copy.wait_recv()
    total = tall_sum[x_rows(x), :].astype(F32)
    for d in range(NX - 1):
        total = total + tall_x[d].astype(F32)
    weight_grad[:, 256:] = total.astype(BF)

    for ring in (o_ring, k_ring, v_ring, tall_ring, y_ring):
        ring.wait_sends()
    for copy in wide_z_copies + tall_x_copies:
        copy.wait_send()
    for apart in range(1, NX):
        wide_copy(apart).wait_send()
    for j in range(NY):
        pair_copy(j).wait_send()


def finish(o, keys, values, cot, w):
    def vm(*shape):
        return pltpu.VMEM(shape, BF)

    def sems(n):
        return pltpu.SemaphoreType.DMA((2, n))

    any_spec = pl.BlockSpec(memory_space=pl.ANY)
    vmem = pl.BlockSpec(memory_space=pltpu.VMEM)
    entry = (ENTRIES_HERE * KEYS, WIDTH)
    return pl.pallas_call(
        finish_kernel,
        out_shape=(
            jax.ShapeDtypeStruct((ROWS, WIDTH), BF),
            jax.ShapeDtypeStruct((128, WIDTH), BF),
            jax.ShapeDtypeStruct(entry, BF),
            jax.ShapeDtypeStruct(entry, BF),
        ),
        in_specs=[vmem, any_spec, any_spec, vmem, any_spec],
        out_specs=(vmem,) * 4,
        scratch_shapes=[
            vm(8 * WIDTH, WIDTH), vm(NX, *entry), vm(NX, *entry),
            vm(2, 2, 2, 256, WIDTH), vm(2, 2, 2, 256, WIDTH),
            vm(2, 2, 2, 256, WIDTH), vm(2, 2, 2, 256, WIDTH),
            vm(2, 2, 4, HALF, WIDTH), vm(2, 2, 4, HALF, WIDTH),
            vm(ROWS + SPAN, WIDTH), vm(8, ROWS, WIDTH), pltpu.VMEM((ROWS, WIDTH), F32),
            vm(NX, 1024, 256), vm(NZ, 512, 256), vm(NX - 1, 1024, 256), vm(NZ, 128, 256),
            vm(NZ - 1, 128, 256), vm(2, 2, 4, 256, 256), vm(2, 2, 4, 256, 256),
            vm(512, 256), vm(NX - 1, 128, 256),
            pltpu.SemaphoreType.DMA((3,)), sems(8), sems(8), sems(16), sems(1), sems(4), sems(6),
            sems(3), sems(7), sems(16), sems(3),
        ],
        compiler_params=pltpu.CompilerParams(
            collective_id=2, has_side_effects=True, vmem_limit_bytes=VMEM_BYTES
        ),
        name="finish",
    )(o, keys, values, cot, w)


def publish_kernel(*refs):
    sems = refs[-1]
    copies = [
        pltpu.make_async_copy(refs[i], refs[4 + i], sems.at[i]) for i in range(4)
    ]
    for copy in copies:
        copy.start()
    for copy in copies:
        copy.wait()


def publish(*arrays):
    any_spec = pl.BlockSpec(memory_space=pl.ANY)
    return pl.pallas_call(
        publish_kernel,
        out_shape=tuple(jax.ShapeDtypeStruct(a.shape, a.dtype) for a in arrays),
        in_specs=[any_spec] * 4,
        out_specs=(any_spec,) * 4,
        scratch_shapes=[pltpu.SemaphoreType.DMA((4,))],
        name="publish",
    )(*arrays)


def body(queries, cache_keys, cache_values, owners, slots, out_weight, cotangent):
    codes = (owners * ENTRIES_HERE + slots).reshape(1, PAIRS)
    codes = jnp.pad(codes, ((0, 7), (0, 128 - PAIRS)))
    q, g, k, v, codes = gather_all(
        queries, cache_keys, cache_values, codes, cotangent, out_weight
    )
    q = q.reshape(NZ * SPANS_HERE, SPAN, WIDTH)
    g = g.reshape(NZ * SPANS_HERE, SPAN, WIDTH)
    k = k.reshape(NX * ENTRIES_HERE, KEYS, WIDTH)
    v = v.reshape(NX * ENTRIES_HERE, KEYS, WIDTH)
    totals = all_totals(local_stats(codes, q, g, k, v))
    out, key_terms, value_terms = local_grads(codes, q, g, k, v, totals)
    entries = (NX, ENTRIES_HERE * KEYS, WIDTH)
    mixed, weight_grad, key_grad, value_grad = publish(
        *finish(
            out.reshape(NZ, ROWS, WIDTH),
            key_terms.reshape(entries),
            value_terms.reshape(entries),
            cotangent,
            out_weight,
        )
    )
    shape = (ENTRIES_HERE, KEYS, WIDTH)
    return mixed, weight_grad, key_grad.reshape(shape), value_grad.reshape(shape)


def solution(mesh):
    placed = (
        P("seq", "head"),
        P("seq", None, "head"),
        P("seq", None, "head"),
        P("seq", None),
        P("seq", None),
        P(None, "head"),
        P("seq", "head"),
    )
    return jax.shard_map(
        body,
        mesh=mesh,
        in_specs=placed,
        out_specs=(
            P("seq", "head"),
            P("seq", "head"),
            P("seq", None, "head"),
            P("seq", None, "head"),
        ),
        check_vma=False,
    )
```

```python
import functools
import math

import jax
import jax.numpy as jnp
from jax import lax
from jax.experimental import pallas as pl
from jax.experimental.pallas import tpu as pltpu
from jax.sharding import PartitionSpec as P

HEAD_DIM = 128
SPAN = 64
TOP = 2
NX, NZ, NY = 4, 8, 4
ROWS, WIDTH = 448, 512
SPANS_HERE = 7
PAIRS = SPANS_HERE * TOP
ENTRIES_HERE = 4
KEYS = 128
HALF = ROWS // 2
SCALE = 1.0 / math.sqrt(HEAD_DIM)
NEVER = -1e30
VMEM_BYTES = 56 * 1024 * 1024
MESH_ID = pl.DeviceIdType.MESH
BF, F32 = jnp.bfloat16, jnp.float32


def place():
    seq, head = lax.axis_index("seq"), lax.axis_index("head")
    return seq, head, seq // NZ, lax.rem(seq, NZ), head // 2, lax.rem(head, 2)


def remote(src, dst, sems, index, device):
    return pltpu.make_async_remote_copy(
        src_ref=src,
        dst_ref=dst,
        send_sem=sems.at[0, index],
        recv_sem=sems.at[1, index],
        device_id=device,
        device_id_type=MESH_ID,
    )


def meet(devices):
    sem = pltpu.get_barrier_semaphore()
    for device in devices:
        pl.semaphore_signal(sem, inc=1, device_id=device, device_id_type=MESH_ID)
    pl.semaphore_wait(sem, len(devices))


def selector(step):
    row = lax.broadcasted_iota(jnp.int32, (SPAN, 2 * SPAN), 0)
    column = lax.broadcasted_iota(jnp.int32, (SPAN, 2 * SPAN), 1)
    return (column == row + step).astype(F32).astype(BF)


def shift_rows(raw, step, write):
    pick = selector(step)

    def one(block, carry):
        window = raw[pl.ds(pl.multiple_of(block * SPAN, SPAN), 2 * SPAN), :]
        write(block, jnp.dot(pick, window, preferred_element_type=F32).astype(BF))
        return carry

    lax.fori_loop(0, SPANS_HERE, one, 0)


class Line:
    def __init__(self, axis):
        seq, head, x, z, y, c = place()
        if axis == "z":
            self.n, self.at, to = NZ, z, lambda i: (x * NZ + i, head)
        elif axis == "x":
            self.n, self.at, to = NX, x, lambda i: (i * NZ + z, head)
        else:
            self.n, self.at, to = NY, y, lambda i: (seq, 2 * i + c)
        self.half = self.n // 2
        self.beside = (to(self.off(1)), to(self.off(-1)))

    def off(self, steps):
        return lax.rem(self.at + steps + self.n, self.n)


class Ring:
    def __init__(self, axis, first, out, rows, sems, slot=lambda place: place):
        self.line, self.first, self.out, self.sems, self.slot = (
            Line(axis), first, out, sems, slot,
        )
        self.rows = rows // 2

    def copy(self, way, main, step):
        slot = self.slot(self.line.off(step if way else -step))
        half = way if main else 1 - way
        rows = pl.ds(half * self.rows, self.rows)
        dst = self.out.at[slot, rows]
        src = dst if step else self.first.at[rows]
        index = way * (self.line.n - 1) + (0 if main else self.line.half) + step
        return remote(src, dst, self.sems, index, self.line.beside[way])

    def start(self, step):
        for main in (True, False):
            if main or step < self.line.half - 1:
                for way in range(2):
                    if step:
                        self.copy(way, main, step - 1).wait_recv()
                    self.copy(way, main, step).start()

    def wait_others(self):
        for way in range(2):
            self.copy(way, False, self.line.half - 2).wait_recv()

    def wait_mains(self):
        for way in range(2):
            self.copy(way, True, self.line.half - 1).wait_recv()

    def wait_sends(self):
        for way in range(2):
            for step in range(self.line.half):
                self.copy(way, True, step).wait_send()
            for step in range(self.line.half - 1):
                self.copy(way, False, step).wait_send()

    def finish(self):
        self.wait_others()
        self.wait_mains()
        self.wait_sends()


class RingSum:
    def __init__(self, axis, blocks, rows, got, sums, sems):
        self.line = Line(axis)
        self.blocks, self.got, self.sums, self.sems = blocks, got, sums, sems
        self.rows = rows // 2

    def copy(self, way, main, step):
        half = way if main else 1 - way
        if step == (0 if main else 1):
            far = self.line.half - step
            block = self.line.off(-far if way else far)
            src = self.blocks.at[block, pl.ds(half * self.rows, self.rows)]
        else:
            src = self.sums.at[way, half, step]
        index = way * self.line.n + (0 if main else self.line.half) + step
        dst = self.got.at[way, half, step]
        return remote(src, dst, self.sems, index, self.line.beside[way])

    def send(self, way, main, step):
        half = way if main else 1 - way
        if step > (0 if main else 1):
            self.copy(way, main, step - 1).wait_recv()
            far = self.line.half - step
            block = self.line.off(-far if way else far)
            piece = 32

            def add(i, carry):
                rows = pl.ds(pl.multiple_of(i * piece, piece), piece)
                from_rows = pl.ds(pl.multiple_of(half * self.rows + i * piece, piece), piece)
                self.sums[way, half, step, rows, :] = (
                    self.blocks[block, from_rows, :].astype(F32)
                    + self.got[way, half, step - 1, rows, :].astype(F32)
                ).astype(BF)
                return carry

            lax.fori_loop(0, self.rows // piece, add, 0)
        self.copy(way, main, step).start()

    def start(self, step):
        for way in range(2):
            self.send(way, True, step)
        if step + 1 < self.line.half:
            for way in range(2):
                self.send(way, False, step + 1)

    def wait_last(self):
        for main in (False, True):
            for way in range(2):
                self.copy(way, main, self.line.half - 1).wait_recv()

    def wait_sends(self):
        for way in range(2):
            for step in range(self.line.half):
                self.copy(way, True, step).wait_send()
            for step in range(1, self.line.half):
                self.copy(way, False, step).wait_send()

    def total(self, write, mine, piece):
        for half in range(2):

            def one(i, carry):
                rows = pl.ds(pl.multiple_of(i * piece, piece), piece)
                at = pl.ds(pl.multiple_of(half * self.rows + i * piece, piece), piece)
                term = mine(at).astype(F32)
                for way in range(2):
                    term = term + self.got[way, half, self.line.half - 1, rows, :].astype(F32)
                write(at, term)
                return carry

            lax.fori_loop(0, self.rows // piece, one, 0)


def gather_kernel(
    q, k, v, codes, cot, w,
    q_all, g_own, k_all, v_all, codes_all,
    q_raw, q_sh, g_raw, g_sh, cot_v, w_v, part, pair_got, y_blocks, y_got, y_sums, g_acc,
    local, q_sems, k_sems, v_sems, code_sems, edge_sems, pair_sems, y_sems,
):
    seq, head, x, z, y, c = place()
    n_seq = NX * NZ
    before = (lax.rem(seq + n_seq - 1, n_seq), head)
    after = (lax.rem(seq + 1, n_seq), head)
    z_peers = [(x * NZ + lax.rem(z + d, NZ), head) for d in range(1, NZ)]
    sibling = (seq, 2 * y + 1 - c)
    own_q = pltpu.make_async_copy(q, q_raw.at[pl.ds(0, ROWS)], local.at[0])
    own_cot = pltpu.make_async_copy(cot, cot_v, local.at[1])
    own_w = pltpu.make_async_copy(w, w_v, local.at[2])
    own_q.start()
    own_cot.start()
    own_w.start()
    meet(
        z_peers + list(Line("x").beside) + list(Line("y").beside) + [sibling, before, after]
    )
    q_edge = remote(q.at[pl.ds(0, SPAN)], q_raw.at[pl.ds(ROWS, SPAN)], edge_sems, 0, before)
    q_edge.start()
    k_ring = Ring("x", k, k_all, ENTRIES_HERE, k_sems)
    v_ring = Ring("x", v, v_all, ENTRIES_HERE, v_sems)
    k_ring.start(0)
    v_ring.start(0)
    code_copies = [
        remote(codes, codes_all.at[z], code_sems, d, z_peers[d]) for d in range(NZ - 1)
    ]
    for copy in code_copies:
        copy.start()
    own_k = pltpu.make_async_copy(k, k_all.at[x], local.at[3])
    own_v = pltpu.make_async_copy(v, v_all.at[x], local.at[4])
    own_codes = pltpu.make_async_copy(codes, codes_all.at[z], local.at[5])
    own_k.start()
    own_v.start()
    own_codes.start()
    own_q.wait()
    q_edge.wait()
    last = seq == n_seq - 1
    tail = q_raw[pl.ds(ROWS, SPAN), :]
    q_raw[pl.ds(ROWS, SPAN), :] = jnp.where(last, jnp.zeros_like(tail), tail)

    def put_q(block, value):
        q_sh[pl.ds(pl.multiple_of(block * SPAN, SPAN), SPAN), :] = value

    shift_rows(q_raw, SPAN - 1, put_q)
    q_ring = Ring("z", q_sh, q_all, ROWS, q_sems)
    q_ring.start(0)
    keep_q = pltpu.make_async_copy(q_sh, q_all.at[z], local.at[6])
    keep_q.start()

    own_cot.wait()
    own_w.wait()

    def product(to_head):
        rows = pl.ds(pl.multiple_of(to_head * WIDTH, WIDTH), WIDTH)
        return lax.dot_general(
            cot_v[...], w_v[rows, :], (((1,), (1,)), ((), ())), preferred_element_type=F32
        )

    def pair_copy(j):
        return remote(part.at[j], pair_got.at[j], pair_sems, j, sibling)

    def for_sibling(i, carry):
        j = NY - 1 - i
        part[j] = product(2 * lax.rem(y + j, NY) + 1 - c).astype(BF)
        pair_copy(j).start()
        return carry

    lax.fori_loop(0, NY, for_sibling, 0)

    def for_row(i, carry):
        j = NY - 1 - i
        to = lax.rem(y + j, NY)
        value = product(2 * to + c)
        pair_copy(j).wait_recv()
        y_blocks[to] = (value + pair_got[j].astype(F32)).astype(BF)
        return carry

    lax.fori_loop(0, NY - 1, for_row, 0)
    y_ring = RingSum("y", y_blocks, ROWS, y_got, y_sums, y_sems)
    y_ring.start(0)
    mine = product(2 * y + c)
    pair_copy(0).wait_recv()
    g_acc[...] = mine + pair_got[0].astype(F32)
    q_ring.start(1)
    y_ring.start(1)
    k_ring.start(1)
    q_ring.start(2)
    v_ring.start(1)
    y_ring.wait_last()

    def put_g(rows, total):
        g_raw[rows, :] = total.astype(BF)

    y_ring.total(put_g, lambda rows: g_acc[rows, :], 32)
    g_edge = remote(
        g_raw.at[pl.ds(0, SPAN)], g_raw.at[pl.ds(ROWS, SPAN)], edge_sems, 1, before
    )
    g_edge.start()
    q_ring.start(3)
    g_edge.wait()
    tail = g_raw[pl.ds(ROWS, SPAN), :]
    g_raw[pl.ds(ROWS, SPAN), :] = jnp.where(last, jnp.zeros_like(tail), tail)

    def put_gs(block, value):
        g_sh[pl.ds(pl.multiple_of(block * SPAN, SPAN), SPAN), :] = value

    shift_rows(g_raw, SPAN - 1, put_gs)
    keep_g = pltpu.make_async_copy(g_sh, g_own, local.at[7])
    keep_g.start()
    q_ring.finish()
    k_ring.finish()
    v_ring.finish()
    for copy in code_copies:
        copy.wait()
    for j in range(NY):
        pair_copy(j).wait_send()
    y_ring.wait_sends()
    own_k.wait()
    own_v.wait()
    own_codes.wait()
    keep_q.wait()
    keep_g.wait()


def gather_all(q, k, v, codes, cot, w):
    def vm(*shape):
        return pltpu.VMEM(shape, BF)

    def sems(n):
        return pltpu.SemaphoreType.DMA((2, n))

    any_spec = pl.BlockSpec(memory_space=pl.ANY)
    entries = (NX, ENTRIES_HERE, KEYS, WIDTH)
    return pl.pallas_call(
        gather_kernel,
        out_shape=(
            jax.ShapeDtypeStruct((NZ, ROWS, WIDTH), BF),
            jax.ShapeDtypeStruct((ROWS, WIDTH), BF),
            jax.ShapeDtypeStruct(entries, BF),
            jax.ShapeDtypeStruct(entries, BF),
            jax.ShapeDtypeStruct((NZ, 8, 128), jnp.int32),
        ),
        in_specs=[any_spec] * 6,
        out_specs=(any_spec,) * 5,
        scratch_shapes=[
            vm(ROWS + SPAN, WIDTH), vm(ROWS, WIDTH), vm(ROWS + SPAN, WIDTH), vm(ROWS, WIDTH),
            vm(ROWS, WIDTH), vm(8 * WIDTH, WIDTH), vm(NY, ROWS, WIDTH), vm(NY, ROWS, WIDTH),
            vm(NY, ROWS, WIDTH), vm(2, 2, 2, HALF, WIDTH), vm(2, 2, 2, HALF, WIDTH),
            pltpu.VMEM((ROWS, WIDTH), F32),
            pltpu.SemaphoreType.DMA((8,)), sems(14), sems(6), sems(6), sems(7),
            sems(2), sems(4), sems(8),
        ],
        compiler_params=pltpu.CompilerParams(
            collective_id=0, has_side_effects=True, vmem_limit_bytes=VMEM_BYTES
        ),
        name="gather_all",
    )(q, k, v, codes, cot, w)


def two_heads(block):
    lane = lax.broadcasted_iota(jnp.int32, block.shape, 1)
    zero = jnp.zeros_like(block)
    upper = jnp.where(lane < HEAD_DIM, block, zero)
    lower = jnp.where(lane < HEAD_DIM, zero, block)
    return jnp.concatenate([upper, lower], axis=0)


def dot_t(a, b):
    return lax.dot_general(a, b, (((1,), (1,)), ((), ())), preferred_element_type=F32)


def each_live(codes, visit):
    z = lax.rem(lax.axis_index("seq"), NZ)

    def source(src, carry):
        def pair(j, inner):
            code = codes[src, 0, j]

            @pl.when(((code >> 2) & (NZ - 1)) == z)
            def _():
                visit(src, j >> 1, ((code >> 5) << 2) + (code & 3))

            return inner

        return lax.fori_loop(0, PAIRS, pair, carry)

    lax.fori_loop(0, NZ, source, 0)


def cost(megabytes):
    return pl.CostEstimate(flops=0, transcendentals=0, bytes_accessed=megabytes * 1000000)


def stats_kernel(codes, q, k, stats):
    stats[...] = jnp.full((NZ, 8, 256), NEVER, F32)

    def visit(src, span, entry):
        row = src * SPANS_HERE + span
        here = lax.broadcasted_iota(jnp.int32, (8, 128), 0) == span
        for pair in range(2):
            columns = pl.ds(pair * 256, 256)
            scores = dot_t(k[entry, :, columns], two_heads(q[row, :, columns])) * SCALE
            top = jnp.max(scores, axis=0, keepdims=True)
            lse = top + jnp.log(jnp.sum(jnp.exp(scores - top), axis=0, keepdims=True))
            at = pl.ds(pair * 128, 128)
            old = stats[src, :, at]
            high = jnp.maximum(old, lse)
            both = high + jnp.log(jnp.exp(old - high) + jnp.exp(lse - high))
            stats[src, :, at] = jnp.where(here, both, old)

    each_live(codes, visit)


def local_stats(codes, q, k):
    vmem = pl.BlockSpec(memory_space=pltpu.VMEM)
    return pl.pallas_call(
        stats_kernel,
        out_shape=jax.ShapeDtypeStruct((NZ, 8, 256), F32),
        in_specs=[pl.BlockSpec(memory_space=pltpu.SMEM), vmem, vmem],
        out_specs=vmem,
        compiler_params=pltpu.CompilerParams(vmem_limit_bytes=VMEM_BYTES),
        cost_estimate=cost(30),
        name="local_stats",
    )(codes, q, k)


def totals_kernel(stats, out, got, summed, there, sems, back_sems):
    seq, head, x, z, _, _ = place()
    peers = [(x * NZ + lax.rem(z + d, NZ), head) for d in range(1, NZ)]
    meet(peers)
    copies = [
        remote(stats.at[lax.rem(z + d + 1, NZ)], got.at[d], sems, d, peers[d])
        for d in range(NZ - 1)
    ]
    for copy in copies:
        copy.start()
    for copy in copies:
        copy.wait_recv()
    terms = [stats[z]] + [got[d] for d in range(NZ - 1)]
    high = terms[0]
    for term in terms[1:]:
        high = jnp.maximum(high, term)
    both = jnp.zeros_like(high)
    for term in terms:
        both = both + jnp.exp(term - high)
    summed[...] = high + jnp.log(both)
    returns = [remote(summed, there.at[d], back_sems, d, peers[d]) for d in range(NZ - 1)]
    for copy in returns:
        copy.start()
    out[z] = summed[...]
    for d in range(NZ - 1):
        returns[d].wait_recv()
        out[lax.rem(z + NZ - d - 1, NZ)] = there[d]
    for copy in copies + returns:
        copy.wait_send()


def all_totals(stats):
    shape = (NZ, 8, 256)
    vmem = pl.BlockSpec(memory_space=pltpu.VMEM)
    return pl.pallas_call(
        totals_kernel,
        out_shape=jax.ShapeDtypeStruct(shape, F32),
        in_specs=[vmem],
        out_specs=vmem,
        scratch_shapes=[
            pltpu.VMEM((NZ - 1, 8, 256), F32),
            pltpu.VMEM((8, 256), F32),
            pltpu.VMEM((NZ - 1, 8, 256), F32),
            pltpu.SemaphoreType.DMA((2, NZ - 1)),
            pltpu.SemaphoreType.DMA((2, NZ - 1)),
        ],
        compiler_params=pltpu.CompilerParams(collective_id=1, has_side_effects=True),
        cost_estimate=cost(30),
        name="all_totals",
    )(stats)


def row_of(table, src, span, pair):
    here = lax.broadcasted_iota(jnp.int32, (8, 128), 0) == span
    block = table[src, :, pl.ds(pair * 128, 128)]
    return jnp.sum(jnp.where(here, block, 0.0), axis=0, keepdims=True)


def outputs_kernel(codes, q, k, v, totals, o):
    def clear(i, carry):
        o[i] = jnp.zeros((SPAN, WIDTH), BF)
        return carry

    lax.fori_loop(0, NZ * SPANS_HERE, clear, 0)

    def visit(src, span, entry):
        row = src * SPANS_HERE + span
        for pair in range(2):
            columns = pl.ds(pair * 256, 256)
            scores = dot_t(k[entry, :, columns], two_heads(q[row, :, columns])) * SCALE
            probs = jnp.exp(scores - row_of(totals, src, span, pair)).astype(BF)
            mixed = lax.dot_general(
                probs, v[entry, :, columns], (((0,), (0,)), ((), ())), preferred_element_type=F32
            )
            for head in range(2):
                at = pl.ds(pair * 256 + head * 128, 128)
                term = mixed[head * SPAN : (head + 1) * SPAN, head * 128 : (head + 1) * 128]
                o[row, :, at] = (o[row, :, at].astype(F32) + term).astype(BF)

    each_live(codes, visit)


def local_outputs(codes, q, k, v, totals):
    vmem = pl.BlockSpec(memory_space=pltpu.VMEM)
    return pl.pallas_call(
        outputs_kernel,
        out_shape=jax.ShapeDtypeStruct((NZ * SPANS_HERE, SPAN, WIDTH), BF),
        in_specs=[pl.BlockSpec(memory_space=pltpu.SMEM)] + [vmem] * 4,
        out_specs=vmem,
        compiler_params=pltpu.CompilerParams(vmem_limit_bytes=VMEM_BYTES),
        cost_estimate=cost(40),
        name="local_outputs",
    )(codes, q, k, v, totals)


def step(ahead, back):
    right = [(x * NZ + z, x * NZ + (z + 1) % NZ) for x in range(NX) for z in range(NZ)]
    left = [(b, a) for a, b in right]
    return lax.ppermute(ahead, "seq", right), lax.ppermute(back, "seq", left)


def grads_kernel(
    codes, q_in, k_in, v_in, g0, l1, r1, l2, r2, l3, r3, l4, r4, totals, deltas,
    key_out, value_out,
    q, k, v, g, key_acc, value_acc, key_low, value_low, loads, stores,
):
    z = lax.rem(lax.axis_index("seq"), NZ)

    def slot(steps):
        return g.at[lax.rem(z + steps + NZ, NZ)]

    moves = [
        (q_in, q), (k_in, k), (v_in, v), (g0, slot(0)),
        (l1, slot(-1)), (r1, slot(1)), (l2, slot(-2)), (r2, slot(2)), (l3, slot(-3)),
        (r3, slot(3)), (l4, slot(4).at[pl.ds(0, HALF)]), (r4, slot(4).at[pl.ds(HALF, HALF)]),
    ]
    copies = [pltpu.make_async_copy(*move, loads.at[i]) for i, move in enumerate(moves)]
    for copy in copies:
        copy.start()

    def clear_acc(i, carry):
        key_acc[i] = jnp.zeros((KEYS, WIDTH), F32)
        value_acc[i] = jnp.zeros((KEYS, WIDTH), F32)
        return carry

    lax.fori_loop(0, NX * ENTRIES_HERE, clear_acc, 0)
    for copy in copies:
        copy.wait()

    def visit(src, span, entry):
        row = src * SPANS_HERE + span
        rows = pl.ds(pl.multiple_of(span * SPAN, SPAN), SPAN)
        for pair in range(2):
            columns = pl.ds(pair * 256, 256)
            q2 = two_heads(q[row, :, columns])
            g2 = two_heads(g[src, rows, columns])
            scores = dot_t(k[entry, :, columns], q2) * SCALE
            prob_grad = dot_t(v[entry, :, columns], g2)
            probs = jnp.exp(scores - row_of(totals, src, span, pair))
            delta = row_of(deltas, src, span, pair)
            score_grad = (probs * (prob_grad - delta)).astype(BF)
            key_acc[entry, :, columns] += jnp.dot(score_grad, q2, preferred_element_type=F32)
            value_acc[entry, :, columns] += jnp.dot(
                probs.astype(BF), g2, preferred_element_type=F32
            )

    each_live(codes, visit)

    def store(i, which):
        low, to = ((key_low, key_out), (value_low, value_out))[which]
        return pltpu.make_async_copy(low.at[i], to.at[i], stores.at[which, i])

    def close(i, carry):
        key_low[i] = (key_acc[i] * SCALE).astype(BF)
        store(i, 0).start()
        value_low[i] = value_acc[i].astype(BF)
        store(i, 1).start()
        return carry

    def wait(i, carry):
        store(i, 0).wait()
        store(i, 1).wait()
        return carry

    lax.fori_loop(0, NX * ENTRIES_HERE, close, 0)
    lax.fori_loop(0, NX * ENTRIES_HERE, wait, 0)


def local_grads(codes, q, k, v, grads, totals, deltas):
    entries = (NX * ENTRIES_HERE, KEYS, WIDTH)
    any_spec = pl.BlockSpec(memory_space=pl.ANY)
    vmem = pl.BlockSpec(memory_space=pltpu.VMEM)
    return pl.pallas_call(
        grads_kernel,
        out_shape=(jax.ShapeDtypeStruct(entries, BF),) * 2,
        in_specs=[pl.BlockSpec(memory_space=pltpu.SMEM)] + [any_spec] * 12 + [vmem] * 2,
        out_specs=(any_spec,) * 2,
        scratch_shapes=[
            pltpu.VMEM((NZ * SPANS_HERE, SPAN, WIDTH), BF),
            pltpu.VMEM(entries, BF), pltpu.VMEM(entries, BF),
            pltpu.VMEM((NZ, ROWS, WIDTH), BF),
            pltpu.VMEM(entries, F32), pltpu.VMEM(entries, F32),
            pltpu.VMEM(entries, BF), pltpu.VMEM(entries, BF),
            pltpu.SemaphoreType.DMA((12,)), pltpu.SemaphoreType.DMA((2, NX * ENTRIES_HERE)),
        ],
        compiler_params=pltpu.CompilerParams(vmem_limit_bytes=VMEM_BYTES),
        cost_estimate=cost(100),
        name="local_grads",
    )(codes, q, k, v, *grads, totals, deltas)


def attend_kernel(
    o, g, cot, w,
    mixed, tall, wide_0, wide_1, wide_2, wide_3, deltas,
    w_v, o_got, o_sums, att_raw, att, acc, wide, delta_mine,
    local, o_sems, edge_sems, pair_sems, y_sems, delta_sems,
):
    seq, head, x, z, y, c = place()
    n_seq = NX * NZ
    before = (lax.rem(seq + n_seq - 1, n_seq), head)
    after = (lax.rem(seq + 1, n_seq), head)
    z_peers = [(x * NZ + lax.rem(z + d, NZ), head) for d in range(1, NZ)]
    sibling = (seq, 2 * y + 1 - c)
    own_w = pltpu.make_async_copy(w, w_v, local.at[0])
    own_w.start()
    meet(z_peers + list(Line("y").beside) + [sibling, before, after])
    o_ring = RingSum("z", o, ROWS, o_got, o_sums, o_sems)
    for step in range(4):
        o_ring.start(step)
    o_ring.wait_last()

    def put_out(rows, total):
        att_raw[pl.ds(pl.multiple_of(rows.start + SPAN, 32), 32), :] = total.astype(BF)

    o_ring.total(put_out, lambda rows: o[z, rows, :], 32)
    edge = remote(
        att_raw.at[pl.ds(ROWS, SPAN)], att_raw.at[pl.ds(0, SPAN)], edge_sems, 0, after
    )
    edge.start()
    edge.wait()
    lead = att_raw[pl.ds(0, SPAN), :]
    att_raw[pl.ds(0, SPAN), :] = jnp.where(seq == 0, jnp.zeros_like(lead), lead)

    def put_att(block, value):
        att[head, pl.ds(pl.multiple_of(block * SPAN, SPAN), SPAN), :] = value

    shift_rows(att_raw, 1, put_att)
    y_ring = Ring("y", att.at[head], att, ROWS, y_sems, lambda place: 2 * place + c)

    def pair_copy(j):
        block = att.at[2 * y_ring.line.off(j) + c]
        return remote(block, block, pair_sems, j, sibling)

    y_ring.start(0)
    pair_copy(0).start()

    delta_mine[...] = jnp.zeros((8, 256), F32)
    for span in range(SPANS_HERE):
        rows = pl.ds(span * SPAN, SPAN)
        terms = g[rows, :].astype(F32) * att_raw[pl.ds((span + 1) * SPAN, SPAN), :].astype(F32)
        for pair in range(2):
            start = pair * 256
            both = jnp.concatenate(
                [terms[:, start : start + 128], terms[:, start + 128 : start + 256]], axis=0
            )
            row = lax.dot_general(
                jnp.ones((8, 128), F32), both, (((1,), (1,)), ((), ())),
                precision=lax.Precision.HIGHEST, preferred_element_type=F32,
            )
            delta_mine[pl.ds(span, 1), pl.ds(pair * 128, 128)] = row[:1]
    deltas[z] = delta_mine[...]
    delta_copies = [
        remote(delta_mine, deltas.at[z], delta_sems, d, z_peers[d]) for d in range(NZ - 1)
    ]
    for copy in delta_copies:
        copy.start()
    own_w.wait()

    def use(block, first=False):
        rows = pl.ds(pl.multiple_of(block * WIDTH, WIDTH), WIDTH)
        term = jnp.dot(att[block], w_v[rows, :], preferred_element_type=F32)
        acc[...] = term if first else acc[...] + term
        terms = lax.dot_general(
            att[block], cot[...], (((0,), (0,)), ((), ())), preferred_element_type=F32
        ).astype(BF)
        to_x, part = block // 2, lax.rem(block, 2)
        wide[to_x, pl.ds(pl.multiple_of(part * WIDTH, WIDTH), WIDTH), :] = terms[:, :256]
        for i in range(4):
            tall[part * 4 + i, pl.ds(pl.multiple_of(to_x * 128, 128), 128), :] = terms[
                i * 128 : (i + 1) * 128, 256:
            ]

    use(head, True)
    pair_copy(0).wait_recv()
    use(2 * y + 1 - c)
    y_ring.start(1)
    y_ring.wait_others()
    pair_copy(1).start()
    pair_copy(3).start()
    for j in (1, 3, 2):
        if j == 2:
            y_ring.wait_mains()
            pair_copy(2).start()
        came = y_ring.line.off(j)
        use(2 * came + c)
        pair_copy(j).wait_recv()
        use(2 * came + 1 - c)
    wide_copies = [
        pltpu.make_async_copy(wide.at[lax.rem(x + apart, NX)], out, local.at[apart])
        for apart, out in enumerate((wide_0, wide_1, wide_2, wide_3))
    ]
    for copy in wide_copies:
        copy.start()
    mixed[...] = acc[...].astype(BF)
    o_ring.wait_sends()
    y_ring.wait_sends()
    for copy in delta_copies:
        copy.wait()
    for j in range(NY):
        pair_copy(j).wait_send()
    for copy in wide_copies:
        copy.wait()


def attend(o, g, cot, w):
    def vm(*shape):
        return pltpu.VMEM(shape, BF)

    def sems(n):
        return pltpu.SemaphoreType.DMA((2, n))

    any_spec = pl.BlockSpec(memory_space=pl.ANY)
    vmem = pl.BlockSpec(memory_space=pltpu.VMEM)
    wide = jax.ShapeDtypeStruct((1024, 256), BF)
    return pl.pallas_call(
        attend_kernel,
        out_shape=(
            jax.ShapeDtypeStruct((ROWS, WIDTH), BF),
            jax.ShapeDtypeStruct((NZ, 512, 256), BF),
            wide, wide, wide, wide,
            jax.ShapeDtypeStruct((NZ, 8, 256), F32),
        ),
        in_specs=[vmem, vmem, vmem, any_spec],
        out_specs=(vmem, vmem) + (any_spec,) * 4 + (vmem,),
        scratch_shapes=[
            vm(8 * WIDTH, WIDTH), vm(2, 2, 4, HALF, WIDTH), vm(2, 2, 4, HALF, WIDTH),
            vm(ROWS + SPAN, WIDTH), vm(8, ROWS, WIDTH), pltpu.VMEM((ROWS, WIDTH), F32),
            vm(NX, 1024, 256), pltpu.VMEM((8, 256), F32),
            pltpu.SemaphoreType.DMA((4,)), sems(16), sems(1), sems(4), sems(6), sems(7),
        ],
        compiler_params=pltpu.CompilerParams(
            collective_id=2, has_side_effects=True, vmem_limit_bytes=VMEM_BYTES
        ),
        cost_estimate=cost(220),
        name="attend",
    )(o, g, cot, w)


def finish_kernel(
    keys, values, tall, wide_0, wide_1, wide_2, wide_3,
    weight_grad, key_grad, value_grad,
    k_v, v_v, k_got, k_sums, v_got, v_sums,
    wide_sum, wide_z, tall_got, tall_sums, tall_sum, tall_x,
    local, k_sems, v_sems, wide_z_sems, tall_sems, tall_x_sems,
):
    seq, head, x, z, y, c = place()
    z_peers = [(x * NZ + lax.rem(z + d, NZ), head) for d in range(1, NZ)]
    x_peers = [(lax.rem(x + d, NX) * NZ + z, head) for d in range(1, NX)]
    own_k = pltpu.make_async_copy(keys, k_v, local.at[0])
    own_v = pltpu.make_async_copy(values, v_v, local.at[1])
    own_k.start()
    own_v.start()
    meet(z_peers + x_peers)
    tall_ring = RingSum("z", tall, 512, tall_got, tall_sums, tall_sems)
    tall_ring.start(0)
    own_k.wait()
    own_v.wait()
    k_ring = RingSum("x", k_v, 512, k_got, k_sums, k_sems)
    v_ring = RingSum("x", v_v, 512, v_got, v_sums, v_sems)
    k_ring.start(0)
    v_ring.start(0)

    def add_wide(i, carry):
        rows = pl.ds(pl.multiple_of(i * 128, 128), 128)
        total = wide_0[rows, :].astype(F32)
        for term in (wide_1, wide_2, wide_3):
            total = total + term[rows, :].astype(F32)
        wide_sum[i] = total.astype(BF)
        return carry

    lax.fori_loop(0, NZ, add_wide, 0)
    wide_z_copies = [
        remote(wide_sum.at[lax.rem(z + d + 1, NZ)], wide_z.at[d], wide_z_sems, d, z_peers[d])
        for d in range(NZ - 1)
    ]
    tall_ring.start(1)
    tall_ring.start(2)
    k_ring.start(1)
    for copy in wide_z_copies:
        copy.start()
    tall_ring.start(3)
    v_ring.start(1)
    tall_ring.wait_last()

    def put_tall(rows, total):
        tall_sum[rows, :] = total.astype(BF)

    tall_ring.total(put_tall, lambda rows: tall[z, rows, :], 32)

    def x_rows(to):
        return pl.ds(pl.multiple_of(to * 128, 128), 128)

    tall_x_copies = [
        remote(
            tall_sum.at[x_rows(lax.rem(x + d + 1, NX))],
            tall_x.at[d], tall_x_sems, d, x_peers[d],
        )
        for d in range(NX - 1)
    ]
    for copy in tall_x_copies:
        copy.start()
    for copy in wide_z_copies:
        copy.wait_recv()
    total = wide_sum[z].astype(F32)
    for d in range(NZ - 1):
        total = total + wide_z[d].astype(F32)
    weight_grad[:, :256] = total.astype(BF)
    for ring, mine, out in ((k_ring, k_v, key_grad), (v_ring, v_v, value_grad)):
        ring.wait_last()

        def put(rows, total, out=out):
            out[rows, :] = total.astype(BF)

        ring.total(put, lambda rows, mine=mine: mine[x, rows, :], 32)
    for copy in tall_x_copies:
        copy.wait_recv()
    total = tall_sum[x_rows(x), :].astype(F32)
    for d in range(NX - 1):
        total = total + tall_x[d].astype(F32)
    weight_grad[:, 256:] = total.astype(BF)
    for ring in (k_ring, v_ring, tall_ring):
        ring.wait_sends()
    for copy in wide_z_copies + tall_x_copies:
        copy.wait_send()


def finish(keys, values, tall, *wides):
    def vm(*shape):
        return pltpu.VMEM(shape, BF)

    def sems(n):
        return pltpu.SemaphoreType.DMA((2, n))

    any_spec = pl.BlockSpec(memory_space=pl.ANY)
    vmem = pl.BlockSpec(memory_space=pltpu.VMEM)
    entry = (ENTRIES_HERE * KEYS, WIDTH)
    return pl.pallas_call(
        finish_kernel,
        out_shape=(
            jax.ShapeDtypeStruct((128, WIDTH), BF),
            jax.ShapeDtypeStruct(entry, BF),
            jax.ShapeDtypeStruct(entry, BF),
        ),
        in_specs=[any_spec, any_spec] + [vmem] * 5,
        out_specs=(vmem,) * 3,
        scratch_shapes=[
            vm(NX, *entry), vm(NX, *entry),
            vm(2, 2, 2, 256, WIDTH), vm(2, 2, 2, 256, WIDTH),
            vm(2, 2, 2, 256, WIDTH), vm(2, 2, 2, 256, WIDTH),
            vm(NZ, 128, 256), vm(NZ - 1, 128, 256),
            vm(2, 2, 4, 256, 256), vm(2, 2, 4, 256, 256), vm(512, 256), vm(NX - 1, 128, 256),
            pltpu.SemaphoreType.DMA((2,)), sems(8), sems(8), sems(7), sems(16), sems(3),
        ],
        compiler_params=pltpu.CompilerParams(
            collective_id=3, has_side_effects=True, vmem_limit_bytes=VMEM_BYTES
        ),
        cost_estimate=cost(150),
        name="finish",
    )(keys, values, tall, *wides)


def publish_kernel(*refs):
    for i in range(4):
        refs[4 + i][...] = refs[i][...]


def publish(*arrays):
    vmem = pl.BlockSpec(memory_space=pltpu.VMEM)
    return pl.pallas_call(
        publish_kernel,
        out_shape=tuple(jax.ShapeDtypeStruct(a.shape, a.dtype) for a in arrays),
        in_specs=[vmem] * 4,
        out_specs=(vmem,) * 4,
        name="publish",
    )(*arrays)


def body(queries, cache_keys, cache_values, owners, slots, out_weight, cotangent):
    codes = (owners * ENTRIES_HERE + slots).reshape(1, PAIRS)
    codes = jnp.pad(codes, ((0, 7), (0, 128 - PAIRS)))
    q, g, k, v, codes = gather_all(
        queries, cache_keys, cache_values, codes, cotangent, out_weight
    )
    q = q.reshape(NZ * SPANS_HERE, SPAN, WIDTH)
    k = k.reshape(NX * ENTRIES_HERE, KEYS, WIDTH)
    v = v.reshape(NX * ENTRIES_HERE, KEYS, WIDTH)
    near, stats = lax.optimization_barrier((step(g, g), local_stats(codes, q, k)))
    next_near, totals = lax.optimization_barrier((step(*near), all_totals(stats)))
    next_far, out = lax.optimization_barrier(
        (step(*next_near), local_outputs(codes, q, k, v, totals))
    )
    far, (mixed, tall, wide_0, *wides, deltas) = lax.optimization_barrier(
        (
            step(next_far[0][:HALF], next_far[1][HALF:]),
            attend(out.reshape(NZ, ROWS, WIDTH), g, cotangent, out_weight),
        )
    )
    grads = (g, *near, *next_near, *next_far, *far)
    sent = [
        lax.ppermute(
            wide,
            "seq",
            [(x * NZ + z, (x + apart) % NX * NZ + z) for x in range(NX) for z in range(NZ)],
        )
        for apart, wide in enumerate(wides, 1)
    ]
    key_terms, value_terms = local_grads(codes, q, k, v, grads, totals, deltas)
    entries = (NX, ENTRIES_HERE * KEYS, WIDTH)
    weight_grad, key_grad, value_grad = finish(
        key_terms.reshape(entries), value_terms.reshape(entries), tall, wide_0, *sent
    )
    mixed, weight_grad, key_grad, value_grad = publish(
        mixed, weight_grad, key_grad, value_grad
    )
    shape = (ENTRIES_HERE, KEYS, WIDTH)
    return mixed, weight_grad, key_grad.reshape(shape), value_grad.reshape(shape)


def solution(mesh):
    placed = (
        P("seq", "head"),
        P("seq", None, "head"),
        P("seq", None, "head"),
        P("seq", None),
        P("seq", None),
        P(None, "head"),
        P("seq", "head"),
    )
    return jax.shard_map(
        body,
        mesh=mesh,
        in_specs=placed,
        out_specs=(
            P("seq", "head"),
            P("seq", "head"),
            P("seq", None, "head"),
            P("seq", None, "head"),
        ),
        check_vma=False,
    )
```

```python
import functools
import math

import jax
import jax.numpy as jnp
from jax import lax
from jax.experimental import pallas as pl
from jax.experimental.pallas import tpu as pltpu
from jax.sharding import PartitionSpec as P

HEAD_DIM = 128
SPAN = 64
TOP = 2
NX, NZ, NY = 4, 8, 4
ROWS, WIDTH = 448, 512
SPANS_HERE = 7
PAIRS = SPANS_HERE * TOP
ENTRIES_HERE = 4
KEYS = 128
HALF = ROWS // 2
WIDE = 128
SCALE = 1.0 / math.sqrt(HEAD_DIM)
NEVER, HUGE = -1e30, 1e30
VMEM_BYTES = 56 * 1024 * 1024
MESH_ID = pl.DeviceIdType.MESH
BF, F32 = jnp.bfloat16, jnp.float32


def place():
    seq, head = lax.axis_index("seq"), lax.axis_index("head")
    return seq, head, seq // NZ, lax.rem(seq, NZ), head // 2, lax.rem(head, 2)


def remote(src, dst, sems, index, device):
    return pltpu.make_async_remote_copy(
        src_ref=src,
        dst_ref=dst,
        send_sem=sems.at[0, index],
        recv_sem=sems.at[1, index],
        device_id=device,
        device_id_type=MESH_ID,
    )


def meet(devices):
    sem = pltpu.get_barrier_semaphore()
    for device in devices:
        pl.semaphore_signal(sem, inc=1, device_id=device, device_id_type=MESH_ID)
    pl.semaphore_wait(sem, len(devices))


def selector(step):
    row = lax.broadcasted_iota(jnp.int32, (SPAN, 2 * SPAN), 0)
    column = lax.broadcasted_iota(jnp.int32, (SPAN, 2 * SPAN), 1)
    return (column == row + step).astype(F32).astype(BF)


def shift_rows(raw, step, write):
    pick = selector(step)

    def one(block, carry):
        window = raw[pl.ds(pl.multiple_of(block * SPAN, SPAN), 2 * SPAN), :]
        write(block, jnp.dot(pick, window, preferred_element_type=F32).astype(BF))
        return carry

    lax.fori_loop(0, SPANS_HERE, one, 0)


class Line:
    def __init__(self, axis):
        seq, head, x, z, y, c = place()
        if axis == "z":
            self.n, self.at, to = NZ, z, lambda i: (x * NZ + i, head)
        elif axis == "x":
            self.n, self.at, to = NX, x, lambda i: (i * NZ + z, head)
        else:
            self.n, self.at, to = NY, y, lambda i: (seq, 2 * i + c)
        self.half = self.n // 2
        self.beside = (to(self.off(1)), to(self.off(-1)))

    def off(self, steps):
        return lax.rem(self.at + steps + self.n, self.n)


class Ring:
    def __init__(self, axis, first, out, rows, sems, slot=lambda place: place):
        self.line, self.first, self.out, self.sems, self.slot = (
            Line(axis), first, out, sems, slot,
        )
        self.rows = rows // 2

    def copy(self, way, main, step):
        slot = self.slot(self.line.off(step if way else -step))
        half = way if main else 1 - way
        rows = pl.ds(half * self.rows, self.rows)
        dst = self.out.at[slot, rows]
        src = dst if step else self.first.at[rows]
        index = way * (self.line.n - 1) + (0 if main else self.line.half) + step
        return remote(src, dst, self.sems, index, self.line.beside[way])

    def start(self, step):
        for main in (True, False):
            if main or step < self.line.half - 1:
                for way in range(2):
                    if step:
                        self.copy(way, main, step - 1).wait_recv()
                    self.copy(way, main, step).start()

    def wait_others(self):
        for way in range(2):
            self.copy(way, False, self.line.half - 2).wait_recv()

    def wait_mains(self):
        for way in range(2):
            self.copy(way, True, self.line.half - 1).wait_recv()

    def wait_sends(self):
        for way in range(2):
            for step in range(self.line.half):
                self.copy(way, True, step).wait_send()
            for step in range(self.line.half - 1):
                self.copy(way, False, step).wait_send()

    def finish(self):
        self.wait_others()
        self.wait_mains()
        self.wait_sends()


class RingSum:
    def __init__(self, axis, blocks, rows, got, sums, sems):
        self.line = Line(axis)
        self.blocks, self.got, self.sums, self.sems = blocks, got, sums, sems
        self.rows = rows // 2

    def copy(self, way, main, step):
        half = way if main else 1 - way
        if step == (0 if main else 1):
            far = self.line.half - step
            block = self.line.off(-far if way else far)
            src = self.blocks.at[block, pl.ds(half * self.rows, self.rows)]
        else:
            src = self.sums.at[way, half, step]
        index = way * self.line.n + (0 if main else self.line.half) + step
        dst = self.got.at[way, half, step]
        return remote(src, dst, self.sems, index, self.line.beside[way])

    def send(self, way, main, step):
        half = way if main else 1 - way
        if step > (0 if main else 1):
            self.copy(way, main, step - 1).wait_recv()
            far = self.line.half - step
            block = self.line.off(-far if way else far)
            piece = 32

            def add(i, carry):
                rows = pl.ds(pl.multiple_of(i * piece, piece), piece)
                from_rows = pl.ds(pl.multiple_of(half * self.rows + i * piece, piece), piece)
                self.sums[way, half, step, rows, :] = (
                    self.blocks[block, from_rows, :].astype(F32)
                    + self.got[way, half, step - 1, rows, :].astype(F32)
                ).astype(BF)
                return carry

            lax.fori_loop(0, self.rows // piece, add, 0)
        self.copy(way, main, step).start()

    def start(self, step):
        for way in range(2):
            self.send(way, True, step)
        if step + 1 < self.line.half:
            for way in range(2):
                self.send(way, False, step + 1)

    def wait_last(self):
        for main in (False, True):
            for way in range(2):
                self.copy(way, main, self.line.half - 1).wait_recv()

    def wait_sends(self):
        for way in range(2):
            for step in range(self.line.half):
                self.copy(way, True, step).wait_send()
            for step in range(1, self.line.half):
                self.copy(way, False, step).wait_send()

    def total(self, write, mine, piece):
        for half in range(2):

            def one(i, carry):
                rows = pl.ds(pl.multiple_of(i * piece, piece), piece)
                at = pl.ds(pl.multiple_of(half * self.rows + i * piece, piece), piece)
                term = mine(at).astype(F32)
                for way in range(2):
                    term = term + self.got[way, half, self.line.half - 1, rows, :].astype(F32)
                write(at, term)
                return carry

            lax.fori_loop(0, self.rows // piece, one, 0)


def gather_kernel(
    q, k, v, codes, cot, w,
    q_all, g_own, k_all, v_all, codes_all,
    q_raw, q_sh, g_raw, g_sh, cot_v, w_v, part, pair_got, y_blocks, y_got, y_sums, g_acc,
    local, q_sems, k_sems, v_sems, code_sems, edge_sems, pair_sems, y_sems,
):
    seq, head, x, z, y, c = place()
    n_seq = NX * NZ
    before = (lax.rem(seq + n_seq - 1, n_seq), head)
    after = (lax.rem(seq + 1, n_seq), head)
    z_peers = [(x * NZ + lax.rem(z + d, NZ), head) for d in range(1, NZ)]
    sibling = (seq, 2 * y + 1 - c)
    own_q = pltpu.make_async_copy(q, q_raw.at[pl.ds(0, ROWS)], local.at[0])
    own_cot = pltpu.make_async_copy(cot, cot_v, local.at[1])
    own_w = pltpu.make_async_copy(w, w_v, local.at[2])
    own_q.start()
    own_cot.start()
    own_w.start()
    meet(
        z_peers + list(Line("x").beside) + list(Line("y").beside) + [sibling, before, after]
    )
    q_edge = remote(q.at[pl.ds(0, SPAN)], q_raw.at[pl.ds(ROWS, SPAN)], edge_sems, 0, before)
    q_edge.start()
    k_ring = Ring("x", k, k_all, ENTRIES_HERE, k_sems)
    v_ring = Ring("x", v, v_all, ENTRIES_HERE, v_sems)
    k_ring.start(0)
    v_ring.start(0)
    code_copies = [
        remote(codes, codes_all.at[z], code_sems, d, z_peers[d]) for d in range(NZ - 1)
    ]
    for copy in code_copies:
        copy.start()
    own_k = pltpu.make_async_copy(k, k_all.at[x], local.at[3])
    own_v = pltpu.make_async_copy(v, v_all.at[x], local.at[4])
    own_codes = pltpu.make_async_copy(codes, codes_all.at[z], local.at[5])
    own_k.start()
    own_v.start()
    own_codes.start()
    own_q.wait()
    q_edge.wait()
    last = seq == n_seq - 1
    tail = q_raw[pl.ds(ROWS, SPAN), :]
    q_raw[pl.ds(ROWS, SPAN), :] = jnp.where(last, jnp.zeros_like(tail), tail)

    def put_q(block, value):
        q_sh[pl.ds(pl.multiple_of(block * SPAN, SPAN), SPAN), :] = value

    shift_rows(q_raw, SPAN - 1, put_q)
    q_ring = Ring("z", q_sh, q_all, ROWS, q_sems)
    q_ring.start(0)
    keep_q = pltpu.make_async_copy(q_sh, q_all.at[z], local.at[6])
    keep_q.start()

    own_cot.wait()
    own_w.wait()

    def product(to_head):
        rows = pl.ds(pl.multiple_of(to_head * WIDTH, WIDTH), WIDTH)
        return lax.dot_general(
            cot_v[...], w_v[rows, :], (((1,), (1,)), ((), ())), preferred_element_type=F32
        )

    def pair_copy(j):
        return remote(part.at[j], pair_got.at[j], pair_sems, j, sibling)

    def for_sibling(i, carry):
        j = NY - 1 - i
        part[j] = product(2 * lax.rem(y + j, NY) + 1 - c).astype(BF)
        pair_copy(j).start()
        return carry

    lax.fori_loop(0, NY, for_sibling, 0)

    def for_row(i, carry):
        j = NY - 1 - i
        to = lax.rem(y + j, NY)
        value = product(2 * to + c)
        pair_copy(j).wait_recv()
        y_blocks[to] = (value + pair_got[j].astype(F32)).astype(BF)
        return carry

    lax.fori_loop(0, NY - 1, for_row, 0)
    y_ring = RingSum("y", y_blocks, ROWS, y_got, y_sums, y_sems)
    y_ring.start(0)
    mine = product(2 * y + c)
    pair_copy(0).wait_recv()
    g_acc[...] = mine + pair_got[0].astype(F32)
    q_ring.start(1)
    y_ring.start(1)
    k_ring.start(1)
    q_ring.start(2)
    v_ring.start(1)
    y_ring.wait_last()

    def put_g(rows, total):
        g_raw[rows, :] = total.astype(BF)

    y_ring.total(put_g, lambda rows: g_acc[rows, :], 32)
    g_edge = remote(
        g_raw.at[pl.ds(0, SPAN)], g_raw.at[pl.ds(ROWS, SPAN)], edge_sems, 1, before
    )
    g_edge.start()
    q_ring.start(3)
    g_edge.wait()
    tail = g_raw[pl.ds(ROWS, SPAN), :]
    g_raw[pl.ds(ROWS, SPAN), :] = jnp.where(last, jnp.zeros_like(tail), tail)

    def put_gs(block, value):
        g_sh[pl.ds(pl.multiple_of(block * SPAN, SPAN), SPAN), :] = value

    shift_rows(g_raw, SPAN - 1, put_gs)
    keep_g = pltpu.make_async_copy(g_sh, g_own, local.at[7])
    keep_g.start()
    q_ring.finish()
    k_ring.finish()
    v_ring.finish()
    for copy in code_copies:
        copy.wait()
    for j in range(NY):
        pair_copy(j).wait_send()
    y_ring.wait_sends()
    own_k.wait()
    own_v.wait()
    own_codes.wait()
    keep_q.wait()
    keep_g.wait()


def gather_all(q, k, v, codes, cot, w):
    def vm(*shape):
        return pltpu.VMEM(shape, BF)

    def sems(n):
        return pltpu.SemaphoreType.DMA((2, n))

    any_spec = pl.BlockSpec(memory_space=pl.ANY)
    entries = (NX, ENTRIES_HERE, KEYS, WIDTH)
    return pl.pallas_call(
        gather_kernel,
        out_shape=(
            jax.ShapeDtypeStruct((NZ, ROWS, WIDTH), BF),
            jax.ShapeDtypeStruct((ROWS, WIDTH), BF),
            jax.ShapeDtypeStruct(entries, BF),
            jax.ShapeDtypeStruct(entries, BF),
            jax.ShapeDtypeStruct((NZ, 8, 128), jnp.int32),
        ),
        in_specs=[any_spec] * 6,
        out_specs=(any_spec,) * 5,
        scratch_shapes=[
            vm(ROWS + SPAN, WIDTH), vm(ROWS, WIDTH), vm(ROWS + SPAN, WIDTH), vm(ROWS, WIDTH),
            vm(ROWS, WIDTH), vm(8 * WIDTH, WIDTH), vm(NY, ROWS, WIDTH), vm(NY, ROWS, WIDTH),
            vm(NY, ROWS, WIDTH), vm(2, 2, 2, HALF, WIDTH), vm(2, 2, 2, HALF, WIDTH),
            pltpu.VMEM((ROWS, WIDTH), F32),
            pltpu.SemaphoreType.DMA((8,)), sems(14), sems(6), sems(6), sems(7),
            sems(2), sems(4), sems(8),
        ],
        compiler_params=pltpu.CompilerParams(
            collective_id=0, has_side_effects=True, vmem_limit_bytes=VMEM_BYTES
        ),
        name="gather_all",
    )(q, k, v, codes, cot, w)


def two_heads(block):
    lane = lax.broadcasted_iota(jnp.int32, block.shape, 1)
    zero = jnp.zeros_like(block)
    upper = jnp.where(lane < HEAD_DIM, block, zero)
    lower = jnp.where(lane < HEAD_DIM, zero, block)
    return jnp.concatenate([upper, lower], axis=0)


def dot_t(a, b):
    return lax.dot_general(a, b, (((1,), (1,)), ((), ())), preferred_element_type=F32)


def each_live(codes, listed, compute, commit):
    z = lax.rem(lax.axis_index("seq"), NZ)

    def source(src, count):
        def pair(j, inner):
            code = codes[src, 0, j]
            entry = ((code >> 5) << 2) + (code & 3)
            listed[inner] = (src << 16) + ((j >> 1) << 8) + entry
            return inner + (((code >> 2) & (NZ - 1)) == z).astype(jnp.int32)

        return lax.fori_loop(0, PAIRS, pair, count)

    count = lax.fori_loop(0, NZ, source, 0)
    listed[count] = listed[jnp.maximum(count - 1, 0)]

    def two(i, carry):
        places, values = [], []
        for half in range(2):
            packed = listed[2 * i + half]
            places.append((packed >> 16, (packed >> 8) & 255, packed & 255))
            off = jnp.where(2 * i + half < count, 0.0, HUGE).astype(F32)
            values.append(compute(*places[half], off))
        for half in range(2):
            commit(*places[half], values[half])
        return carry

    lax.fori_loop(0, (count + 1) // 2, two, 0)


LISTED = pltpu.SMEM((128,), jnp.int32)


def cost(megabytes):
    return pl.CostEstimate(flops=0, transcendentals=0, bytes_accessed=megabytes * 1000000)


def stats_kernel(codes, q, k, stats, listed):
    stats[...] = jnp.full((NZ, 8, 256), NEVER, F32)

    def compute(src, span, entry, off):
        row = src * SPANS_HERE + span
        found = []
        for pair in range(2):
            columns = pl.ds(pair * 256, 256)
            scores = dot_t(k[entry, :, columns], two_heads(q[row, :, columns])) * SCALE
            top = jnp.max(scores, axis=0, keepdims=True)
            lse = top + jnp.log(jnp.sum(jnp.exp(scores - top), axis=0, keepdims=True))
            found.append(jnp.where(off > 0.0, NEVER, lse))
        return found

    def commit(src, span, entry, found):
        here = lax.broadcasted_iota(jnp.int32, (8, 128), 0) == span
        for pair, lse in enumerate(found):
            at = pl.ds(pair * 128, 128)
            old = stats[src, :, at]
            high = jnp.maximum(old, lse)
            both = high + jnp.log(jnp.exp(old - high) + jnp.exp(lse - high))
            stats[src, :, at] = jnp.where(here, both, old)

    each_live(codes, listed, compute, commit)


def local_stats(codes, q, k):
    vmem = pl.BlockSpec(memory_space=pltpu.VMEM)
    return pl.pallas_call(
        stats_kernel,
        out_shape=jax.ShapeDtypeStruct((NZ, 8, 256), F32),
        in_specs=[pl.BlockSpec(memory_space=pltpu.SMEM), vmem, vmem],
        out_specs=vmem,
        scratch_shapes=[LISTED],
        compiler_params=pltpu.CompilerParams(vmem_limit_bytes=VMEM_BYTES),
        cost_estimate=cost(30),
        name="local_stats",
    )(codes, q, k)


def totals_kernel(stats, out, got, summed, there, sems, back_sems):
    seq, head, x, z, _, _ = place()
    peers = [(x * NZ + lax.rem(z + d, NZ), head) for d in range(1, NZ)]
    meet(peers)
    copies = [
        remote(stats.at[lax.rem(z + d + 1, NZ)], got.at[d], sems, d, peers[d])
        for d in range(NZ - 1)
    ]
    for copy in copies:
        copy.start()
    for copy in copies:
        copy.wait_recv()
    terms = [stats[z]] + [got[d] for d in range(NZ - 1)]
    high = terms[0]
    for term in terms[1:]:
        high = jnp.maximum(high, term)
    both = jnp.zeros_like(high)
    for term in terms:
        both = both + jnp.exp(term - high)
    summed[...] = high + jnp.log(both)
    returns = [remote(summed, there.at[d], back_sems, d, peers[d]) for d in range(NZ - 1)]
    for copy in returns:
        copy.start()
    out[z] = summed[...]
    for d in range(NZ - 1):
        returns[d].wait_recv()
        out[lax.rem(z + NZ - d - 1, NZ)] = there[d]
    for copy in copies + returns:
        copy.wait_send()


def all_totals(stats):
    shape = (NZ, 8, 256)
    vmem = pl.BlockSpec(memory_space=pltpu.VMEM)
    return pl.pallas_call(
        totals_kernel,
        out_shape=jax.ShapeDtypeStruct(shape, F32),
        in_specs=[vmem],
        out_specs=vmem,
        scratch_shapes=[
            pltpu.VMEM((NZ - 1, 8, 256), F32),
            pltpu.VMEM((8, 256), F32),
            pltpu.VMEM((NZ - 1, 8, 256), F32),
            pltpu.SemaphoreType.DMA((2, NZ - 1)),
            pltpu.SemaphoreType.DMA((2, NZ - 1)),
        ],
        compiler_params=pltpu.CompilerParams(collective_id=1, has_side_effects=True),
        cost_estimate=cost(30),
        name="all_totals",
    )(stats)


def row_of(table, src, span, pair):
    here = lax.broadcasted_iota(jnp.int32, (8, 128), 0) == span
    block = table[src, :, pl.ds(pair * 128, 128)]
    return jnp.sum(jnp.where(here, block, 0.0), axis=0, keepdims=True)


def outputs_kernel(codes, q, k, v, totals, o, listed):
    def clear(i, carry):
        o[i] = jnp.zeros((SPAN, WIDTH), BF)
        return carry

    lax.fori_loop(0, NZ * SPANS_HERE, clear, 0)

    def compute(src, span, entry, off):
        row = src * SPANS_HERE + span
        terms = []
        for pair in range(2):
            columns = pl.ds(pair * 256, 256)
            scores = dot_t(k[entry, :, columns], two_heads(q[row, :, columns])) * SCALE
            probs = jnp.exp(scores - (row_of(totals, src, span, pair) + off)).astype(BF)
            terms.append(
                lax.dot_general(
                    probs, v[entry, :, columns], (((0,), (0,)), ((), ())),
                    preferred_element_type=F32,
                )
            )
        return terms

    def commit(src, span, entry, terms):
        row = src * SPANS_HERE + span
        for pair in range(2):
            for head in range(2):
                at = pl.ds(pair * 256 + head * 128, 128)
                term = terms[pair][head * SPAN : (head + 1) * SPAN, head * 128 : (head + 1) * 128]
                o[row, :, at] = (o[row, :, at].astype(F32) + term).astype(BF)

    each_live(codes, listed, compute, commit)


def local_outputs(codes, q, k, v, totals):
    vmem = pl.BlockSpec(memory_space=pltpu.VMEM)
    return pl.pallas_call(
        outputs_kernel,
        out_shape=jax.ShapeDtypeStruct((NZ * SPANS_HERE, SPAN, WIDTH), BF),
        in_specs=[pl.BlockSpec(memory_space=pltpu.SMEM)] + [vmem] * 4,
        out_specs=vmem,
        scratch_shapes=[LISTED],
        compiler_params=pltpu.CompilerParams(vmem_limit_bytes=VMEM_BYTES),
        cost_estimate=cost(40),
        name="local_outputs",
    )(codes, q, k, v, totals)


def step(ahead, back):
    right = [(x * NZ + z, x * NZ + (z + 1) % NZ) for x in range(NX) for z in range(NZ)]
    left = [(b, a) for a, b in right]
    return lax.ppermute(ahead, "seq", right), lax.ppermute(back, "seq", left)


def y_step(block, apart):
    pairs = [
        (2 * y + c, 2 * ((y + apart) % NY) + c) for y in range(NY) for c in range(2)
    ]
    return lax.ppermute(block, "head", pairs)


def grads_kernel(
    codes, q_in, k_in, v_in, g0, l1, r1, l2, r2, l3, r3, l4, r4, totals, deltas,
    key_out, value_out,
    q, k, v, g, key_acc, value_acc, key_low, value_low, loads, stores, listed,
):
    z = lax.rem(lax.axis_index("seq"), NZ)

    def slot(steps):
        return g.at[lax.rem(z + steps + NZ, NZ)]

    moves = [
        (q_in, q), (k_in, k), (v_in, v), (g0, slot(0)),
        (l1, slot(-1)), (r1, slot(1)), (l2, slot(-2)), (r2, slot(2)), (l3, slot(-3)),
        (r3, slot(3)), (l4, slot(4).at[pl.ds(0, HALF)]), (r4, slot(4).at[pl.ds(HALF, HALF)]),
    ]
    copies = [pltpu.make_async_copy(*move, loads.at[i]) for i, move in enumerate(moves)]
    for copy in copies:
        copy.start()

    def clear_acc(i, carry):
        key_acc[i] = jnp.zeros((KEYS, WIDTH), F32)
        value_acc[i] = jnp.zeros((KEYS, WIDTH), F32)
        return carry

    lax.fori_loop(0, NX * ENTRIES_HERE, clear_acc, 0)
    for copy in copies:
        copy.wait()

    def compute(src, span, entry, off):
        row = src * SPANS_HERE + span
        rows = pl.ds(pl.multiple_of(span * SPAN, SPAN), SPAN)
        terms = []
        for pair in range(2):
            columns = pl.ds(pair * 256, 256)
            q2 = two_heads(q[row, :, columns])
            g2 = two_heads(g[src, rows, columns])
            scores = dot_t(k[entry, :, columns], q2) * SCALE
            prob_grad = dot_t(v[entry, :, columns], g2)
            probs = jnp.exp(scores - (row_of(totals, src, span, pair) + off))
            delta = row_of(deltas, src, span, pair)
            score_grad = (probs * (prob_grad - delta)).astype(BF)
            terms.append(
                (
                    jnp.dot(score_grad, q2, preferred_element_type=F32),
                    jnp.dot(probs.astype(BF), g2, preferred_element_type=F32),
                )
            )
        return terms

    def commit(src, span, entry, terms):
        for pair, (key_term, value_term) in enumerate(terms):
            columns = pl.ds(pair * 256, 256)
            key_acc[entry, :, columns] += key_term
            value_acc[entry, :, columns] += value_term

    each_live(codes, listed, compute, commit)

    def store(i, which):
        low, to = ((key_low, key_out), (value_low, value_out))[which]
        return pltpu.make_async_copy(low.at[i], to.at[i], stores.at[which, i])

    def close(i, carry):
        key_low[i] = (key_acc[i] * SCALE).astype(BF)
        store(i, 0).start()
        value_low[i] = value_acc[i].astype(BF)
        store(i, 1).start()
        return carry

    def wait(i, carry):
        store(i, 0).wait()
        store(i, 1).wait()
        return carry

    lax.fori_loop(0, NX * ENTRIES_HERE, close, 0)
    lax.fori_loop(0, NX * ENTRIES_HERE, wait, 0)


def local_grads(codes, q, k, v, grads, totals, deltas):
    entries = (NX * ENTRIES_HERE, KEYS, WIDTH)
    any_spec = pl.BlockSpec(memory_space=pl.ANY)
    vmem = pl.BlockSpec(memory_space=pltpu.VMEM)
    return pl.pallas_call(
        grads_kernel,
        out_shape=(jax.ShapeDtypeStruct(entries, BF),) * 2,
        in_specs=[pl.BlockSpec(memory_space=pltpu.SMEM)] + [any_spec] * 12 + [vmem] * 2,
        out_specs=(any_spec,) * 2,
        scratch_shapes=[
            pltpu.VMEM((NZ * SPANS_HERE, SPAN, WIDTH), BF),
            pltpu.VMEM(entries, BF), pltpu.VMEM(entries, BF),
            pltpu.VMEM((NZ, ROWS, WIDTH), BF),
            pltpu.VMEM(entries, F32), pltpu.VMEM(entries, F32),
            pltpu.VMEM(entries, BF), pltpu.VMEM(entries, BF),
            pltpu.SemaphoreType.DMA((12,)), pltpu.SemaphoreType.DMA((2, NX * ENTRIES_HERE)),
            LISTED,
        ],
        compiler_params=pltpu.CompilerParams(vmem_limit_bytes=VMEM_BYTES),
        cost_estimate=cost(100),
        name="local_grads",
    )(codes, q, k, v, *grads, totals, deltas)


def collect_kernel(
    o, g,
    att, deltas,
    o_got, o_sums, att_raw, delta_mine,
    o_sems, edge_sems, delta_sems,
):
    seq, head, x, z, y, c = place()
    n_seq = NX * NZ
    before = (lax.rem(seq + n_seq - 1, n_seq), head)
    after = (lax.rem(seq + 1, n_seq), head)
    z_peers = [(x * NZ + lax.rem(z + d, NZ), head) for d in range(1, NZ)]
    meet(z_peers + [before, after])
    o_ring = RingSum("z", o, ROWS, o_got, o_sums, o_sems)
    for step in range(4):
        o_ring.start(step)
    o_ring.wait_last()

    def put_out(rows, total):
        att_raw[pl.ds(pl.multiple_of(rows.start + SPAN, 32), 32), :] = total.astype(BF)

    o_ring.total(put_out, lambda rows: o[z, rows, :], 32)
    edge = remote(
        att_raw.at[pl.ds(ROWS, SPAN)], att_raw.at[pl.ds(0, SPAN)], edge_sems, 0, after
    )
    edge.start()
    delta_mine[...] = jnp.zeros((8, 256), F32)
    for span in range(SPANS_HERE):
        rows = pl.ds(span * SPAN, SPAN)
        terms = g[rows, :].astype(F32) * att_raw[pl.ds((span + 1) * SPAN, SPAN), :].astype(F32)
        for pair in range(2):
            start = pair * 256
            both = jnp.concatenate(
                [terms[:, start : start + 128], terms[:, start + 128 : start + 256]], axis=0
            )
            row = lax.dot_general(
                jnp.ones((8, 128), F32), both, (((1,), (1,)), ((), ())),
                precision=lax.Precision.HIGHEST, preferred_element_type=F32,
            )
            delta_mine[pl.ds(span, 1), pl.ds(pair * 128, 128)] = row[:1]
    deltas[z] = delta_mine[...]
    delta_copies = [
        remote(delta_mine, deltas.at[z], delta_sems, d, z_peers[d]) for d in range(NZ - 1)
    ]
    for copy in delta_copies:
        copy.start()
    edge.wait()
    lead = att_raw[pl.ds(0, SPAN), :]
    att_raw[pl.ds(0, SPAN), :] = jnp.where(seq == 0, jnp.zeros_like(lead), lead)

    def put_att(block, value):
        att[pl.ds(pl.multiple_of(block * SPAN, SPAN), SPAN), :] = value

    shift_rows(att_raw, 1, put_att)
    o_ring.wait_sends()
    for copy in delta_copies:
        copy.wait()


def collect(o, g):
    def vm(*shape):
        return pltpu.VMEM(shape, BF)

    def sems(n):
        return pltpu.SemaphoreType.DMA((2, n))

    vmem = pl.BlockSpec(memory_space=pltpu.VMEM)
    return pl.pallas_call(
        collect_kernel,
        out_shape=(
            jax.ShapeDtypeStruct((ROWS, WIDTH), BF),
            jax.ShapeDtypeStruct((NZ, 8, 256), F32),
        ),
        in_specs=[vmem, vmem],
        out_specs=(vmem, vmem),
        scratch_shapes=[
            vm(2, 2, 4, HALF, WIDTH), vm(2, 2, 4, HALF, WIDTH),
            vm(ROWS + SPAN, WIDTH), pltpu.VMEM((8, 256), F32),
            sems(16), sems(1), sems(7),
        ],
        compiler_params=pltpu.CompilerParams(
            collective_id=2, has_side_effects=True, vmem_limit_bytes=VMEM_BYTES
        ),
        cost_estimate=cost(140),
        name="collect",
    )(o, g)


def finish_kernel(
    att_0, att_1, att_2, att_3, cot, w, keys, values,
    mixed, weight_grad, key_grad, value_grad,
    w_v, k_v, v_v, k_got, k_sums, v_got, v_sums, pair_got, acc,
    wide, tall, wide_got, wide_sum, wide_z, tall_got, tall_sums, tall_sum, tall_x,
    local, k_sems, v_sems, pair_sems, wide_sems, wide_z_sems, tall_sems, tall_x_sems,
):
    seq, head, x, z, y, c = place()
    blocks = (att_0, att_1, att_2, att_3)
    z_peers = [(x * NZ + lax.rem(z + d, NZ), head) for d in range(1, NZ)]
    x_peers = [(lax.rem(x + d, NX) * NZ + z, head) for d in range(1, NX)]
    sibling = (seq, 2 * y + 1 - c)
    own_w = pltpu.make_async_copy(w, w_v, local.at[0])
    own_k = pltpu.make_async_copy(keys, k_v, local.at[1])
    own_v = pltpu.make_async_copy(values, v_v, local.at[2])
    own_k.start()
    own_v.start()
    own_w.start()
    meet(z_peers + x_peers + [sibling])
    pair_copies = [
        remote(block, pair_got.at[j], pair_sems, j, sibling) for j, block in enumerate(blocks)
    ]
    for copy in pair_copies:
        copy.start()
    own_k.wait()
    own_v.wait()
    k_ring = RingSum("x", k_v, 512, k_got, k_sums, k_sems)
    v_ring = RingSum("x", v_v, 512, v_got, v_sums, v_sems)
    k_ring.start(0)
    v_ring.start(0)
    own_w.wait()

    def use(att, to_x, part, first=False):
        rows = pl.ds(pl.multiple_of((2 * to_x + part) * WIDTH, WIDTH), WIDTH)
        term = jnp.dot(att, w_v[rows, :], preferred_element_type=F32)
        acc[...] = term if first else acc[...] + term
        terms = lax.dot_general(
            att, cot[...], (((0,), (0,)), ((), ())), preferred_element_type=F32
        ).astype(BF)
        wide[to_x, pl.ds(pl.multiple_of(part * WIDTH, WIDTH), WIDTH), :] = terms[:, :WIDE]
        for i in range(4):
            tall[part * 4 + i, pl.ds(pl.multiple_of(to_x * 128, 128), 128), :] = terms[
                i * 128 : (i + 1) * 128, WIDE:
            ]

    def wide_copy(apart):
        to = lax.rem(x + apart, NX)
        return remote(
            wide.at[to], wide_got.at[apart - 1], wide_sems, apart - 1, (to * NZ + z, head)
        )

    for j in range(NY):
        came = lax.rem(y + NY - j, NY)
        use(blocks[j][...], came, c, j == 0)
        pair_copies[j].wait_recv()
        use(pair_got[j], came, 1 - c)
        apart = lax.rem(came - x + NX, NX)

        @pl.when(apart != 0)
        def _():
            wide_copy(apart).start()

    tall_ring = RingSum("z", tall, 512, tall_got, tall_sums, tall_sems)
    tall_ring.start(0)
    k_ring.start(1)
    mixed[...] = acc[...].astype(BF)
    tall_ring.start(1)
    v_ring.start(1)
    tall_ring.start(2)
    for apart in range(1, NX):
        wide_copy(apart).wait_recv()

    def add_wide(i, carry):
        rows = pl.ds(pl.multiple_of(i * 128, 128), 128)
        total = wide[x, rows, :].astype(F32)
        for d in range(NX - 1):
            total = total + wide_got[d, rows, :].astype(F32)
        wide_sum[i] = total.astype(BF)
        return carry

    lax.fori_loop(0, NZ, add_wide, 0)
    wide_z_copies = [
        remote(wide_sum.at[lax.rem(z + d + 1, NZ)], wide_z.at[d], wide_z_sems, d, z_peers[d])
        for d in range(NZ - 1)
    ]
    for copy in wide_z_copies:
        copy.start()
    tall_ring.start(3)
    for ring, mine, out in ((k_ring, k_v, key_grad), (v_ring, v_v, value_grad)):
        ring.wait_last()

        def put(rows, total, out=out):
            out[rows, :] = total.astype(BF)

        ring.total(put, lambda rows, mine=mine: mine[x, rows, :], 32)
    tall_ring.wait_last()

    def put_tall(rows, total):
        tall_sum[rows, :] = total.astype(BF)

    tall_ring.total(put_tall, lambda rows: tall[z, rows, :], 32)

    def x_rows(to):
        return pl.ds(pl.multiple_of(to * 128, 128), 128)

    tall_x_copies = [
        remote(
            tall_sum.at[x_rows(lax.rem(x + d + 1, NX))],
            tall_x.at[d], tall_x_sems, d, x_peers[d],
        )
        for d in range(NX - 1)
    ]
    for copy in tall_x_copies:
        copy.start()
    for copy in wide_z_copies:
        copy.wait_recv()
    total = wide_sum[z].astype(F32)
    for d in range(NZ - 1):
        total = total + wide_z[d].astype(F32)
    weight_grad[:, :WIDE] = total.astype(BF)
    for copy in tall_x_copies:
        copy.wait_recv()
    total = tall_sum[x_rows(x), :].astype(F32)
    for d in range(NX - 1):
        total = total + tall_x[d].astype(F32)
    weight_grad[:, WIDE:] = total.astype(BF)
    for ring in (k_ring, v_ring, tall_ring):
        ring.wait_sends()
    for copy in pair_copies + wide_z_copies + tall_x_copies:
        copy.wait_send()
    for apart in range(1, NX):
        wide_copy(apart).wait_send()


def finish(blocks, cot, w, keys, values):
    def vm(*shape):
        return pltpu.VMEM(shape, BF)

    def sems(n):
        return pltpu.SemaphoreType.DMA((2, n))

    any_spec = pl.BlockSpec(memory_space=pl.ANY)
    vmem = pl.BlockSpec(memory_space=pltpu.VMEM)
    entry = (ENTRIES_HERE * KEYS, WIDTH)
    tall = WIDTH - WIDE
    return pl.pallas_call(
        finish_kernel,
        out_shape=(
            jax.ShapeDtypeStruct((ROWS, WIDTH), BF),
            jax.ShapeDtypeStruct((128, WIDTH), BF),
            jax.ShapeDtypeStruct(entry, BF),
            jax.ShapeDtypeStruct(entry, BF),
        ),
        in_specs=[vmem] * 5 + [any_spec] * 3,
        out_specs=(vmem,) * 4,
        scratch_shapes=[
            vm(8 * WIDTH, WIDTH), vm(NX, *entry), vm(NX, *entry),
            vm(2, 2, 2, 256, WIDTH), vm(2, 2, 2, 256, WIDTH),
            vm(2, 2, 2, 256, WIDTH), vm(2, 2, 2, 256, WIDTH),
            vm(NY, ROWS, WIDTH), pltpu.VMEM((ROWS, WIDTH), F32),
            vm(NX, 1024, WIDE), vm(NZ, 512, tall), vm(NX - 1, 1024, WIDE), vm(NZ, 128, WIDE),
            vm(NZ - 1, 128, WIDE), vm(2, 2, 4, 256, tall), vm(2, 2, 4, 256, tall),
            vm(512, tall), vm(NX - 1, 128, tall),
            pltpu.SemaphoreType.DMA((3,)), sems(8), sems(8), sems(4),
            sems(3), sems(7), sems(16), sems(3),
        ],
        compiler_params=pltpu.CompilerParams(
            collective_id=3, has_side_effects=True, vmem_limit_bytes=VMEM_BYTES
        ),
        cost_estimate=cost(180),
        name="finish",
    )(*blocks, cot, w, keys, values)


def publish_kernel(*refs):
    for i in range(4):
        refs[4 + i][...] = refs[i][...]


def publish(*arrays):
    vmem = pl.BlockSpec(memory_space=pltpu.VMEM)
    return pl.pallas_call(
        publish_kernel,
        out_shape=tuple(jax.ShapeDtypeStruct(a.shape, a.dtype) for a in arrays),
        in_specs=[vmem] * 4,
        out_specs=(vmem,) * 4,
        name="publish",
    )(*arrays)


def body(queries, cache_keys, cache_values, owners, slots, out_weight, cotangent):
    codes = (owners * ENTRIES_HERE + slots).reshape(1, PAIRS)
    codes = jnp.pad(codes, ((0, 7), (0, 128 - PAIRS)))
    q, g, k, v, codes = gather_all(
        queries, cache_keys, cache_values, codes, cotangent, out_weight
    )
    q = q.reshape(NZ * SPANS_HERE, SPAN, WIDTH)
    k = k.reshape(NX * ENTRIES_HERE, KEYS, WIDTH)
    v = v.reshape(NX * ENTRIES_HERE, KEYS, WIDTH)
    near, stats = lax.optimization_barrier((step(g, g), local_stats(codes, q, k)))
    next_near, totals = lax.optimization_barrier((step(*near), all_totals(stats)))
    next_far, out = lax.optimization_barrier(
        (step(*next_near), local_outputs(codes, q, k, v, totals))
    )
    far, (att, deltas) = lax.optimization_barrier(
        (
            step(next_far[0][:HALF], next_far[1][HALF:]),
            collect(out.reshape(NZ, ROWS, WIDTH), g),
        )
    )
    grads = (g, *near, *next_near, *next_far, *far)
    blocks, (key_terms, value_terms) = lax.optimization_barrier(
        (
            [att] + [y_step(att, apart) for apart in (1, 2, 3)],
            local_grads(codes, q, k, v, grads, totals, deltas),
        )
    )
    entries = (NX, ENTRIES_HERE * KEYS, WIDTH)
    mixed, weight_grad, key_grad, value_grad = finish(
        blocks, cotangent, out_weight, key_terms.reshape(entries), value_terms.reshape(entries)
    )
    mixed, weight_grad, key_grad, value_grad = publish(
        mixed, weight_grad, key_grad, value_grad
    )
    shape = (ENTRIES_HERE, KEYS, WIDTH)
    return mixed, weight_grad, key_grad.reshape(shape), value_grad.reshape(shape)


def solution(mesh):
    placed = (
        P("seq", "head"),
        P("seq", None, "head"),
        P("seq", None, "head"),
        P("seq", None),
        P("seq", None),
        P(None, "head"),
        P("seq", "head"),
    )
    return jax.shard_map(
        body,
        mesh=mesh,
        in_specs=placed,
        out_specs=(
            P("seq", "head"),
            P("seq", "head"),
            P("seq", None, "head"),
            P("seq", None, "head"),
        ),
        check_vma=False,
    )
```

```python
import functools
import math

import jax
import jax.numpy as jnp
from jax import lax
from jax.experimental import pallas as pl
from jax.experimental.pallas import tpu as pltpu
from jax.sharding import PartitionSpec as P

HEAD_DIM = 128
SPAN = 64
TOP = 2
NX, NZ, NY = 4, 8, 4
ROWS, WIDTH = 448, 512
SPANS_HERE = 7
PAIRS = SPANS_HERE * TOP
ENTRIES_HERE = 4
KEYS = 128
HALF = ROWS // 2
WIDE = 128
SCALE = 1.0 / math.sqrt(HEAD_DIM)
NEVER, HUGE = -1e30, 1e30
VMEM_BYTES = 56 * 1024 * 1024
MESH_ID = pl.DeviceIdType.MESH
BF, F32 = jnp.bfloat16, jnp.float32


def place():
    seq, head = lax.axis_index("seq"), lax.axis_index("head")
    return seq, head, seq // NZ, lax.rem(seq, NZ), head // 2, lax.rem(head, 2)


def remote(src, dst, sems, index, device):
    return pltpu.make_async_remote_copy(
        src_ref=src,
        dst_ref=dst,
        send_sem=sems.at[0, index],
        recv_sem=sems.at[1, index],
        device_id=device,
        device_id_type=MESH_ID,
    )


def meet(devices):
    sem = pltpu.get_barrier_semaphore()
    for device in devices:
        pl.semaphore_signal(sem, inc=1, device_id=device, device_id_type=MESH_ID)
    pl.semaphore_wait(sem, len(devices))


def selector(step):
    row = lax.broadcasted_iota(jnp.int32, (SPAN, 2 * SPAN), 0)
    column = lax.broadcasted_iota(jnp.int32, (SPAN, 2 * SPAN), 1)
    return (column == row + step).astype(F32).astype(BF)


def shift_rows(raw, step, write):
    pick = selector(step)

    def one(block, carry):
        window = raw[pl.ds(pl.multiple_of(block * SPAN, SPAN), 2 * SPAN), :]
        write(block, jnp.dot(pick, window, preferred_element_type=F32).astype(BF))
        return carry

    lax.fori_loop(0, SPANS_HERE, one, 0)


class Line:
    def __init__(self, axis):
        seq, head, x, z, y, c = place()
        if axis == "z":
            self.n, self.at, to = NZ, z, lambda i: (x * NZ + i, head)
        elif axis == "x":
            self.n, self.at, to = NX, x, lambda i: (i * NZ + z, head)
        else:
            self.n, self.at, to = NY, y, lambda i: (seq, 2 * i + c)
        self.half = self.n // 2
        self.beside = (to(self.off(1)), to(self.off(-1)))

    def off(self, steps):
        return lax.rem(self.at + steps + self.n, self.n)


class Ring:
    def __init__(self, axis, first, out, rows, sems, slot=lambda place: place):
        self.line, self.first, self.out, self.sems, self.slot = (
            Line(axis), first, out, sems, slot,
        )
        self.rows = rows // 2

    def copy(self, way, main, step):
        slot = self.slot(self.line.off(step if way else -step))
        half = way if main else 1 - way
        rows = pl.ds(half * self.rows, self.rows)
        dst = self.out.at[slot, rows]
        src = dst if step else self.first.at[rows]
        index = way * (self.line.n - 1) + (0 if main else self.line.half) + step
        return remote(src, dst, self.sems, index, self.line.beside[way])

    def start(self, step):
        for main in (True, False):
            if main or step < self.line.half - 1:
                for way in range(2):
                    if step:
                        self.copy(way, main, step - 1).wait_recv()
                    self.copy(way, main, step).start()

    def wait_others(self):
        for way in range(2):
            self.copy(way, False, self.line.half - 2).wait_recv()

    def wait_mains(self):
        for way in range(2):
            self.copy(way, True, self.line.half - 1).wait_recv()

    def wait_sends(self):
        for way in range(2):
            for step in range(self.line.half):
                self.copy(way, True, step).wait_send()
            for step in range(self.line.half - 1):
                self.copy(way, False, step).wait_send()

    def finish(self):
        self.wait_others()
        self.wait_mains()
        self.wait_sends()


class RingSum:
    def __init__(self, axis, blocks, rows, got, sums, sems):
        self.line = Line(axis)
        self.blocks, self.got, self.sums, self.sems = blocks, got, sums, sems
        self.rows = rows // 2

    def copy(self, way, main, step):
        half = way if main else 1 - way
        if step == (0 if main else 1):
            far = self.line.half - step
            block = self.line.off(-far if way else far)
            src = self.blocks.at[block, pl.ds(half * self.rows, self.rows)]
        else:
            src = self.sums.at[way, half, step]
        index = way * self.line.n + (0 if main else self.line.half) + step
        dst = self.got.at[way, half, step]
        return remote(src, dst, self.sems, index, self.line.beside[way])

    def send(self, way, main, step):
        half = way if main else 1 - way
        if step > (0 if main else 1):
            self.copy(way, main, step - 1).wait_recv()
            far = self.line.half - step
            block = self.line.off(-far if way else far)
            piece = 32

            def add(i, carry):
                rows = pl.ds(pl.multiple_of(i * piece, piece), piece)
                from_rows = pl.ds(pl.multiple_of(half * self.rows + i * piece, piece), piece)
                self.sums[way, half, step, rows, :] = (
                    self.blocks[block, from_rows, :].astype(F32)
                    + self.got[way, half, step - 1, rows, :].astype(F32)
                ).astype(BF)
                return carry

            lax.fori_loop(0, self.rows // piece, add, 0)
        self.copy(way, main, step).start()

    def start(self, step):
        for way in range(2):
            self.send(way, True, step)
        if step + 1 < self.line.half:
            for way in range(2):
                self.send(way, False, step + 1)

    def wait_last(self):
        for main in (False, True):
            for way in range(2):
                self.copy(way, main, self.line.half - 1).wait_recv()

    def wait_sends(self):
        for way in range(2):
            for step in range(self.line.half):
                self.copy(way, True, step).wait_send()
            for step in range(1, self.line.half):
                self.copy(way, False, step).wait_send()

    def total(self, write, mine, piece):
        for half in range(2):

            def one(i, carry):
                rows = pl.ds(pl.multiple_of(i * piece, piece), piece)
                at = pl.ds(pl.multiple_of(half * self.rows + i * piece, piece), piece)
                term = mine(at).astype(F32)
                for way in range(2):
                    term = term + self.got[way, half, self.line.half - 1, rows, :].astype(F32)
                write(at, term)
                return carry

            lax.fori_loop(0, self.rows // piece, one, 0)


def gather_kernel(
    q, k, v, codes, cot, w,
    q_all, g_own, k_all, v_all, codes_all,
    q_raw, q_sh, g_raw, g_sh, cot_v, w_v, part, pair_got, y_blocks, y_got, y_sums, g_acc,
    local, q_sems, k_sems, v_sems, code_sems, edge_sems, pair_sems, y_sems,
):
    seq, head, x, z, y, c = place()
    n_seq = NX * NZ
    before = (lax.rem(seq + n_seq - 1, n_seq), head)
    after = (lax.rem(seq + 1, n_seq), head)
    z_peers = [(x * NZ + lax.rem(z + d, NZ), head) for d in range(1, NZ)]
    sibling = (seq, 2 * y + 1 - c)
    own_q = pltpu.make_async_copy(q, q_raw.at[pl.ds(0, ROWS)], local.at[0])
    own_cot = pltpu.make_async_copy(cot, cot_v, local.at[1])
    own_w = pltpu.make_async_copy(w, w_v, local.at[2])
    own_q.start()
    own_cot.start()
    own_w.start()
    meet(
        z_peers + list(Line("x").beside) + list(Line("y").beside) + [sibling, before, after]
    )
    q_edge = remote(q.at[pl.ds(0, SPAN)], q_raw.at[pl.ds(ROWS, SPAN)], edge_sems, 0, before)
    q_edge.start()
    k_ring = Ring("x", k, k_all, ENTRIES_HERE, k_sems)
    v_ring = Ring("x", v, v_all, ENTRIES_HERE, v_sems)
    k_ring.start(0)
    v_ring.start(0)
    code_copies = [
        remote(codes, codes_all.at[z], code_sems, d, z_peers[d]) for d in range(NZ - 1)
    ]
    for copy in code_copies:
        copy.start()
    own_k = pltpu.make_async_copy(k, k_all.at[x], local.at[3])
    own_v = pltpu.make_async_copy(v, v_all.at[x], local.at[4])
    own_codes = pltpu.make_async_copy(codes, codes_all.at[z], local.at[5])
    own_k.start()
    own_v.start()
    own_codes.start()
    own_q.wait()
    q_edge.wait()
    last = seq == n_seq - 1
    tail = q_raw[pl.ds(ROWS, SPAN), :]
    q_raw[pl.ds(ROWS, SPAN), :] = jnp.where(last, jnp.zeros_like(tail), tail)

    def put_q(block, value):
        q_sh[pl.ds(pl.multiple_of(block * SPAN, SPAN), SPAN), :] = value

    shift_rows(q_raw, SPAN - 1, put_q)
    q_ring = Ring("z", q_sh, q_all, ROWS, q_sems)
    q_ring.start(0)
    keep_q = pltpu.make_async_copy(q_sh, q_all.at[z], local.at[6])
    keep_q.start()

    own_cot.wait()
    own_w.wait()

    def product(to_head):
        rows = pl.ds(pl.multiple_of(to_head * WIDTH, WIDTH), WIDTH)
        return lax.dot_general(
            cot_v[...], w_v[rows, :], (((1,), (1,)), ((), ())), preferred_element_type=F32
        )

    def pair_copy(j):
        return remote(part.at[j], pair_got.at[j], pair_sems, j, sibling)

    def for_sibling(i, carry):
        j = NY - 1 - i
        part[j] = product(2 * lax.rem(y + j, NY) + 1 - c).astype(BF)
        pair_copy(j).start()
        return carry

    lax.fori_loop(0, NY, for_sibling, 0)

    def for_row(i, carry):
        j = NY - 1 - i
        to = lax.rem(y + j, NY)
        value = product(2 * to + c)
        pair_copy(j).wait_recv()
        y_blocks[to] = (value + pair_got[j].astype(F32)).astype(BF)
        return carry

    lax.fori_loop(0, NY - 1, for_row, 0)
    y_ring = RingSum("y", y_blocks, ROWS, y_got, y_sums, y_sems)
    y_ring.start(0)
    mine = product(2 * y + c)
    pair_copy(0).wait_recv()
    g_acc[...] = mine + pair_got[0].astype(F32)
    q_ring.start(1)
    y_ring.start(1)
    k_ring.start(1)
    q_ring.start(2)
    v_ring.start(1)
    y_ring.wait_last()

    def put_g(rows, total):
        g_raw[rows, :] = total.astype(BF)

    y_ring.total(put_g, lambda rows: g_acc[rows, :], 32)
    g_edge = remote(
        g_raw.at[pl.ds(0, SPAN)], g_raw.at[pl.ds(ROWS, SPAN)], edge_sems, 1, before
    )
    g_edge.start()
    q_ring.start(3)
    g_edge.wait()
    tail = g_raw[pl.ds(ROWS, SPAN), :]
    g_raw[pl.ds(ROWS, SPAN), :] = jnp.where(last, jnp.zeros_like(tail), tail)

    def put_gs(block, value):
        g_sh[pl.ds(pl.multiple_of(block * SPAN, SPAN), SPAN), :] = value

    shift_rows(g_raw, SPAN - 1, put_gs)
    keep_g = pltpu.make_async_copy(g_sh, g_own, local.at[7])
    keep_g.start()
    q_ring.finish()
    k_ring.finish()
    v_ring.finish()
    for copy in code_copies:
        copy.wait()
    for j in range(NY):
        pair_copy(j).wait_send()
    y_ring.wait_sends()
    own_k.wait()
    own_v.wait()
    own_codes.wait()
    keep_q.wait()
    keep_g.wait()


def gather_all(q, k, v, codes, cot, w):
    def vm(*shape):
        return pltpu.VMEM(shape, BF)

    def sems(n):
        return pltpu.SemaphoreType.DMA((2, n))

    any_spec = pl.BlockSpec(memory_space=pl.ANY)
    entries = (NX, ENTRIES_HERE, KEYS, WIDTH)
    return pl.pallas_call(
        gather_kernel,
        out_shape=(
            jax.ShapeDtypeStruct((NZ, ROWS, WIDTH), BF),
            jax.ShapeDtypeStruct((ROWS, WIDTH), BF),
            jax.ShapeDtypeStruct(entries, BF),
            jax.ShapeDtypeStruct(entries, BF),
            jax.ShapeDtypeStruct((NZ, 8, 128), jnp.int32),
        ),
        in_specs=[any_spec] * 6,
        out_specs=(any_spec,) * 5,
        scratch_shapes=[
            vm(ROWS + SPAN, WIDTH), vm(ROWS, WIDTH), vm(ROWS + SPAN, WIDTH), vm(ROWS, WIDTH),
            vm(ROWS, WIDTH), vm(8 * WIDTH, WIDTH), vm(NY, ROWS, WIDTH), vm(NY, ROWS, WIDTH),
            vm(NY, ROWS, WIDTH), vm(2, 2, 2, HALF, WIDTH), vm(2, 2, 2, HALF, WIDTH),
            pltpu.VMEM((ROWS, WIDTH), F32),
            pltpu.SemaphoreType.DMA((8,)), sems(14), sems(6), sems(6), sems(7),
            sems(2), sems(4), sems(8),
        ],
        compiler_params=pltpu.CompilerParams(
            collective_id=0, has_side_effects=True, vmem_limit_bytes=VMEM_BYTES
        ),
        name="gather_all",
    )(q, k, v, codes, cot, w)


def two_heads(block):
    lane = lax.broadcasted_iota(jnp.int32, block.shape, 1)
    zero = jnp.zeros_like(block)
    upper = jnp.where(lane < HEAD_DIM, block, zero)
    lower = jnp.where(lane < HEAD_DIM, zero, block)
    return jnp.concatenate([upper, lower], axis=0)


def dot_t(a, b):
    return lax.dot_general(a, b, (((1,), (1,)), ((), ())), preferred_element_type=F32)


def list_live(codes, listed):
    z = lax.rem(lax.axis_index("seq"), NZ)

    def source(src, count):
        def pair(j, inner):
            code = codes[src, 0, j]
            entry = ((code >> 5) << 2) + (code & 3)
            listed[inner] = (src << 16) + ((j >> 1) << 8) + entry
            return inner + (((code >> 2) & (NZ - 1)) == z).astype(jnp.int32)

        return lax.fori_loop(0, PAIRS, pair, count)

    count = lax.fori_loop(0, NZ, source, 0)
    listed[count] = listed[jnp.maximum(count - 1, 0)]
    return count


def each_live(count, listed, compute, commit):
    def two(i, carry):
        places, values = [], []
        for half in range(2):
            packed = listed[2 * i + half]
            places.append((packed >> 16, (packed >> 8) & 255, packed & 255))
            off = jnp.where(2 * i + half < count, 0.0, HUGE).astype(F32)
            values.append(compute(*places[half], off))
        for half in range(2):
            commit(*places[half], values[half])
        return carry

    lax.fori_loop(0, (count + 1) // 2, two, 0)


LISTED = pltpu.SMEM((128,), jnp.int32)


def row_of(table, src, span, pair):
    here = lax.broadcasted_iota(jnp.int32, (8, 128), 0) == span
    block = table[src, pair]
    return jnp.sum(jnp.where(here, block, 0.0), axis=0, keepdims=True)


def attention_kernel(codes, q, k, v, o, stats, listed):
    stats[...] = jnp.full((NZ, 2, 8, 128), NEVER, F32)

    def clear(i, carry):
        for pair in range(2):
            o[i, pair] = jnp.zeros((ROWS, 256), BF)
        return carry

    lax.fori_loop(0, NZ, clear, 0)
    count = list_live(codes, listed)

    def scores_of(src, span, entry, pair):
        columns = pl.ds(pair * 256, 256)
        q2 = two_heads(q[src * SPANS_HERE + span, :, columns])
        return dot_t(k[entry, :, columns], q2) * SCALE

    def compute_lse(src, span, entry, off):
        found = []
        for pair in range(2):
            scores = scores_of(src, span, entry, pair)
            top = jnp.max(scores, axis=0, keepdims=True)
            lse = top + jnp.log(jnp.sum(jnp.exp(scores - top), axis=0, keepdims=True))
            found.append(jnp.where(off > 0.0, NEVER, lse))
        return found

    def commit_lse(src, span, entry, found):
        here = lax.broadcasted_iota(jnp.int32, (8, 128), 0) == span
        for pair, lse in enumerate(found):
            old = stats[src, pair]
            high = jnp.maximum(old, lse)
            both = high + jnp.log(jnp.exp(old - high) + jnp.exp(lse - high))
            stats[src, pair] = jnp.where(here, both, old)

    each_live(count, listed, compute_lse, commit_lse)

    def compute(src, span, entry, off):
        terms = []
        for pair in range(2):
            scores = scores_of(src, span, entry, pair)
            probs = jnp.exp(scores - (row_of(stats, src, span, pair) + off)).astype(BF)
            terms.append(
                lax.dot_general(
                    probs, v[entry, :, pl.ds(pair * 256, 256)], (((0,), (0,)), ((), ())),
                    preferred_element_type=F32,
                )
            )
        return terms

    def commit(src, span, entry, terms):
        rows = pl.ds(pl.multiple_of(span * SPAN, SPAN), SPAN)
        for pair in range(2):
            for head in range(2):
                at = pl.ds(head * 128, 128)
                term = terms[pair][head * SPAN : (head + 1) * SPAN, head * 128 : (head + 1) * 128]
                o[src, pair, rows, at] = (o[src, pair, rows, at].astype(F32) + term).astype(BF)

    each_live(count, listed, compute, commit)


def local_attention(codes, q, k, v):
    vmem = pl.BlockSpec(memory_space=pltpu.VMEM)
    return pl.pallas_call(
        attention_kernel,
        out_shape=(
            jax.ShapeDtypeStruct((NZ, 2, ROWS, 256), BF),
            jax.ShapeDtypeStruct((NZ, 2, 8, 128), F32),
        ),
        in_specs=[pl.BlockSpec(memory_space=pltpu.SMEM)] + [vmem] * 3,
        out_specs=(vmem, vmem),
        scratch_shapes=[LISTED],
        compiler_params=pltpu.CompilerParams(vmem_limit_bytes=VMEM_BYTES),
        name="local_attention",
    )(codes, q, k, v)


def grads_kernel(
    codes, q_in, k_in, v_in, g_in, totals, key_out, value_out,
    q, k, v, g, key_acc, value_acc, key_low, value_low, loads, stores, listed,
):
    copies = [
        pltpu.make_async_copy(src, dst, loads.at[i])
        for i, (src, dst) in enumerate(((q_in, q), (k_in, k), (v_in, v), (g_in, g)))
    ]
    for copy in copies:
        copy.start()

    def clear_acc(i, carry):
        key_acc[i] = jnp.zeros((KEYS, WIDTH), F32)
        value_acc[i] = jnp.zeros((KEYS, WIDTH), F32)
        return carry

    lax.fori_loop(0, NX * ENTRIES_HERE, clear_acc, 0)
    count = list_live(codes, listed)
    for copy in copies:
        copy.wait()

    def compute(src, span, entry, off):
        row = src * SPANS_HERE + span
        rows = pl.ds(pl.multiple_of(span * SPAN, SPAN), SPAN)
        terms = []
        for pair in range(2):
            columns = pl.ds(pair * 256, 256)
            q2 = two_heads(q[row, :, columns])
            g2 = two_heads(g[src, rows, columns])
            scores = dot_t(k[entry, :, columns], q2) * SCALE
            prob_grad = dot_t(v[entry, :, columns], g2)
            probs = jnp.exp(scores - (row_of(totals, src, span, pair) + off))
            delta = row_of(totals, src, span, 2 + pair)
            score_grad = (probs * (prob_grad - delta)).astype(BF)
            terms.append(
                (
                    jnp.dot(score_grad, q2, preferred_element_type=F32),
                    jnp.dot(probs.astype(BF), g2, preferred_element_type=F32),
                )
            )
        return terms

    def commit(src, span, entry, terms):
        for pair, (key_term, value_term) in enumerate(terms):
            columns = pl.ds(pair * 256, 256)
            key_acc[entry, :, columns] += key_term
            value_acc[entry, :, columns] += value_term

    each_live(count, listed, compute, commit)

    def store(i, which):
        low, to = ((key_low, key_out), (value_low, value_out))[which]
        return pltpu.make_async_copy(low.at[i], to.at[i], stores.at[which, i])

    def close(i, carry):
        key_low[i] = (key_acc[i] * SCALE).astype(BF)
        store(i, 0).start()
        value_low[i] = value_acc[i].astype(BF)
        store(i, 1).start()
        return carry

    def wait(i, carry):
        store(i, 0).wait()
        store(i, 1).wait()
        return carry

    lax.fori_loop(0, NX * ENTRIES_HERE, close, 0)
    lax.fori_loop(0, NX * ENTRIES_HERE, wait, 0)


def local_grads(codes, q, k, v, g, totals):
    entries = (NX * ENTRIES_HERE, KEYS, WIDTH)
    any_spec = pl.BlockSpec(memory_space=pl.ANY)
    vmem = pl.BlockSpec(memory_space=pltpu.VMEM)
    return pl.pallas_call(
        grads_kernel,
        out_shape=(jax.ShapeDtypeStruct(entries, BF),) * 2,
        in_specs=[pl.BlockSpec(memory_space=pltpu.SMEM)] + [any_spec] * 4 + [vmem],
        out_specs=(any_spec,) * 2,
        scratch_shapes=[
            pltpu.VMEM((NZ * SPANS_HERE, SPAN, WIDTH), BF),
            pltpu.VMEM(entries, BF), pltpu.VMEM(entries, BF),
            pltpu.VMEM((NZ, ROWS, WIDTH), BF),
            pltpu.VMEM(entries, F32), pltpu.VMEM(entries, F32),
            pltpu.VMEM(entries, BF), pltpu.VMEM(entries, BF),
            pltpu.SemaphoreType.DMA((4,)), pltpu.SemaphoreType.DMA((2, NX * ENTRIES_HERE)),
            LISTED,
        ],
        compiler_params=pltpu.CompilerParams(vmem_limit_bytes=VMEM_BYTES),
        name="local_grads",
    )(codes, q, k, v, g, totals)


def merge(first, second, write):
    (a_of, a_lse), (b_of, b_lse) = first, second
    high = jnp.maximum(a_lse, b_lse)
    a_part, b_part = jnp.exp(a_lse - high), jnp.exp(b_lse - high)
    both = a_part + b_part
    share = a_part / both
    upper = share.astype(BF).astype(F32)
    lower = share - upper
    row = lax.broadcasted_iota(jnp.int32, (128, 128), 0)
    column = lax.broadcasted_iota(jnp.int32, (128, 128), 1)
    ones = jnp.ones((256, 128), BF)
    for span in range(SPANS_HERE):
        spread = jnp.concatenate(
            [
                jnp.where(row == column, part[span : span + 1, :], 0.0).astype(BF)
                for part in (upper, lower)
            ],
            axis=1,
        )
        weight = jnp.dot(spread, ones, preferred_element_type=F32)
        weight = jnp.concatenate([weight[:SPAN], weight[SPAN:]], axis=1)
        rows = pl.ds(span * SPAN, SPAN)
        a, b = a_of(rows).astype(F32), b_of(rows).astype(F32)
        write(span, b + weight * (a - b))
    return high + jnp.log(both)


class RingMerge:
    def __init__(self, o, lse, got, lse_got, out, lse_out, sems, lse_sems):
        self.line = Line("z")
        self.o, self.lse, self.got, self.lse_got = o, lse, got, lse_got
        self.out, self.lse_out, self.sems, self.lse_sems = out, lse_out, sems, lse_sems

    def copies(self, way, main, step):
        half = way if main else 1 - way
        if step == (0 if main else 1):
            far = self.line.half - step
            block = self.line.off(-far if way else far)
            src, lse = self.o.at[block, half], self.lse.at[block, half]
        else:
            src, lse = self.out.at[way, half, step], self.lse_out.at[way, half, step]
        index = way * 8 + (0 if main else 4) + step
        to = self.line.beside[way]
        return (
            remote(src, self.got.at[way, half, step], self.sems, index, to),
            remote(lse, self.lse_got.at[way, half, step], self.lse_sems, index, to),
        )

    def wait(self, way, main, step):
        for copy in self.copies(way, main, step):
            copy.wait_recv()

    def arrived(self, way, half, step):
        return (lambda rows: self.got[way, half, step, rows, :], self.lse_got[way, half, step])

    def held(self, block, half):
        return (lambda rows: self.o[block, half, rows, :], self.lse[block, half])

    def send(self, way, main, step):
        half = way if main else 1 - way
        if step > (0 if main else 1):
            self.wait(way, main, step - 1)
            far = self.line.half - step
            block = self.line.off(-far if way else far)

            def write(span, value):
                self.out[way, half, step, pl.ds(span * SPAN, SPAN), :] = value.astype(BF)

            self.lse_out[way, half, step] = merge(
                self.arrived(way, half, step - 1), self.held(block, half), write
            )
        for copy in self.copies(way, main, step):
            copy.start()

    def start(self, step):
        for way in range(2):
            self.send(way, True, step)
        if step + 1 < self.line.half:
            for way in range(2):
                self.send(way, False, step + 1)

    def finish(self, half, middle, write):
        for way in range(2):
            self.wait(way, half == way, 3)

        def keep(span, value):
            middle[pl.ds(span * SPAN, SPAN), :] = value

        lse = merge(self.arrived(0, half, 3), self.arrived(1, half, 3), keep)
        return merge(
            (lambda rows: middle[rows, :], lse), self.held(self.line.at, half), write
        )

    def wait_sends(self):
        for way in range(2):
            for main in (True, False):
                for step in range(0 if main else 1, 4):
                    for copy in self.copies(way, main, step):
                        copy.wait_send()


def collect_kernel(
    o, lse, g, cot, w,
    mixed, tall, wide, g_all, totals,
    w_v, o_got, lse_got, o_out, lse_out, middle, att_raw, att, acc, mine,
    local, o_sems, lse_sems, g_sems, edge_sems, pair_sems, y_sems, total_sems,
):
    seq, head, x, z, y, c = place()
    n_seq = NX * NZ
    before = (lax.rem(seq + n_seq - 1, n_seq), head)
    after = (lax.rem(seq + 1, n_seq), head)
    z_peers = [(x * NZ + lax.rem(z + d, NZ), head) for d in range(1, NZ)]
    sibling = (seq, 2 * y + 1 - c)
    own_w = pltpu.make_async_copy(w, w_v, local.at[0])
    own_g = pltpu.make_async_copy(g, g_all.at[z], local.at[1])
    own_w.start()
    own_g.start()
    meet(z_peers + list(Line("y").beside) + [sibling, before, after])
    o_ring = RingMerge(o, lse, o_got, lse_got, o_out, lse_out, o_sems, lse_sems)
    for step in range(4):
        o_ring.start(step)
    g_ring = Ring("z", g, g_all, ROWS, g_sems)
    g_ring.start(0)
    for half in range(2):

        def put_out(span, value):
            att_raw[pl.ds((span + 1) * SPAN, SPAN), pl.ds(half * 256, 256)] = value.astype(BF)

        mine[half] = o_ring.finish(half, middle, put_out)
    edge = remote(
        att_raw.at[pl.ds(ROWS, SPAN)], att_raw.at[pl.ds(0, SPAN)], edge_sems, 0, after
    )
    edge.start()
    mine[2] = jnp.zeros((8, 128), F32)
    mine[3] = jnp.zeros((8, 128), F32)
    for span in range(SPANS_HERE):
        rows = pl.ds(span * SPAN, SPAN)
        terms = g[rows, :].astype(F32) * att_raw[pl.ds((span + 1) * SPAN, SPAN), :].astype(F32)
        for pair in range(2):
            start = pair * 256
            both = jnp.concatenate(
                [terms[:, start : start + 128], terms[:, start + 128 : start + 256]], axis=0
            )
            row = lax.dot_general(
                jnp.ones((8, 128), F32), both, (((1,), (1,)), ((), ())),
                precision=lax.Precision.HIGHEST, preferred_element_type=F32,
            )
            mine[2 + pair, pl.ds(span, 1), :] = row[:1]
    edge.wait()
    lead = att_raw[pl.ds(0, SPAN), :]
    att_raw[pl.ds(0, SPAN), :] = jnp.where(seq == 0, jnp.zeros_like(lead), lead)

    def put_att(block, value):
        att[head, pl.ds(pl.multiple_of(block * SPAN, SPAN), SPAN), :] = value

    shift_rows(att_raw, 1, put_att)
    y_ring = Ring("y", att.at[head], att, ROWS, y_sems, lambda place: 2 * place + c)

    def pair_copy(j):
        block = att.at[2 * y_ring.line.off(j) + c]
        return remote(block, block, pair_sems, j, sibling)

    y_ring.start(0)
    pair_copy(0).start()
    totals[z] = mine[...]
    total_copies = [
        remote(mine, totals.at[z], total_sems, d, z_peers[d]) for d in range(NZ - 1)
    ]
    for copy in total_copies:
        copy.start()
    own_w.wait()

    def use(block, first=False):
        rows = pl.ds(pl.multiple_of(block * WIDTH, WIDTH), WIDTH)
        term = jnp.dot(att[block], w_v[rows, :], preferred_element_type=F32)
        acc[...] = term if first else acc[...] + term
        terms = lax.dot_general(
            att[block], cot[...], (((0,), (0,)), ((), ())), preferred_element_type=F32
        ).astype(BF)
        to_x, part = block // 2, lax.rem(block, 2)
        wide[to_x, pl.ds(pl.multiple_of(part * WIDTH, WIDTH), WIDTH), :] = terms[:, :WIDE]
        for i in range(4):
            tall[part * 4 + i, pl.ds(pl.multiple_of(to_x * 128, 128), 128), :] = terms[
                i * 128 : (i + 1) * 128, WIDE:
            ]

    use(head, True)
    g_ring.start(1)
    pair_copy(0).wait_recv()
    use(2 * y + 1 - c)
    y_ring.start(1)
    y_ring.wait_others()
    pair_copy(1).start()
    pair_copy(3).start()
    for j in (1, 3, 2):
        if j == 2:
            g_ring.start(2)
            y_ring.wait_mains()
            pair_copy(2).start()
        came = y_ring.line.off(j)
        use(2 * came + c)
        pair_copy(j).wait_recv()
        use(2 * came + 1 - c)
    g_ring.start(3)
    mixed[...] = acc[...].astype(BF)
    o_ring.wait_sends()
    y_ring.wait_sends()
    for copy in total_copies:
        copy.wait()
    for j in range(NY):
        pair_copy(j).wait_send()
    own_g.wait()
    g_ring.finish()


def collect(o, lse, g, cot, w):
    def vm(*shape):
        return pltpu.VMEM(shape, BF)

    def sems(n):
        return pltpu.SemaphoreType.DMA((2, n))

    any_spec = pl.BlockSpec(memory_space=pl.ANY)
    vmem = pl.BlockSpec(memory_space=pltpu.VMEM)
    return pl.pallas_call(
        collect_kernel,
        out_shape=(
            jax.ShapeDtypeStruct((ROWS, WIDTH), BF),
            jax.ShapeDtypeStruct((NZ, 512, WIDTH - WIDE), BF),
            jax.ShapeDtypeStruct((NX, 1024, WIDE), BF),
            jax.ShapeDtypeStruct((NZ, ROWS, WIDTH), BF),
            jax.ShapeDtypeStruct((NZ, 4, 8, 128), F32),
        ),
        in_specs=[vmem] * 4 + [any_spec],
        out_specs=(vmem, vmem, vmem, any_spec, vmem),
        scratch_shapes=[
            vm(8 * WIDTH, WIDTH),
            vm(2, 2, 4, ROWS, 256), pltpu.VMEM((2, 2, 4, 8, 128), F32),
            vm(2, 2, 4, ROWS, 256), pltpu.VMEM((2, 2, 4, 8, 128), F32),
            pltpu.VMEM((ROWS, 256), F32), vm(ROWS + SPAN, WIDTH), vm(8, ROWS, WIDTH),
            pltpu.VMEM((ROWS, WIDTH), F32), pltpu.VMEM((4, 8, 128), F32),
            pltpu.SemaphoreType.DMA((2,)), sems(16), sems(16), sems(14), sems(1), sems(4),
            sems(6), sems(7),
        ],
        compiler_params=pltpu.CompilerParams(
            collective_id=2, has_side_effects=True, vmem_limit_bytes=VMEM_BYTES
        ),
        name="collect",
    )(o, lse, g, cot, w)


def finish_kernel(
    wide, tall, keys, values,
    weight_grad, key_grad, value_grad,
    k_v, v_v, k_got, k_sums, v_got, v_sums,
    wide_got, wide_sum, wide_z, tall_got, tall_sums, tall_sum, tall_x,
    local, k_sems, v_sems, wide_sems, wide_z_sems, tall_sems, tall_x_sems,
):
    seq, head, x, z, y, c = place()
    z_peers = [(x * NZ + lax.rem(z + d, NZ), head) for d in range(1, NZ)]
    x_peers = [(lax.rem(x + d, NX) * NZ + z, head) for d in range(1, NX)]
    own_k = pltpu.make_async_copy(keys, k_v, local.at[0])
    own_v = pltpu.make_async_copy(values, v_v, local.at[1])
    own_k.start()
    own_v.start()
    meet(z_peers + x_peers)
    tall_ring = RingSum("z", tall, 512, tall_got, tall_sums, tall_sems)
    tall_ring.start(0)

    def wide_copy(apart):
        to = lax.rem(x + apart, NX)
        return remote(
            wide.at[to], wide_got.at[apart - 1], wide_sems, apart - 1, (to * NZ + z, head)
        )

    for apart in range(1, NX):
        wide_copy(apart).start()
    own_k.wait()
    own_v.wait()
    k_ring = RingSum("x", k_v, 512, k_got, k_sums, k_sems)
    v_ring = RingSum("x", v_v, 512, v_got, v_sums, v_sems)
    k_ring.start(0)
    v_ring.start(0)
    tall_ring.start(1)
    tall_ring.start(2)
    k_ring.start(1)
    for apart in range(1, NX):
        wide_copy(apart).wait_recv()

    def add_wide(i, carry):
        rows = pl.ds(pl.multiple_of(i * 128, 128), 128)
        total = wide[x, rows, :].astype(F32)
        for d in range(NX - 1):
            total = total + wide_got[d, rows, :].astype(F32)
        wide_sum[i] = total.astype(BF)
        return carry

    lax.fori_loop(0, NZ, add_wide, 0)
    wide_z_copies = [
        remote(wide_sum.at[lax.rem(z + d + 1, NZ)], wide_z.at[d], wide_z_sems, d, z_peers[d])
        for d in range(NZ - 1)
    ]
    for copy in wide_z_copies:
        copy.start()
    tall_ring.start(3)
    v_ring.start(1)
    tall_ring.wait_last()

    def put_tall(rows, total):
        tall_sum[rows, :] = total.astype(BF)

    tall_ring.total(put_tall, lambda rows: tall[z, rows, :], 32)

    def x_rows(to):
        return pl.ds(pl.multiple_of(to * 128, 128), 128)

    tall_x_copies = [
        remote(
            tall_sum.at[x_rows(lax.rem(x + d + 1, NX))],
            tall_x.at[d], tall_x_sems, d, x_peers[d],
        )
        for d in range(NX - 1)
    ]
    for copy in tall_x_copies:
        copy.start()
    for ring, mine, out in ((k_ring, k_v, key_grad), (v_ring, v_v, value_grad)):
        ring.wait_last()

        def put(rows, total, out=out):
            out[rows, :] = total.astype(BF)

        ring.total(put, lambda rows, mine=mine: mine[x, rows, :], 32)
    for copy in wide_z_copies:
        copy.wait_recv()
    total = wide_sum[z].astype(F32)
    for d in range(NZ - 1):
        total = total + wide_z[d].astype(F32)
    weight_grad[:, :WIDE] = total.astype(BF)
    for copy in tall_x_copies:
        copy.wait_recv()
    total = tall_sum[x_rows(x), :].astype(F32)
    for d in range(NX - 1):
        total = total + tall_x[d].astype(F32)
    weight_grad[:, WIDE:] = total.astype(BF)
    for ring in (k_ring, v_ring, tall_ring):
        ring.wait_sends()
    for copy in wide_z_copies + tall_x_copies:
        copy.wait_send()
    for apart in range(1, NX):
        wide_copy(apart).wait_send()


def finish(wide, tall_blocks, keys, values):
    def vm(*shape):
        return pltpu.VMEM(shape, BF)

    def sems(n):
        return pltpu.SemaphoreType.DMA((2, n))

    any_spec = pl.BlockSpec(memory_space=pl.ANY)
    vmem = pl.BlockSpec(memory_space=pltpu.VMEM)
    entry = (ENTRIES_HERE * KEYS, WIDTH)
    tall = WIDTH - WIDE
    return pl.pallas_call(
        finish_kernel,
        out_shape=(
            jax.ShapeDtypeStruct((128, WIDTH), BF),
            jax.ShapeDtypeStruct(entry, BF),
            jax.ShapeDtypeStruct(entry, BF),
        ),
        in_specs=[vmem] * 2 + [any_spec] * 2,
        out_specs=(vmem,) * 3,
        scratch_shapes=[
            vm(NX, *entry), vm(NX, *entry),
            vm(2, 2, 2, 256, WIDTH), vm(2, 2, 2, 256, WIDTH),
            vm(2, 2, 2, 256, WIDTH), vm(2, 2, 2, 256, WIDTH),
            vm(NX - 1, 1024, WIDE), vm(NZ, 128, WIDE),
            vm(NZ - 1, 128, WIDE), vm(2, 2, 4, 256, tall), vm(2, 2, 4, 256, tall),
            vm(512, tall), vm(NX - 1, 128, tall),
            pltpu.SemaphoreType.DMA((2,)), sems(8), sems(8),
            sems(3), sems(7), sems(16), sems(3),
        ],
        compiler_params=pltpu.CompilerParams(
            collective_id=3, has_side_effects=True, vmem_limit_bytes=VMEM_BYTES
        ),
        name="finish",
    )(wide, tall_blocks, keys, values)


def publish_kernel(*refs):
    for i in range(4):
        refs[4 + i][...] = refs[i][...]


def publish(*arrays):
    vmem = pl.BlockSpec(memory_space=pltpu.VMEM)
    return pl.pallas_call(
        publish_kernel,
        out_shape=tuple(jax.ShapeDtypeStruct(a.shape, a.dtype) for a in arrays),
        in_specs=[vmem] * 4,
        out_specs=(vmem,) * 4,
        name="publish",
    )(*arrays)


def body(queries, cache_keys, cache_values, owners, slots, out_weight, cotangent):
    codes = (owners * ENTRIES_HERE + slots).reshape(1, PAIRS)
    codes = jnp.pad(codes, ((0, 7), (0, 128 - PAIRS)))
    q, g, k, v, codes = gather_all(
        queries, cache_keys, cache_values, codes, cotangent, out_weight
    )
    q = q.reshape(NZ * SPANS_HERE, SPAN, WIDTH)
    k = k.reshape(NX * ENTRIES_HERE, KEYS, WIDTH)
    v = v.reshape(NX * ENTRIES_HERE, KEYS, WIDTH)
    out, lse = local_attention(codes, q, k, v)
    mixed, tall, wide, g_all, totals = collect(out, lse, g, cotangent, out_weight)
    key_terms, value_terms = local_grads(codes, q, k, v, g_all, totals)
    entries = (NX, ENTRIES_HERE * KEYS, WIDTH)
    weight_grad, key_grad, value_grad = finish(
        wide, tall, key_terms.reshape(entries), value_terms.reshape(entries)
    )
    mixed, weight_grad, key_grad, value_grad = publish(
        mixed, weight_grad, key_grad, value_grad
    )
    shape = (ENTRIES_HERE, KEYS, WIDTH)
    return mixed, weight_grad, key_grad.reshape(shape), value_grad.reshape(shape)


def solution(mesh):
    placed = (
        P("seq", "head"),
        P("seq", None, "head"),
        P("seq", None, "head"),
        P("seq", None),
        P("seq", None),
        P(None, "head"),
        P("seq", "head"),
    )
    return jax.shard_map(
        body,
        mesh=mesh,
        in_specs=placed,
        out_specs=(
            P("seq", "head"),
            P("seq", "head"),
            P("seq", None, "head"),
            P("seq", None, "head"),
        ),
        check_vma=False,
    )
```

```python
import functools
import math

import jax
import jax.numpy as jnp
from jax import lax
from jax.experimental import pallas as pl
from jax.experimental.pallas import tpu as pltpu
from jax.sharding import PartitionSpec as P

HEAD_DIM = 128
SPAN = 64
TOP = 2
NX, NZ, NY = 4, 8, 4
ROWS, WIDTH = 448, 512
SPANS_HERE = 7
PAIRS = SPANS_HERE * TOP
ENTRIES_HERE = 4
KEYS = 128
HALF = ROWS // 2
WIDE = 128
SCALE = 1.0 / math.sqrt(HEAD_DIM)
NEVER, HUGE = -1e30, 1e30
VMEM_BYTES = 56 * 1024 * 1024
MESH_ID = pl.DeviceIdType.MESH
BF, F32 = jnp.bfloat16, jnp.float32


def place():
    seq, head = lax.axis_index("seq"), lax.axis_index("head")
    return seq, head, seq // NZ, lax.rem(seq, NZ), head // 2, lax.rem(head, 2)


def remote(src, dst, sems, index, device):
    return pltpu.make_async_remote_copy(
        src_ref=src,
        dst_ref=dst,
        send_sem=sems.at[0, index],
        recv_sem=sems.at[1, index],
        device_id=device,
        device_id_type=MESH_ID,
    )


def meet(devices):
    sem = pltpu.get_barrier_semaphore()
    for device in devices:
        pl.semaphore_signal(sem, inc=1, device_id=device, device_id_type=MESH_ID)
    pl.semaphore_wait(sem, len(devices))


def selector(step):
    row = lax.broadcasted_iota(jnp.int32, (SPAN, 2 * SPAN), 0)
    column = lax.broadcasted_iota(jnp.int32, (SPAN, 2 * SPAN), 1)
    return (column == row + step).astype(F32).astype(BF)


def shift_rows(raw, step, write):
    pick = selector(step)

    def one(block, carry):
        window = raw[pl.ds(pl.multiple_of(block * SPAN, SPAN), 2 * SPAN), :]
        write(block, jnp.dot(pick, window, preferred_element_type=F32).astype(BF))
        return carry

    lax.fori_loop(0, SPANS_HERE, one, 0)


class Line:
    def __init__(self, axis):
        seq, head, x, z, y, c = place()
        if axis == "z":
            self.n, self.at, to = NZ, z, lambda i: (x * NZ + i, head)
        elif axis == "x":
            self.n, self.at, to = NX, x, lambda i: (i * NZ + z, head)
        else:
            self.n, self.at, to = NY, y, lambda i: (seq, 2 * i + c)
        self.half = self.n // 2
        self.beside = (to(self.off(1)), to(self.off(-1)))

    def off(self, steps):
        return lax.rem(self.at + steps + self.n, self.n)


class Ring:
    def __init__(self, axis, first, out, rows, sems, slot=lambda place: place):
        self.line, self.first, self.out, self.sems, self.slot = (
            Line(axis), first, out, sems, slot,
        )
        self.rows = rows // 2

    def copy(self, way, main, step):
        slot = self.slot(self.line.off(step if way else -step))
        half = way if main else 1 - way
        rows = pl.ds(half * self.rows, self.rows)
        dst = self.out.at[slot, rows]
        src = dst if step else self.first.at[rows]
        index = way * (self.line.n - 1) + (0 if main else self.line.half) + step
        return remote(src, dst, self.sems, index, self.line.beside[way])

    def start(self, step):
        for main in (True, False):
            if main or step < self.line.half - 1:
                for way in range(2):
                    if step:
                        self.copy(way, main, step - 1).wait_recv()
                    self.copy(way, main, step).start()

    def wait_others(self):
        for way in range(2):
            self.copy(way, False, self.line.half - 2).wait_recv()

    def wait_mains(self):
        for way in range(2):
            self.copy(way, True, self.line.half - 1).wait_recv()

    def wait_sends(self):
        for way in range(2):
            for step in range(self.line.half):
                self.copy(way, True, step).wait_send()
            for step in range(self.line.half - 1):
                self.copy(way, False, step).wait_send()

    def finish(self):
        self.wait_others()
        self.wait_mains()
        self.wait_sends()


class RingSum:
    def __init__(self, axis, blocks, rows, got, sums, sems):
        self.line = Line(axis)
        self.blocks, self.got, self.sums, self.sems = blocks, got, sums, sems
        self.rows = rows // 2

    def copy(self, way, main, step):
        half = way if main else 1 - way
        if step == (0 if main else 1):
            far = self.line.half - step
            block = self.line.off(-far if way else far)
            src = self.blocks.at[block, pl.ds(half * self.rows, self.rows)]
        else:
            src = self.sums.at[way, half, step]
        index = way * self.line.n + (0 if main else self.line.half) + step
        dst = self.got.at[way, half, step]
        return remote(src, dst, self.sems, index, self.line.beside[way])

    def send(self, way, main, step):
        half = way if main else 1 - way
        if step > (0 if main else 1):
            self.copy(way, main, step - 1).wait_recv()
            far = self.line.half - step
            block = self.line.off(-far if way else far)
            piece = 32

            def add(i, carry):
                rows = pl.ds(pl.multiple_of(i * piece, piece), piece)
                from_rows = pl.ds(pl.multiple_of(half * self.rows + i * piece, piece), piece)
                self.sums[way, half, step, rows, :] = (
                    self.blocks[block, from_rows, :].astype(F32)
                    + self.got[way, half, step - 1, rows, :].astype(F32)
                ).astype(BF)
                return carry

            lax.fori_loop(0, self.rows // piece, add, 0)
        self.copy(way, main, step).start()

    def start(self, step):
        for way in range(2):
            self.send(way, True, step)
        if step + 1 < self.line.half:
            for way in range(2):
                self.send(way, False, step + 1)

    def wait_last(self):
        for main in (False, True):
            for way in range(2):
                self.copy(way, main, self.line.half - 1).wait_recv()

    def wait_sends(self):
        for way in range(2):
            for step in range(self.line.half):
                self.copy(way, True, step).wait_send()
            for step in range(1, self.line.half):
                self.copy(way, False, step).wait_send()

    def total(self, write, mine, piece):
        for half in range(2):

            def one(i, carry):
                rows = pl.ds(pl.multiple_of(i * piece, piece), piece)
                at = pl.ds(pl.multiple_of(half * self.rows + i * piece, piece), piece)
                term = mine(at).astype(F32)
                for way in range(2):
                    term = term + self.got[way, half, self.line.half - 1, rows, :].astype(F32)
                write(at, term)
                return carry

            lax.fori_loop(0, self.rows // piece, one, 0)


def gather_kernel(
    q, k, v, codes, cot, w,
    q_all, g_own, k_all, v_all, codes_all,
    q_raw, q_sh, g_raw, g_sh, cot_v, w_v, part, pair_got, y_blocks, y_got, y_sums, g_acc,
    local, q_sems, k_sems, v_sems, code_sems, edge_sems, pair_sems, y_sems,
):
    seq, head, x, z, y, c = place()
    n_seq = NX * NZ
    before = (lax.rem(seq + n_seq - 1, n_seq), head)
    after = (lax.rem(seq + 1, n_seq), head)
    z_peers = [(x * NZ + lax.rem(z + d, NZ), head) for d in range(1, NZ)]
    sibling = (seq, 2 * y + 1 - c)
    own_q = pltpu.make_async_copy(q, q_raw.at[pl.ds(0, ROWS)], local.at[0])
    own_cot = pltpu.make_async_copy(cot, cot_v, local.at[1])
    own_w = pltpu.make_async_copy(w, w_v, local.at[2])
    own_q.start()
    own_cot.start()
    own_w.start()
    meet(
        z_peers + list(Line("x").beside) + list(Line("y").beside) + [sibling, before, after]
    )
    q_edge = remote(q.at[pl.ds(0, SPAN)], q_raw.at[pl.ds(ROWS, SPAN)], edge_sems, 0, before)
    q_edge.start()
    k_ring = Ring("x", k, k_all, ENTRIES_HERE, k_sems)
    v_ring = Ring("x", v, v_all, ENTRIES_HERE, v_sems)
    k_ring.start(0)
    v_ring.start(0)
    code_copies = [
        remote(codes, codes_all.at[z], code_sems, d, z_peers[d]) for d in range(NZ - 1)
    ]
    for copy in code_copies:
        copy.start()
    own_k = pltpu.make_async_copy(k, k_all.at[x], local.at[3])
    own_v = pltpu.make_async_copy(v, v_all.at[x], local.at[4])
    own_codes = pltpu.make_async_copy(codes, codes_all.at[z], local.at[5])
    own_k.start()
    own_v.start()
    own_codes.start()
    own_q.wait()
    q_edge.wait()
    last = seq == n_seq - 1
    tail = q_raw[pl.ds(ROWS, SPAN), :]
    q_raw[pl.ds(ROWS, SPAN), :] = jnp.where(last, jnp.zeros_like(tail), tail)

    def put_q(block, value):
        q_sh[pl.ds(pl.multiple_of(block * SPAN, SPAN), SPAN), :] = value

    shift_rows(q_raw, SPAN - 1, put_q)
    q_ring = Ring("z", q_sh, q_all, ROWS, q_sems)
    q_ring.start(0)
    keep_q = pltpu.make_async_copy(q_sh, q_all.at[z], local.at[6])
    keep_q.start()

    own_cot.wait()
    own_w.wait()

    def product(to_head):
        rows = pl.ds(pl.multiple_of(to_head * WIDTH, WIDTH), WIDTH)
        return lax.dot_general(
            cot_v[...], w_v[rows, :], (((1,), (1,)), ((), ())), preferred_element_type=F32
        )

    def pair_copy(j):
        return remote(part.at[j], pair_got.at[j], pair_sems, j, sibling)

    def for_sibling(i, carry):
        j = NY - 1 - i
        part[j] = product(2 * lax.rem(y + j, NY) + 1 - c).astype(BF)
        pair_copy(j).start()
        return carry

    lax.fori_loop(0, NY, for_sibling, 0)

    def for_row(i, carry):
        j = NY - 1 - i
        to = lax.rem(y + j, NY)
        value = product(2 * to + c)
        pair_copy(j).wait_recv()
        y_blocks[to] = (value + pair_got[j].astype(F32)).astype(BF)
        return carry

    lax.fori_loop(0, NY - 1, for_row, 0)
    y_ring = RingSum("y", y_blocks, ROWS, y_got, y_sums, y_sems)
    y_ring.start(0)
    mine = product(2 * y + c)
    pair_copy(0).wait_recv()
    g_acc[...] = mine + pair_got[0].astype(F32)
    q_ring.start(1)
    y_ring.start(1)
    k_ring.start(1)
    q_ring.start(2)
    v_ring.start(1)
    y_ring.wait_last()

    def put_g(rows, total):
        g_raw[rows, :] = total.astype(BF)

    y_ring.total(put_g, lambda rows: g_acc[rows, :], 32)
    g_edge = remote(
        g_raw.at[pl.ds(0, SPAN)], g_raw.at[pl.ds(ROWS, SPAN)], edge_sems, 1, before
    )
    g_edge.start()
    q_ring.start(3)
    g_edge.wait()
    tail = g_raw[pl.ds(ROWS, SPAN), :]
    g_raw[pl.ds(ROWS, SPAN), :] = jnp.where(last, jnp.zeros_like(tail), tail)

    def put_gs(block, value):
        g_sh[pl.ds(pl.multiple_of(block * SPAN, SPAN), SPAN), :] = value

    shift_rows(g_raw, SPAN - 1, put_gs)
    keep_g = pltpu.make_async_copy(g_sh, g_own, local.at[7])
    keep_g.start()
    q_ring.finish()
    k_ring.finish()
    v_ring.finish()
    for copy in code_copies:
        copy.wait()
    for j in range(NY):
        pair_copy(j).wait_send()
    y_ring.wait_sends()
    own_k.wait()
    own_v.wait()
    own_codes.wait()
    keep_q.wait()
    keep_g.wait()


def gather_all(q, k, v, codes, cot, w):
    def vm(*shape):
        return pltpu.VMEM(shape, BF)

    def sems(n):
        return pltpu.SemaphoreType.DMA((2, n))

    any_spec = pl.BlockSpec(memory_space=pl.ANY)
    entries = (NX, ENTRIES_HERE, KEYS, WIDTH)
    return pl.pallas_call(
        gather_kernel,
        out_shape=(
            jax.ShapeDtypeStruct((NZ, ROWS, WIDTH), BF),
            jax.ShapeDtypeStruct((ROWS, WIDTH), BF),
            jax.ShapeDtypeStruct(entries, BF),
            jax.ShapeDtypeStruct(entries, BF),
            jax.ShapeDtypeStruct((NZ, 8, 128), jnp.int32),
        ),
        in_specs=[any_spec] * 6,
        out_specs=(any_spec,) * 5,
        scratch_shapes=[
            vm(ROWS + SPAN, WIDTH), vm(ROWS, WIDTH), vm(ROWS + SPAN, WIDTH), vm(ROWS, WIDTH),
            vm(ROWS, WIDTH), vm(8 * WIDTH, WIDTH), vm(NY, ROWS, WIDTH), vm(NY, ROWS, WIDTH),
            vm(NY, ROWS, WIDTH), vm(2, 2, 2, HALF, WIDTH), vm(2, 2, 2, HALF, WIDTH),
            pltpu.VMEM((ROWS, WIDTH), F32),
            pltpu.SemaphoreType.DMA((8,)), sems(14), sems(6), sems(6), sems(7),
            sems(2), sems(4), sems(8),
        ],
        compiler_params=pltpu.CompilerParams(
            collective_id=0, has_side_effects=True, vmem_limit_bytes=VMEM_BYTES
        ),
        name="gather_all",
    )(q, k, v, codes, cot, w)


def two_heads(block):
    lane = lax.broadcasted_iota(jnp.int32, block.shape, 1)
    zero = jnp.zeros_like(block)
    upper = jnp.where(lane < HEAD_DIM, block, zero)
    lower = jnp.where(lane < HEAD_DIM, zero, block)
    return jnp.concatenate([upper, lower], axis=0)


def dot_t(a, b):
    return lax.dot_general(a, b, (((1,), (1,)), ((), ())), preferred_element_type=F32)


GROUP = 4


def list_live(codes, listed):
    z = lax.rem(lax.axis_index("seq"), NZ)

    def source(src, count):
        def pair(j, inner):
            code = codes[src, 0, j]
            entry = ((code >> 5) << 2) + (code & 3)
            listed[inner] = (src << 16) + ((j >> 1) << 8) + entry
            return inner + (((code >> 2) & (NZ - 1)) == z).astype(jnp.int32)

        return lax.fori_loop(0, PAIRS, pair, count)

    count = lax.fori_loop(0, NZ, source, 0)
    for i in range(GROUP - 1):
        listed[count + i] = listed[jnp.maximum(count - 1, 0)]
    return count


def each_live(count, listed, compute, commit):
    def group(i, carry):
        places, values = [], []
        for member in range(GROUP):
            at = GROUP * i + member
            packed = listed[at]
            places.append((packed >> 16, (packed >> 8) & 255, packed & 255))
            off = jnp.where(at < count, 0.0, HUGE).astype(F32)
            values.append(compute(*places[member], off))
        for member in range(GROUP):
            commit(*places[member], values[member])
        return carry

    lax.fori_loop(0, (count + GROUP - 1) // GROUP, group, 0)


LISTED = pltpu.SMEM((128,), jnp.int32)


def row_of(table, src, span, pair):
    here = lax.broadcasted_iota(jnp.int32, (8, 128), 0) == span
    block = table[src, pair]
    return jnp.sum(jnp.where(here, block, 0.0), axis=0, keepdims=True)


def attention_kernel(codes, q_in, k_in, v_in, o, stats, q, k, v, listed, loads):
    copies = [
        pltpu.make_async_copy(src, dst, loads.at[i])
        for i, (src, dst) in enumerate(((k_in, k), (q_in, q), (v_in, v)))
    ]
    for copy in copies:
        copy.start()
    stats[...] = jnp.full((NZ, 2, 8, 128), NEVER, F32)

    def clear(i, carry):
        for pair in range(2):
            o[i, pair] = jnp.zeros((ROWS, 256), BF)
        return carry

    lax.fori_loop(0, NZ, clear, 0)
    count = list_live(codes, listed)
    copies[0].wait()
    copies[1].wait()

    def scores_of(src, span, entry, pair):
        columns = pl.ds(pair * 256, 256)
        q2 = two_heads(q[src * SPANS_HERE + span, :, columns])
        return dot_t(k[entry, :, columns], q2) * SCALE

    def compute_lse(src, span, entry, off):
        found = []
        for pair in range(2):
            scores = scores_of(src, span, entry, pair)
            top = jnp.max(scores, axis=0, keepdims=True)
            lse = top + jnp.log(jnp.sum(jnp.exp(scores - top), axis=0, keepdims=True))
            found.append(jnp.where(off > 0.0, NEVER, lse))
        return found

    def commit_lse(src, span, entry, found):
        here = lax.broadcasted_iota(jnp.int32, (8, 128), 0) == span
        for pair, lse in enumerate(found):
            old = stats[src, pair]
            high = jnp.maximum(old, lse)
            both = high + jnp.log(jnp.exp(old - high) + jnp.exp(lse - high))
            stats[src, pair] = jnp.where(here, both, old)

    each_live(count, listed, compute_lse, commit_lse)
    copies[2].wait()

    def compute(src, span, entry, off):
        terms = []
        for pair in range(2):
            scores = scores_of(src, span, entry, pair)
            probs = jnp.exp(scores - (row_of(stats, src, span, pair) + off)).astype(BF)
            terms.append(
                lax.dot_general(
                    probs, v[entry, :, pl.ds(pair * 256, 256)], (((0,), (0,)), ((), ())),
                    preferred_element_type=F32,
                )
            )
        return terms

    def commit(src, span, entry, terms):
        rows = pl.ds(pl.multiple_of(span * SPAN, SPAN), SPAN)
        for pair in range(2):
            for head in range(2):
                at = pl.ds(head * 128, 128)
                term = terms[pair][head * SPAN : (head + 1) * SPAN, head * 128 : (head + 1) * 128]
                o[src, pair, rows, at] = (o[src, pair, rows, at].astype(F32) + term).astype(BF)

    each_live(count, listed, compute, commit)


def local_attention(codes, q, k, v):
    vmem = pl.BlockSpec(memory_space=pltpu.VMEM)
    entries = (NX * ENTRIES_HERE, KEYS, WIDTH)
    return pl.pallas_call(
        attention_kernel,
        out_shape=(
            jax.ShapeDtypeStruct((NZ, 2, ROWS, 256), BF),
            jax.ShapeDtypeStruct((NZ, 2, 8, 128), F32),
        ),
        in_specs=[pl.BlockSpec(memory_space=pltpu.SMEM)]
        + [pl.BlockSpec(memory_space=pl.ANY)] * 3,
        out_specs=(vmem, vmem),
        scratch_shapes=[
            pltpu.VMEM((NZ * SPANS_HERE, SPAN, WIDTH), BF),
            pltpu.VMEM(entries, BF), pltpu.VMEM(entries, BF),
            LISTED, pltpu.SemaphoreType.DMA((3,)),
        ],
        compiler_params=pltpu.CompilerParams(vmem_limit_bytes=VMEM_BYTES),
        name="local_attention",
    )(codes, q, k, v)


def grads_kernel(
    codes, q_in, k_in, v_in, g_in, totals, key_out, value_out,
    q, k, v, g, key_acc, value_acc, key_low, value_low, loads, stores, listed,
):
    copies = [
        pltpu.make_async_copy(src, dst, loads.at[i])
        for i, (src, dst) in enumerate(((q_in, q), (k_in, k), (v_in, v), (g_in, g)))
    ]
    for copy in copies:
        copy.start()

    def clear_acc(i, carry):
        key_acc[i] = jnp.zeros((KEYS, WIDTH), F32)
        value_acc[i] = jnp.zeros((KEYS, WIDTH), F32)
        return carry

    lax.fori_loop(0, NX * ENTRIES_HERE, clear_acc, 0)
    count = list_live(codes, listed)
    for copy in copies:
        copy.wait()

    def compute(src, span, entry, off):
        row = src * SPANS_HERE + span
        rows = pl.ds(pl.multiple_of(span * SPAN, SPAN), SPAN)
        terms = []
        for pair in range(2):
            columns = pl.ds(pair * 256, 256)
            q2 = two_heads(q[row, :, columns])
            g2 = two_heads(g[src, rows, columns])
            scores = dot_t(k[entry, :, columns], q2) * SCALE
            prob_grad = dot_t(v[entry, :, columns], g2)
            probs = jnp.exp(scores - (row_of(totals, src, span, pair) + off))
            delta = row_of(totals, src, span, 2 + pair)
            score_grad = (probs * (prob_grad - delta)).astype(BF)
            terms.append(
                (
                    jnp.dot(score_grad, q2, preferred_element_type=F32),
                    jnp.dot(probs.astype(BF), g2, preferred_element_type=F32),
                )
            )
        return terms

    def commit(src, span, entry, terms):
        for pair, (key_term, value_term) in enumerate(terms):
            columns = pl.ds(pair * 256, 256)
            key_acc[entry, :, columns] += key_term
            value_acc[entry, :, columns] += value_term

    each_live(count, listed, compute, commit)

    def store(i, which):
        low, to = ((key_low, key_out), (value_low, value_out))[which]
        return pltpu.make_async_copy(low.at[i], to.at[i], stores.at[which, i])

    def close(i, carry):
        key_low[i] = (key_acc[i] * SCALE).astype(BF)
        store(i, 0).start()
        value_low[i] = value_acc[i].astype(BF)
        store(i, 1).start()
        return carry

    def wait(i, carry):
        store(i, 0).wait()
        store(i, 1).wait()
        return carry

    lax.fori_loop(0, NX * ENTRIES_HERE, close, 0)
    lax.fori_loop(0, NX * ENTRIES_HERE, wait, 0)


def local_grads(codes, q, k, v, g, totals):
    entries = (NX * ENTRIES_HERE, KEYS, WIDTH)
    any_spec = pl.BlockSpec(memory_space=pl.ANY)
    vmem = pl.BlockSpec(memory_space=pltpu.VMEM)
    return pl.pallas_call(
        grads_kernel,
        out_shape=(jax.ShapeDtypeStruct(entries, BF),) * 2,
        in_specs=[pl.BlockSpec(memory_space=pltpu.SMEM)] + [any_spec] * 4 + [vmem],
        out_specs=(any_spec,) * 2,
        scratch_shapes=[
            pltpu.VMEM((NZ * SPANS_HERE, SPAN, WIDTH), BF),
            pltpu.VMEM(entries, BF), pltpu.VMEM(entries, BF),
            pltpu.VMEM((NZ, ROWS, WIDTH), BF),
            pltpu.VMEM(entries, F32), pltpu.VMEM(entries, F32),
            pltpu.VMEM(entries, BF), pltpu.VMEM(entries, BF),
            pltpu.SemaphoreType.DMA((4,)), pltpu.SemaphoreType.DMA((2, NX * ENTRIES_HERE)),
            LISTED,
        ],
        compiler_params=pltpu.CompilerParams(vmem_limit_bytes=VMEM_BYTES),
        name="local_grads",
    )(codes, q, k, v, g, totals)


def merge(first, second, write):
    (a_of, a_lse), (b_of, b_lse) = first, second
    high = jnp.maximum(a_lse, b_lse)
    a_part, b_part = jnp.exp(a_lse - high), jnp.exp(b_lse - high)
    both = a_part + b_part
    share = a_part / both
    upper = share.astype(BF).astype(F32)
    lower = share - upper
    row = lax.broadcasted_iota(jnp.int32, (128, 128), 0)
    column = lax.broadcasted_iota(jnp.int32, (128, 128), 1)
    ones = jnp.ones((256, 128), BF)
    for span in range(SPANS_HERE):
        spread = jnp.concatenate(
            [
                jnp.where(row == column, part[span : span + 1, :], 0.0).astype(BF)
                for part in (upper, lower)
            ],
            axis=1,
        )
        weight = jnp.dot(spread, ones, preferred_element_type=F32)
        weight = jnp.concatenate([weight[:SPAN], weight[SPAN:]], axis=1)
        rows = pl.ds(span * SPAN, SPAN)
        a, b = a_of(rows).astype(F32), b_of(rows).astype(F32)
        write(span, b + weight * (a - b))
    return high + jnp.log(both)


class RingMerge:
    def __init__(self, o, lse, got, lse_got, out, lse_out, sems, lse_sems):
        self.line = Line("z")
        self.o, self.lse, self.got, self.lse_got = o, lse, got, lse_got
        self.out, self.lse_out, self.sems, self.lse_sems = out, lse_out, sems, lse_sems

    def copies(self, way, main, step):
        half = way if main else 1 - way
        if step == (0 if main else 1):
            far = self.line.half - step
            block = self.line.off(-far if way else far)
            src, lse = self.o.at[block, half], self.lse.at[block, half]
        else:
            src, lse = self.out.at[way, half, step], self.lse_out.at[way, half, step]
        index = way * 8 + (0 if main else 4) + step
        to = self.line.beside[way]
        return (
            remote(src, self.got.at[way, half, step], self.sems, index, to),
            remote(lse, self.lse_got.at[way, half, step], self.lse_sems, index, to),
        )

    def wait(self, way, main, step):
        for copy in self.copies(way, main, step):
            copy.wait_recv()

    def arrived(self, way, half, step):
        return (lambda rows: self.got[way, half, step, rows, :], self.lse_got[way, half, step])

    def held(self, block, half):
        return (lambda rows: self.o[block, half, rows, :], self.lse[block, half])

    def send(self, way, main, step):
        half = way if main else 1 - way
        if step > (0 if main else 1):
            self.wait(way, main, step - 1)
            far = self.line.half - step
            block = self.line.off(-far if way else far)

            def write(span, value):
                self.out[way, half, step, pl.ds(span * SPAN, SPAN), :] = value.astype(BF)

            self.lse_out[way, half, step] = merge(
                self.arrived(way, half, step - 1), self.held(block, half), write
            )
        for copy in self.copies(way, main, step):
            copy.start()

    def start(self, step):
        for way in range(2):
            self.send(way, True, step)
        if step + 1 < self.line.half:
            for way in range(2):
                self.send(way, False, step + 1)

    def finish(self, half, middle, write):
        for way in range(2):
            self.wait(way, half == way, 3)

        def keep(span, value):
            middle[pl.ds(span * SPAN, SPAN), :] = value

        lse = merge(self.arrived(0, half, 3), self.arrived(1, half, 3), keep)
        return merge(
            (lambda rows: middle[rows, :], lse), self.held(self.line.at, half), write
        )

    def wait_sends(self):
        for way in range(2):
            for main in (True, False):
                for step in range(0 if main else 1, 4):
                    for copy in self.copies(way, main, step):
                        copy.wait_send()


def collect_kernel(
    o, lse, g, cot, w,
    mixed, tall, wide_sum, g_all, totals,
    w_v, wide, wide_got, o_got, lse_got, o_out, lse_out, middle, att_raw, att, acc, mine,
    local, o_sems, lse_sems, g_sems, edge_sems, pair_sems, y_sems, total_sems, wide_sems,
):
    seq, head, x, z, y, c = place()
    n_seq = NX * NZ
    before = (lax.rem(seq + n_seq - 1, n_seq), head)
    after = (lax.rem(seq + 1, n_seq), head)
    z_peers = [(x * NZ + lax.rem(z + d, NZ), head) for d in range(1, NZ)]
    x_peers = [(lax.rem(x + d, NX) * NZ + z, head) for d in range(1, NX)]
    sibling = (seq, 2 * y + 1 - c)
    own_w = pltpu.make_async_copy(w, w_v, local.at[0])
    own_g = pltpu.make_async_copy(g, g_all.at[z], local.at[1])
    own_w.start()
    own_g.start()
    meet(z_peers + x_peers + list(Line("y").beside) + [sibling, before, after])
    o_ring = RingMerge(o, lse, o_got, lse_got, o_out, lse_out, o_sems, lse_sems)
    for step in range(4):
        o_ring.start(step)
    g_ring = Ring("z", g, g_all, ROWS, g_sems)
    g_ring.start(0)
    for half in range(2):

        def put_out(span, value):
            att_raw[pl.ds((span + 1) * SPAN, SPAN), pl.ds(half * 256, 256)] = value.astype(BF)

        mine[half] = o_ring.finish(half, middle, put_out)
    edge = remote(
        att_raw.at[pl.ds(ROWS, SPAN)], att_raw.at[pl.ds(0, SPAN)], edge_sems, 0, after
    )
    edge.start()
    mine[2] = jnp.zeros((8, 128), F32)
    mine[3] = jnp.zeros((8, 128), F32)
    for span in range(SPANS_HERE):
        rows = pl.ds(span * SPAN, SPAN)
        terms = g[rows, :].astype(F32) * att_raw[pl.ds((span + 1) * SPAN, SPAN), :].astype(F32)
        for pair in range(2):
            start = pair * 256
            both = jnp.concatenate(
                [terms[:, start : start + 128], terms[:, start + 128 : start + 256]], axis=0
            )
            row = lax.dot_general(
                jnp.ones((8, 128), F32), both, (((1,), (1,)), ((), ())),
                precision=lax.Precision.HIGHEST, preferred_element_type=F32,
            )
            mine[2 + pair, pl.ds(span, 1), :] = row[:1]
    edge.wait()
    lead = att_raw[pl.ds(0, SPAN), :]
    att_raw[pl.ds(0, SPAN), :] = jnp.where(seq == 0, jnp.zeros_like(lead), lead)

    def put_att(block, value):
        att[head, pl.ds(pl.multiple_of(block * SPAN, SPAN), SPAN), :] = value

    shift_rows(att_raw, 1, put_att)
    y_ring = Ring("y", att.at[head], att, ROWS, y_sems, lambda place: 2 * place + c)

    def pair_copy(j):
        block = att.at[2 * y_ring.line.off(j) + c]
        return remote(block, block, pair_sems, j, sibling)

    y_ring.start(0)
    pair_copy(0).start()
    totals[z] = mine[...]
    total_copies = [
        remote(mine, totals.at[z], total_sems, d, z_peers[d]) for d in range(NZ - 1)
    ]
    for copy in total_copies:
        copy.start()
    own_w.wait()

    def use(block, first=False):
        rows = pl.ds(pl.multiple_of(block * WIDTH, WIDTH), WIDTH)
        term = jnp.dot(att[block], w_v[rows, :], preferred_element_type=F32)
        acc[...] = term if first else acc[...] + term
        terms = lax.dot_general(
            att[block], cot[...], (((0,), (0,)), ((), ())), preferred_element_type=F32
        ).astype(BF)
        to_x, part = block // 2, lax.rem(block, 2)
        wide[to_x, pl.ds(pl.multiple_of(part * WIDTH, WIDTH), WIDTH), :] = terms[:, :WIDE]
        for i in range(4):
            tall[part * 4 + i, pl.ds(pl.multiple_of(to_x * 128, 128), 128), :] = terms[
                i * 128 : (i + 1) * 128, WIDE:
            ]

    def wide_copy(apart):
        to = lax.rem(x + apart, NX)
        return remote(
            wide.at[to], wide_got.at[apart - 1], wide_sems, apart - 1, (to * NZ + z, head)
        )

    def send_wide(to):
        apart = lax.rem(to - x + NX, NX)

        @pl.when(apart != 0)
        def _():
            wide_copy(apart).start()

    use(head, True)
    g_ring.start(1)
    pair_copy(0).wait_recv()
    use(2 * y + 1 - c)
    send_wide(y)
    y_ring.start(1)
    y_ring.wait_others()
    pair_copy(1).start()
    pair_copy(3).start()
    for j in (1, 3, 2):
        if j == 2:
            g_ring.start(2)
            y_ring.wait_mains()
            pair_copy(2).start()
        came = y_ring.line.off(j)
        use(2 * came + c)
        pair_copy(j).wait_recv()
        use(2 * came + 1 - c)
        send_wide(came)
    g_ring.start(3)
    mixed[...] = acc[...].astype(BF)
    o_ring.wait_sends()
    y_ring.wait_sends()
    for copy in total_copies:
        copy.wait()
    for j in range(NY):
        pair_copy(j).wait_send()
    own_g.wait()
    for apart in range(1, NX):
        wide_copy(apart).wait()

    def add_wide(i, carry):
        rows = pl.ds(pl.multiple_of(i * 128, 128), 128)
        total = wide[x, rows, :].astype(F32)
        for d in range(NX - 1):
            total = total + wide_got[d, rows, :].astype(F32)
        wide_sum[i] = total.astype(BF)
        return carry

    lax.fori_loop(0, NZ, add_wide, 0)
    g_ring.finish()


def collect(o, lse, g, cot, w):
    def vm(*shape):
        return pltpu.VMEM(shape, BF)

    def sems(n):
        return pltpu.SemaphoreType.DMA((2, n))

    any_spec = pl.BlockSpec(memory_space=pl.ANY)
    vmem = pl.BlockSpec(memory_space=pltpu.VMEM)
    return pl.pallas_call(
        collect_kernel,
        out_shape=(
            jax.ShapeDtypeStruct((ROWS, WIDTH), BF),
            jax.ShapeDtypeStruct((NZ, 512, WIDTH - WIDE), BF),
            jax.ShapeDtypeStruct((NZ, 128, WIDE), BF),
            jax.ShapeDtypeStruct((NZ, ROWS, WIDTH), BF),
            jax.ShapeDtypeStruct((NZ, 4, 8, 128), F32),
        ),
        in_specs=[vmem] * 4 + [any_spec],
        out_specs=(vmem, vmem, vmem, any_spec, vmem),
        scratch_shapes=[
            vm(8 * WIDTH, WIDTH), vm(NX, 1024, WIDE), vm(NX - 1, 1024, WIDE),
            vm(2, 2, 4, ROWS, 256), pltpu.VMEM((2, 2, 4, 8, 128), F32),
            vm(2, 2, 4, ROWS, 256), pltpu.VMEM((2, 2, 4, 8, 128), F32),
            pltpu.VMEM((ROWS, 256), F32), vm(ROWS + SPAN, WIDTH), vm(8, ROWS, WIDTH),
            pltpu.VMEM((ROWS, WIDTH), F32), pltpu.VMEM((4, 8, 128), F32),
            pltpu.SemaphoreType.DMA((2,)), sems(16), sems(16), sems(14), sems(1), sems(4),
            sems(6), sems(7), sems(3),
        ],
        compiler_params=pltpu.CompilerParams(
            collective_id=2, has_side_effects=True, vmem_limit_bytes=VMEM_BYTES
        ),
        name="collect",
    )(o, lse, g, cot, w)


def finish_kernel(
    wide_sum, tall, keys, values,
    weight_grad, key_grad, value_grad,
    k_v, v_v, k_got, k_sums, v_got, v_sums,
    wide_z, tall_got, tall_sums, tall_sum, tall_x,
    local, k_sems, v_sems, wide_z_sems, tall_sems, tall_x_sems,
):
    seq, head, x, z, y, c = place()
    z_peers = [(x * NZ + lax.rem(z + d, NZ), head) for d in range(1, NZ)]
    x_peers = [(lax.rem(x + d, NX) * NZ + z, head) for d in range(1, NX)]
    own_k = pltpu.make_async_copy(keys, k_v, local.at[0])
    own_v = pltpu.make_async_copy(values, v_v, local.at[1])
    own_k.start()
    own_v.start()
    meet(z_peers + x_peers)
    tall_ring = RingSum("z", tall, 512, tall_got, tall_sums, tall_sems)
    tall_ring.start(0)

    own_k.wait()
    own_v.wait()
    k_ring = RingSum("x", k_v, 512, k_got, k_sums, k_sems)
    v_ring = RingSum("x", v_v, 512, v_got, v_sums, v_sems)
    k_ring.start(0)
    v_ring.start(0)
    tall_ring.start(1)
    tall_ring.start(2)
    k_ring.start(1)
    wide_z_copies = [
        remote(wide_sum.at[lax.rem(z + d + 1, NZ)], wide_z.at[d], wide_z_sems, d, z_peers[d])
        for d in range(NZ - 1)
    ]
    for copy in wide_z_copies:
        copy.start()
    tall_ring.start(3)
    v_ring.start(1)
    tall_ring.wait_last()

    def put_tall(rows, total):
        tall_sum[rows, :] = total.astype(BF)

    tall_ring.total(put_tall, lambda rows: tall[z, rows, :], 32)

    def x_rows(to):
        return pl.ds(pl.multiple_of(to * 128, 128), 128)

    tall_x_copies = [
        remote(
            tall_sum.at[x_rows(lax.rem(x + d + 1, NX))],
            tall_x.at[d], tall_x_sems, d, x_peers[d],
        )
        for d in range(NX - 1)
    ]
    for copy in tall_x_copies:
        copy.start()
    for ring, mine, out in ((k_ring, k_v, key_grad), (v_ring, v_v, value_grad)):
        ring.wait_last()

        def put(rows, total, out=out):
            out[rows, :] = total.astype(BF)

        ring.total(put, lambda rows, mine=mine: mine[x, rows, :], 32)
    for copy in wide_z_copies:
        copy.wait_recv()
    total = wide_sum[z].astype(F32)
    for d in range(NZ - 1):
        total = total + wide_z[d].astype(F32)
    weight_grad[:, :WIDE] = total.astype(BF)
    for copy in tall_x_copies:
        copy.wait_recv()
    total = tall_sum[x_rows(x), :].astype(F32)
    for d in range(NX - 1):
        total = total + tall_x[d].astype(F32)
    weight_grad[:, WIDE:] = total.astype(BF)
    for ring in (k_ring, v_ring, tall_ring):
        ring.wait_sends()
    for copy in wide_z_copies + tall_x_copies:
        copy.wait_send()


def finish(wide, tall_blocks, keys, values):
    def vm(*shape):
        return pltpu.VMEM(shape, BF)

    def sems(n):
        return pltpu.SemaphoreType.DMA((2, n))

    any_spec = pl.BlockSpec(memory_space=pl.ANY)
    vmem = pl.BlockSpec(memory_space=pltpu.VMEM)
    entry = (ENTRIES_HERE * KEYS, WIDTH)
    tall = WIDTH - WIDE
    return pl.pallas_call(
        finish_kernel,
        out_shape=(
            jax.ShapeDtypeStruct((128, WIDTH), BF),
            jax.ShapeDtypeStruct(entry, BF),
            jax.ShapeDtypeStruct(entry, BF),
        ),
        in_specs=[vmem] * 2 + [any_spec] * 2,
        out_specs=(vmem,) * 3,
        scratch_shapes=[
            vm(NX, *entry), vm(NX, *entry),
            vm(2, 2, 2, 256, WIDTH), vm(2, 2, 2, 256, WIDTH),
            vm(2, 2, 2, 256, WIDTH), vm(2, 2, 2, 256, WIDTH),
            vm(NZ - 1, 128, WIDE), vm(2, 2, 4, 256, tall), vm(2, 2, 4, 256, tall),
            vm(512, tall), vm(NX - 1, 128, tall),
            pltpu.SemaphoreType.DMA((2,)), sems(8), sems(8),
            sems(7), sems(16), sems(3),
        ],
        compiler_params=pltpu.CompilerParams(
            collective_id=3, has_side_effects=True, vmem_limit_bytes=VMEM_BYTES
        ),
        name="finish",
    )(wide, tall_blocks, keys, values)


def publish_kernel(*refs):
    for i in range(4):
        refs[4 + i][...] = refs[i][...]


def publish(*arrays):
    vmem = pl.BlockSpec(memory_space=pltpu.VMEM)
    return pl.pallas_call(
        publish_kernel,
        out_shape=tuple(jax.ShapeDtypeStruct(a.shape, a.dtype) for a in arrays),
        in_specs=[vmem] * 4,
        out_specs=(vmem,) * 4,
        name="publish",
    )(*arrays)


def body(queries, cache_keys, cache_values, owners, slots, out_weight, cotangent):
    codes = (owners * ENTRIES_HERE + slots).reshape(1, PAIRS)
    codes = jnp.pad(codes, ((0, 7), (0, 128 - PAIRS)))
    q, g, k, v, codes = gather_all(
        queries, cache_keys, cache_values, codes, cotangent, out_weight
    )
    q = q.reshape(NZ * SPANS_HERE, SPAN, WIDTH)
    k = k.reshape(NX * ENTRIES_HERE, KEYS, WIDTH)
    v = v.reshape(NX * ENTRIES_HERE, KEYS, WIDTH)
    out, lse = local_attention(codes, q, k, v)
    mixed, tall, wide, g_all, totals = collect(out, lse, g, cotangent, out_weight)
    key_terms, value_terms = local_grads(codes, q, k, v, g_all, totals)
    entries = (NX, ENTRIES_HERE * KEYS, WIDTH)
    weight_grad, key_grad, value_grad = finish(
        wide, tall, key_terms.reshape(entries), value_terms.reshape(entries)
    )
    mixed, weight_grad, key_grad, value_grad = publish(
        mixed, weight_grad, key_grad, value_grad
    )
    shape = (ENTRIES_HERE, KEYS, WIDTH)
    return mixed, weight_grad, key_grad.reshape(shape), value_grad.reshape(shape)


def solution(mesh):
    placed = (
        P("seq", "head"),
        P("seq", None, "head"),
        P("seq", None, "head"),
        P("seq", None),
        P("seq", None),
        P(None, "head"),
        P("seq", "head"),
    )
    return jax.shard_map(
        body,
        mesh=mesh,
        in_specs=placed,
        out_specs=(
            P("seq", "head"),
            P("seq", "head"),
            P("seq", None, "head"),
            P("seq", None, "head"),
        ),
        check_vma=False,
    )
```

```python
import functools
import math

import jax
import jax.numpy as jnp
from jax import lax
from jax.experimental import pallas as pl
from jax.experimental.pallas import tpu as pltpu
from jax.sharding import PartitionSpec as P

HEAD_DIM = 128
SPAN = 64
TOP = 2
NX, NZ, NY = 4, 8, 4
ROWS, WIDTH = 448, 512
SPANS_HERE = 7
PAIRS = SPANS_HERE * TOP
ENTRIES_HERE = 4
KEYS = 128
HALF = ROWS // 2
WIDE = 128
SCALE = 1.0 / math.sqrt(HEAD_DIM)
NEVER, HUGE = -1e30, 1e30
VMEM_BYTES = 56 * 1024 * 1024
MESH_ID = pl.DeviceIdType.MESH
BF, F32 = jnp.bfloat16, jnp.float32


def place():
    seq, head = lax.axis_index("seq"), lax.axis_index("head")
    return seq, head, seq // NZ, lax.rem(seq, NZ), head // 2, lax.rem(head, 2)


def remote(src, dst, sems, index, device):
    return pltpu.make_async_remote_copy(
        src_ref=src,
        dst_ref=dst,
        send_sem=sems.at[0, index],
        recv_sem=sems.at[1, index],
        device_id=device,
        device_id_type=MESH_ID,
    )


def meet(devices):
    sem = pltpu.get_barrier_semaphore()
    for device in devices:
        pl.semaphore_signal(sem, inc=1, device_id=device, device_id_type=MESH_ID)
    pl.semaphore_wait(sem, len(devices))


def selector(step):
    row = lax.broadcasted_iota(jnp.int32, (SPAN, 2 * SPAN), 0)
    column = lax.broadcasted_iota(jnp.int32, (SPAN, 2 * SPAN), 1)
    return (column == row + step).astype(F32).astype(BF)


def shift_rows(raw, step, write):
    pick = selector(step)

    def one(block, carry):
        window = raw[pl.ds(pl.multiple_of(block * SPAN, SPAN), 2 * SPAN), :]
        write(block, jnp.dot(pick, window, preferred_element_type=F32).astype(BF))
        return carry

    lax.fori_loop(0, SPANS_HERE, one, 0)


class Line:
    def __init__(self, axis):
        seq, head, x, z, y, c = place()
        if axis == "z":
            self.n, self.at, to = NZ, z, lambda i: (x * NZ + i, head)
        elif axis == "x":
            self.n, self.at, to = NX, x, lambda i: (i * NZ + z, head)
        else:
            self.n, self.at, to = NY, y, lambda i: (seq, 2 * i + c)
        self.half = self.n // 2
        self.beside = (to(self.off(1)), to(self.off(-1)))

    def off(self, steps):
        return lax.rem(self.at + steps + self.n, self.n)


class Ring:
    def __init__(self, axis, first, out, rows, sems, slot=lambda place: place):
        self.line, self.first, self.out, self.sems, self.slot = (
            Line(axis), first, out, sems, slot,
        )
        self.rows = rows // 2

    def copy(self, way, main, step):
        slot = self.slot(self.line.off(step if way else -step))
        half = way if main else 1 - way
        rows = pl.ds(half * self.rows, self.rows)
        dst = self.out.at[slot, rows]
        src = dst if step else self.first.at[rows]
        index = way * (self.line.n - 1) + (0 if main else self.line.half) + step
        return remote(src, dst, self.sems, index, self.line.beside[way])

    def start(self, step):
        for main in (True, False):
            if main or step < self.line.half - 1:
                for way in range(2):
                    if step:
                        self.copy(way, main, step - 1).wait_recv()
                    self.copy(way, main, step).start()

    def wait_others(self):
        for way in range(2):
            self.copy(way, False, self.line.half - 2).wait_recv()

    def wait_mains(self):
        for way in range(2):
            self.copy(way, True, self.line.half - 1).wait_recv()

    def wait_sends(self):
        for way in range(2):
            for step in range(self.line.half):
                self.copy(way, True, step).wait_send()
            for step in range(self.line.half - 1):
                self.copy(way, False, step).wait_send()

    def finish(self):
        self.wait_others()
        self.wait_mains()
        self.wait_sends()


class RingSum:
    def __init__(self, axis, blocks, rows, got, sums, sems):
        self.line = Line(axis)
        self.blocks, self.got, self.sums, self.sems = blocks, got, sums, sems
        self.rows = rows // 2

    def copy(self, way, main, step):
        half = way if main else 1 - way
        if step == (0 if main else 1):
            far = self.line.half - step
            block = self.line.off(-far if way else far)
            src = self.blocks.at[block, pl.ds(half * self.rows, self.rows)]
        else:
            src = self.sums.at[way, half, step]
        index = way * self.line.n + (0 if main else self.line.half) + step
        dst = self.got.at[way, half, step]
        return remote(src, dst, self.sems, index, self.line.beside[way])

    def send(self, way, main, step):
        half = way if main else 1 - way
        if step > (0 if main else 1):
            self.copy(way, main, step - 1).wait_recv()
            far = self.line.half - step
            block = self.line.off(-far if way else far)
            piece = 32

            def add(i, carry):
                rows = pl.ds(pl.multiple_of(i * piece, piece), piece)
                from_rows = pl.ds(pl.multiple_of(half * self.rows + i * piece, piece), piece)
                self.sums[way, half, step, rows, :] = (
                    self.blocks[block, from_rows, :].astype(F32)
                    + self.got[way, half, step - 1, rows, :].astype(F32)
                ).astype(BF)
                return carry

            lax.fori_loop(0, self.rows // piece, add, 0)
        self.copy(way, main, step).start()

    def start(self, step):
        for way in range(2):
            self.send(way, True, step)
        if step + 1 < self.line.half:
            for way in range(2):
                self.send(way, False, step + 1)

    def wait_last(self):
        for main in (False, True):
            for way in range(2):
                self.copy(way, main, self.line.half - 1).wait_recv()

    def wait_sends(self):
        for way in range(2):
            for step in range(self.line.half):
                self.copy(way, True, step).wait_send()
            for step in range(1, self.line.half):
                self.copy(way, False, step).wait_send()

    def total(self, write, mine, piece):
        for half in range(2):

            def one(i, carry):
                rows = pl.ds(pl.multiple_of(i * piece, piece), piece)
                at = pl.ds(pl.multiple_of(half * self.rows + i * piece, piece), piece)
                term = mine(at).astype(F32)
                for way in range(2):
                    term = term + self.got[way, half, self.line.half - 1, rows, :].astype(F32)
                write(at, term)
                return carry

            lax.fori_loop(0, self.rows // piece, one, 0)


def gather_kernel(
    q, k, v, codes, cot, w,
    q_all, g_own, k_all, v_all, codes_all,
    q_raw, q_sh, g_raw, g_sh, cot_v, w_v, part, pair_got, y_blocks, y_got, y_sums, g_acc,
    local, q_sems, k_sems, v_sems, code_sems, edge_sems, pair_sems, y_sems,
):
    seq, head, x, z, y, c = place()
    n_seq = NX * NZ
    before = (lax.rem(seq + n_seq - 1, n_seq), head)
    after = (lax.rem(seq + 1, n_seq), head)
    z_peers = [(x * NZ + lax.rem(z + d, NZ), head) for d in range(1, NZ)]
    sibling = (seq, 2 * y + 1 - c)
    own_q = pltpu.make_async_copy(q, q_raw.at[pl.ds(0, ROWS)], local.at[0])
    own_cot = pltpu.make_async_copy(cot, cot_v, local.at[1])
    own_w = pltpu.make_async_copy(w, w_v, local.at[2])
    own_q.start()
    own_cot.start()
    own_w.start()
    meet(
        z_peers + list(Line("x").beside) + list(Line("y").beside) + [sibling, before, after]
    )
    q_edge = remote(q.at[pl.ds(0, SPAN)], q_raw.at[pl.ds(ROWS, SPAN)], edge_sems, 0, before)
    q_edge.start()
    k_ring = Ring("x", k, k_all, ENTRIES_HERE, k_sems)
    v_ring = Ring("x", v, v_all, ENTRIES_HERE, v_sems)
    k_ring.start(0)
    v_ring.start(0)
    code_copies = [
        remote(codes, codes_all.at[z], code_sems, d, z_peers[d]) for d in range(NZ - 1)
    ]
    for copy in code_copies:
        copy.start()
    own_k = pltpu.make_async_copy(k, k_all.at[x], local.at[3])
    own_v = pltpu.make_async_copy(v, v_all.at[x], local.at[4])
    own_codes = pltpu.make_async_copy(codes, codes_all.at[z], local.at[5])
    own_k.start()
    own_v.start()
    own_codes.start()
    own_q.wait()
    q_edge.wait()
    last = seq == n_seq - 1
    tail = q_raw[pl.ds(ROWS, SPAN), :]
    q_raw[pl.ds(ROWS, SPAN), :] = jnp.where(last, jnp.zeros_like(tail), tail)

    def put_q(block, value):
        q_sh[pl.ds(pl.multiple_of(block * SPAN, SPAN), SPAN), :] = value

    shift_rows(q_raw, SPAN - 1, put_q)
    q_ring = Ring("z", q_sh, q_all, ROWS, q_sems)
    q_ring.start(0)
    keep_q = pltpu.make_async_copy(q_sh, q_all.at[z], local.at[6])
    keep_q.start()

    own_cot.wait()
    own_w.wait()

    def product(to_head):
        rows = pl.ds(pl.multiple_of(to_head * WIDTH, WIDTH), WIDTH)
        return lax.dot_general(
            cot_v[...], w_v[rows, :], (((1,), (1,)), ((), ())), preferred_element_type=F32
        )

    def pair_copy(j):
        return remote(part.at[j], pair_got.at[j], pair_sems, j, sibling)

    def for_sibling(i, carry):
        j = NY - 1 - i
        part[j] = product(2 * lax.rem(y + j, NY) + 1 - c).astype(BF)
        pair_copy(j).start()
        return carry

    lax.fori_loop(0, NY, for_sibling, 0)

    def for_row(i, carry):
        j = NY - 1 - i
        to = lax.rem(y + j, NY)
        value = product(2 * to + c)
        pair_copy(j).wait_recv()
        y_blocks[to] = (value + pair_got[j].astype(F32)).astype(BF)
        return carry

    lax.fori_loop(0, NY - 1, for_row, 0)
    y_ring = RingSum("y", y_blocks, ROWS, y_got, y_sums, y_sems)
    y_ring.start(0)
    mine = product(2 * y + c)
    pair_copy(0).wait_recv()
    g_acc[...] = mine + pair_got[0].astype(F32)
    q_ring.start(1)
    y_ring.start(1)
    k_ring.start(1)
    q_ring.start(2)
    v_ring.start(1)
    y_ring.wait_last()

    def put_g(rows, total):
        g_raw[rows, :] = total.astype(BF)

    y_ring.total(put_g, lambda rows: g_acc[rows, :], 32)
    g_edge = remote(
        g_raw.at[pl.ds(0, SPAN)], g_raw.at[pl.ds(ROWS, SPAN)], edge_sems, 1, before
    )
    g_edge.start()
    q_ring.start(3)
    g_edge.wait()
    tail = g_raw[pl.ds(ROWS, SPAN), :]
    g_raw[pl.ds(ROWS, SPAN), :] = jnp.where(last, jnp.zeros_like(tail), tail)

    def put_gs(block, value):
        g_sh[pl.ds(pl.multiple_of(block * SPAN, SPAN), SPAN), :] = value

    shift_rows(g_raw, SPAN - 1, put_gs)
    keep_g = pltpu.make_async_copy(g_sh, g_own, local.at[7])
    keep_g.start()
    q_ring.finish()
    k_ring.finish()
    v_ring.finish()
    for copy in code_copies:
        copy.wait()
    for j in range(NY):
        pair_copy(j).wait_send()
    y_ring.wait_sends()
    own_k.wait()
    own_v.wait()
    own_codes.wait()
    keep_q.wait()
    keep_g.wait()


def gather_all(q, k, v, codes, cot, w):
    def vm(*shape):
        return pltpu.VMEM(shape, BF)

    def sems(n):
        return pltpu.SemaphoreType.DMA((2, n))

    any_spec = pl.BlockSpec(memory_space=pl.ANY)
    entries = (NX, ENTRIES_HERE, KEYS, WIDTH)
    return pl.pallas_call(
        gather_kernel,
        out_shape=(
            jax.ShapeDtypeStruct((NZ, ROWS, WIDTH), BF),
            jax.ShapeDtypeStruct((ROWS, WIDTH), BF),
            jax.ShapeDtypeStruct(entries, BF),
            jax.ShapeDtypeStruct(entries, BF),
            jax.ShapeDtypeStruct((NZ, 8, 128), jnp.int32),
        ),
        in_specs=[any_spec] * 6,
        out_specs=(any_spec,) * 5,
        scratch_shapes=[
            vm(ROWS + SPAN, WIDTH), vm(ROWS, WIDTH), vm(ROWS + SPAN, WIDTH), vm(ROWS, WIDTH),
            vm(ROWS, WIDTH), vm(8 * WIDTH, WIDTH), vm(NY, ROWS, WIDTH), vm(NY, ROWS, WIDTH),
            vm(NY, ROWS, WIDTH), vm(2, 2, 2, HALF, WIDTH), vm(2, 2, 2, HALF, WIDTH),
            pltpu.VMEM((ROWS, WIDTH), F32),
            pltpu.SemaphoreType.DMA((8,)), sems(14), sems(6), sems(6), sems(7),
            sems(2), sems(4), sems(8),
        ],
        compiler_params=pltpu.CompilerParams(
            collective_id=0, has_side_effects=True, vmem_limit_bytes=VMEM_BYTES
        ),
        name="gather_all",
    )(q, k, v, codes, cot, w)


def two_heads(block):
    lane = lax.broadcasted_iota(jnp.int32, block.shape, 1)
    zero = jnp.zeros_like(block)
    upper = jnp.where(lane < HEAD_DIM, block, zero)
    lower = jnp.where(lane < HEAD_DIM, zero, block)
    return jnp.concatenate([upper, lower], axis=0)


def dot_t(a, b):
    return lax.dot_general(a, b, (((1,), (1,)), ((), ())), preferred_element_type=F32)


GROUP = 4


def list_live(codes, listed):
    z = lax.rem(lax.axis_index("seq"), NZ)

    def source(src, count):
        def pair(j, inner):
            code = codes[src, 0, j]
            entry = ((code >> 5) << 2) + (code & 3)
            listed[inner] = (src << 16) + ((j >> 1) << 8) + entry
            return inner + (((code >> 2) & (NZ - 1)) == z).astype(jnp.int32)

        return lax.fori_loop(0, PAIRS, pair, count)

    count = lax.fori_loop(0, NZ, source, 0)
    for i in range(GROUP - 1):
        listed[count + i] = listed[jnp.maximum(count - 1, 0)]
    return count


def each_live(count, listed, compute, commit):
    def group(i, carry):
        places, values = [], []
        for member in range(GROUP):
            at = GROUP * i + member
            packed = listed[at]
            places.append((packed >> 16, (packed >> 8) & 255, packed & 255))
            off = jnp.where(at < count, 0.0, HUGE).astype(F32)
            values.append(compute(*places[member], off))
        for member in range(GROUP):
            commit(*places[member], values[member])
        return carry

    lax.fori_loop(0, (count + GROUP - 1) // GROUP, group, 0)


LISTED = pltpu.SMEM((128,), jnp.int32)


def row_of(table, src, span, pair):
    here = lax.broadcasted_iota(jnp.int32, (8, 128), 0) == span
    block = table[src, pair]
    return jnp.sum(jnp.where(here, block, 0.0), axis=0, keepdims=True)


def attention_kernel(codes, q_in, k_in, v_in, o, stats, q, k, v, listed, loads):
    copies = [
        pltpu.make_async_copy(src, dst, loads.at[i])
        for i, (src, dst) in enumerate(((k_in, k), (q_in, q), (v_in, v)))
    ]
    for copy in copies:
        copy.start()
    stats[...] = jnp.full((NZ, 2, 8, 128), NEVER, F32)

    def clear(i, carry):
        for pair in range(2):
            o[i, pair] = jnp.zeros((ROWS, 256), BF)
        return carry

    lax.fori_loop(0, NZ, clear, 0)
    count = list_live(codes, listed)
    copies[0].wait()
    copies[1].wait()

    def scores_of(src, span, entry, pair):
        columns = pl.ds(pair * 256, 256)
        q2 = two_heads(q[src * SPANS_HERE + span, :, columns])
        return dot_t(k[entry, :, columns], q2) * SCALE

    def compute_lse(src, span, entry, off):
        found = []
        for pair in range(2):
            scores = scores_of(src, span, entry, pair)
            top = jnp.max(scores, axis=0, keepdims=True)
            lse = top + jnp.log(jnp.sum(jnp.exp(scores - top), axis=0, keepdims=True))
            found.append(jnp.where(off > 0.0, NEVER, lse))
        return found

    def commit_lse(src, span, entry, found):
        here = lax.broadcasted_iota(jnp.int32, (8, 128), 0) == span
        for pair, lse in enumerate(found):
            old = stats[src, pair]
            high = jnp.maximum(old, lse)
            both = high + jnp.log(jnp.exp(old - high) + jnp.exp(lse - high))
            stats[src, pair] = jnp.where(here, both, old)

    each_live(count, listed, compute_lse, commit_lse)
    copies[2].wait()

    def compute(src, span, entry, off):
        terms = []
        for pair in range(2):
            scores = scores_of(src, span, entry, pair)
            probs = jnp.exp(scores - (row_of(stats, src, span, pair) + off)).astype(BF)
            terms.append(
                lax.dot_general(
                    probs, v[entry, :, pl.ds(pair * 256, 256)], (((0,), (0,)), ((), ())),
                    preferred_element_type=F32,
                )
            )
        return terms

    def commit(src, span, entry, terms):
        rows = pl.ds(pl.multiple_of(span * SPAN, SPAN), SPAN)
        for pair in range(2):
            for head in range(2):
                at = pl.ds(head * 128, 128)
                term = terms[pair][head * SPAN : (head + 1) * SPAN, head * 128 : (head + 1) * 128]
                o[src, pair, rows, at] = (o[src, pair, rows, at].astype(F32) + term).astype(BF)

    each_live(count, listed, compute, commit)


def local_attention(codes, q, k, v):
    vmem = pl.BlockSpec(memory_space=pltpu.VMEM)
    entries = (NX * ENTRIES_HERE, KEYS, WIDTH)
    return pl.pallas_call(
        attention_kernel,
        out_shape=(
            jax.ShapeDtypeStruct((NZ, 2, ROWS, 256), BF),
            jax.ShapeDtypeStruct((NZ, 2, 8, 128), F32),
        ),
        in_specs=[pl.BlockSpec(memory_space=pltpu.SMEM)]
        + [pl.BlockSpec(memory_space=pl.ANY)] * 3,
        out_specs=(vmem, vmem),
        scratch_shapes=[
            pltpu.VMEM((NZ * SPANS_HERE, SPAN, WIDTH), BF),
            pltpu.VMEM(entries, BF), pltpu.VMEM(entries, BF),
            LISTED, pltpu.SemaphoreType.DMA((3,)),
        ],
        compiler_params=pltpu.CompilerParams(vmem_limit_bytes=VMEM_BYTES),
        name="local_attention",
    )(codes, q, k, v)


def grads_kernel(
    codes, q_in, k_in, v_in, g_in, totals, key_out, value_out,
    q, k, v, g, key_acc, value_acc, key_low, value_low, loads, stores, listed,
):
    copies = [
        pltpu.make_async_copy(src, dst, loads.at[i])
        for i, (src, dst) in enumerate(((q_in, q), (k_in, k), (v_in, v), (g_in, g)))
    ]
    for copy in copies:
        copy.start()

    def clear_acc(i, carry):
        key_acc[i] = jnp.zeros((KEYS, WIDTH), F32)
        value_acc[i] = jnp.zeros((KEYS, WIDTH), F32)
        return carry

    lax.fori_loop(0, NX * ENTRIES_HERE, clear_acc, 0)
    count = list_live(codes, listed)
    for copy in copies:
        copy.wait()

    def compute(src, span, entry, off):
        row = src * SPANS_HERE + span
        rows = pl.ds(pl.multiple_of(span * SPAN, SPAN), SPAN)
        terms = []
        for pair in range(2):
            columns = pl.ds(pair * 256, 256)
            q2 = two_heads(q[row, :, columns])
            g2 = two_heads(g[src, rows, columns])
            scores = dot_t(k[entry, :, columns], q2) * SCALE
            prob_grad = dot_t(v[entry, :, columns], g2)
            probs = jnp.exp(scores - (row_of(totals, src, span, pair) + off))
            delta = row_of(totals, src, span, 2 + pair)
            score_grad = (probs * (prob_grad - delta)).astype(BF)
            terms.append(
                (
                    jnp.dot(score_grad, q2, preferred_element_type=F32),
                    jnp.dot(probs.astype(BF), g2, preferred_element_type=F32),
                )
            )
        return terms

    def commit(src, span, entry, terms):
        for pair, (key_term, value_term) in enumerate(terms):
            columns = pl.ds(pair * 256, 256)
            key_acc[entry, :, columns] += key_term
            value_acc[entry, :, columns] += value_term

    each_live(count, listed, compute, commit)

    def store(i, which):
        low, to = ((key_low, key_out), (value_low, value_out))[which]
        return pltpu.make_async_copy(low.at[i], to.at[i], stores.at[which, i])

    def close(i, carry):
        key_low[i] = (key_acc[i] * SCALE).astype(BF)
        store(i, 0).start()
        value_low[i] = value_acc[i].astype(BF)
        store(i, 1).start()
        return carry

    def wait(i, carry):
        store(i, 0).wait()
        store(i, 1).wait()
        return carry

    lax.fori_loop(0, NX * ENTRIES_HERE, close, 0)
    lax.fori_loop(0, NX * ENTRIES_HERE, wait, 0)


def local_grads(codes, q, k, v, g, totals):
    entries = (NX * ENTRIES_HERE, KEYS, WIDTH)
    any_spec = pl.BlockSpec(memory_space=pl.ANY)
    vmem = pl.BlockSpec(memory_space=pltpu.VMEM)
    return pl.pallas_call(
        grads_kernel,
        out_shape=(jax.ShapeDtypeStruct(entries, BF),) * 2,
        in_specs=[pl.BlockSpec(memory_space=pltpu.SMEM)] + [any_spec] * 4 + [vmem],
        out_specs=(any_spec,) * 2,
        scratch_shapes=[
            pltpu.VMEM((NZ * SPANS_HERE, SPAN, WIDTH), BF),
            pltpu.VMEM(entries, BF), pltpu.VMEM(entries, BF),
            pltpu.VMEM((NZ, ROWS, WIDTH), BF),
            pltpu.VMEM(entries, F32), pltpu.VMEM(entries, F32),
            pltpu.VMEM(entries, BF), pltpu.VMEM(entries, BF),
            pltpu.SemaphoreType.DMA((4,)), pltpu.SemaphoreType.DMA((2, NX * ENTRIES_HERE)),
            LISTED,
        ],
        compiler_params=pltpu.CompilerParams(vmem_limit_bytes=VMEM_BYTES),
        name="local_grads",
    )(codes, q, k, v, g, totals)


def merge(first, second, write):
    (a_of, a_lse), (b_of, b_lse) = first, second
    high = jnp.maximum(a_lse, b_lse)
    a_part, b_part = jnp.exp(a_lse - high), jnp.exp(b_lse - high)
    both = a_part + b_part
    share = a_part / both
    upper = share.astype(BF).astype(F32)
    lower = share - upper
    row = lax.broadcasted_iota(jnp.int32, (128, 128), 0)
    column = lax.broadcasted_iota(jnp.int32, (128, 128), 1)
    ones = jnp.ones((256, 128), BF)
    for span in range(SPANS_HERE):
        spread = jnp.concatenate(
            [
                jnp.where(row == column, part[span : span + 1, :], 0.0).astype(BF)
                for part in (upper, lower)
            ],
            axis=1,
        )
        weight = jnp.dot(spread, ones, preferred_element_type=F32)
        weight = jnp.concatenate([weight[:SPAN], weight[SPAN:]], axis=1)
        rows = pl.ds(span * SPAN, SPAN)
        a, b = a_of(rows).astype(F32), b_of(rows).astype(F32)
        write(span, b + weight * (a - b))
    return high + jnp.log(both)


class RingMerge:
    def __init__(self, o, lse, got, lse_got, out, lse_out, sems, lse_sems):
        self.line = Line("z")
        self.o, self.lse, self.got, self.lse_got = o, lse, got, lse_got
        self.out, self.lse_out, self.sems, self.lse_sems = out, lse_out, sems, lse_sems

    def copies(self, way, main, step):
        half = way if main else 1 - way
        if step == (0 if main else 1):
            far = self.line.half - step
            block = self.line.off(-far if way else far)
            src, lse = self.o.at[block, half], self.lse.at[block, half]
        else:
            src, lse = self.out.at[way, half, step], self.lse_out.at[way, half, step]
        index = way * 8 + (0 if main else 4) + step
        to = self.line.beside[way]
        return (
            remote(src, self.got.at[way, half, step], self.sems, index, to),
            remote(lse, self.lse_got.at[way, half, step], self.lse_sems, index, to),
        )

    def wait(self, way, main, step):
        for copy in self.copies(way, main, step):
            copy.wait_recv()

    def arrived(self, way, half, step):
        return (lambda rows: self.got[way, half, step, rows, :], self.lse_got[way, half, step])

    def held(self, block, half):
        return (lambda rows: self.o[block, half, rows, :], self.lse[block, half])

    def send(self, way, main, step):
        half = way if main else 1 - way
        if step > (0 if main else 1):
            self.wait(way, main, step - 1)
            far = self.line.half - step
            block = self.line.off(-far if way else far)

            def write(span, value):
                self.out[way, half, step, pl.ds(span * SPAN, SPAN), :] = value.astype(BF)

            self.lse_out[way, half, step] = merge(
                self.arrived(way, half, step - 1), self.held(block, half), write
            )
        for copy in self.copies(way, main, step):
            copy.start()

    def start(self, step):
        for way in range(2):
            self.send(way, True, step)
        if step + 1 < self.line.half:
            for way in range(2):
                self.send(way, False, step + 1)

    def finish(self, half, middle, write):
        for way in range(2):
            self.wait(way, half == way, 3)

        def keep(span, value):
            middle[pl.ds(span * SPAN, SPAN), :] = value

        lse = merge(self.arrived(0, half, 3), self.arrived(1, half, 3), keep)
        return merge(
            (lambda rows: middle[rows, :], lse), self.held(self.line.at, half), write
        )

    def wait_sends(self):
        for way in range(2):
            for main in (True, False):
                for step in range(0 if main else 1, 4):
                    for copy in self.copies(way, main, step):
                        copy.wait_send()


def collect_kernel(
    o, lse, g, cot, w,
    mixed, tall, wide_sum, g_all, totals,
    w_v, wide, wide_got, o_got, lse_got, o_out, lse_out, middle, att_raw, att, acc, mine,
    local, o_sems, lse_sems, g_sems, edge_sems, pair_sems, y_sems, total_sems, wide_sems,
):
    seq, head, x, z, y, c = place()
    n_seq = NX * NZ
    before = (lax.rem(seq + n_seq - 1, n_seq), head)
    after = (lax.rem(seq + 1, n_seq), head)
    z_peers = [(x * NZ + lax.rem(z + d, NZ), head) for d in range(1, NZ)]
    x_peers = [(lax.rem(x + d, NX) * NZ + z, head) for d in range(1, NX)]
    sibling = (seq, 2 * y + 1 - c)
    own_w = pltpu.make_async_copy(w, w_v, local.at[0])
    own_g = pltpu.make_async_copy(g, g_all.at[z], local.at[1])
    own_w.start()
    own_g.start()
    meet(z_peers + x_peers + list(Line("y").beside) + [sibling, before, after])
    o_ring = RingMerge(o, lse, o_got, lse_got, o_out, lse_out, o_sems, lse_sems)
    for step in range(4):
        o_ring.start(step)
    g_ring = Ring("z", g, g_all, ROWS, g_sems)
    g_ring.start(0)
    for half in range(2):

        def put_out(span, value):
            att_raw[pl.ds((span + 1) * SPAN, SPAN), pl.ds(half * 256, 256)] = value.astype(BF)

        mine[half] = o_ring.finish(half, middle, put_out)
    edge = remote(
        att_raw.at[pl.ds(ROWS, SPAN)], att_raw.at[pl.ds(0, SPAN)], edge_sems, 0, after
    )
    edge.start()
    mine[2] = jnp.zeros((8, 128), F32)
    mine[3] = jnp.zeros((8, 128), F32)
    for span in range(SPANS_HERE):
        rows = pl.ds(span * SPAN, SPAN)
        terms = g[rows, :].astype(F32) * att_raw[pl.ds((span + 1) * SPAN, SPAN), :].astype(F32)
        for pair in range(2):
            start = pair * 256
            both = jnp.concatenate(
                [terms[:, start : start + 128], terms[:, start + 128 : start + 256]], axis=0
            )
            row = lax.dot_general(
                jnp.ones((8, 128), F32), both, (((1,), (1,)), ((), ())),
                precision=lax.Precision.HIGHEST, preferred_element_type=F32,
            )
            mine[2 + pair, pl.ds(span, 1), :] = row[:1]
    edge.wait()
    lead = att_raw[pl.ds(0, SPAN), :]
    att_raw[pl.ds(0, SPAN), :] = jnp.where(seq == 0, jnp.zeros_like(lead), lead)

    def put_att(block, value):
        att[head, pl.ds(pl.multiple_of(block * SPAN, SPAN), SPAN), :] = value

    shift_rows(att_raw, 1, put_att)
    y_ring = Ring("y", att.at[head], att, ROWS, y_sems, lambda place: 2 * place + c)

    def pair_copy(j):
        block = att.at[2 * y_ring.line.off(j) + c]
        return remote(block, block, pair_sems, j, sibling)

    y_ring.start(0)
    pair_copy(0).start()
    totals[z] = mine[...]
    total_copies = [
        remote(mine, totals.at[z], total_sems, d, z_peers[d]) for d in range(NZ - 1)
    ]
    for copy in total_copies:
        copy.start()
    own_w.wait()

    def use(block, first=False):
        rows = pl.ds(pl.multiple_of(block * WIDTH, WIDTH), WIDTH)
        term = jnp.dot(att[block], w_v[rows, :], preferred_element_type=F32)
        acc[...] = term if first else acc[...] + term
        terms = lax.dot_general(
            att[block], cot[...], (((0,), (0,)), ((), ())), preferred_element_type=F32
        ).astype(BF)
        to_x, part = block // 2, lax.rem(block, 2)
        wide[to_x, pl.ds(pl.multiple_of(part * WIDTH, WIDTH), WIDTH), :] = terms[:, :WIDE]
        for i in range(4):
            tall[part * 4 + i, pl.ds(pl.multiple_of(to_x * 128, 128), 128), :] = terms[
                i * 128 : (i + 1) * 128, WIDE:
            ]

    def wide_copy(apart):
        to = lax.rem(x + apart, NX)
        return remote(
            wide.at[to], wide_got.at[apart - 1], wide_sems, apart - 1, (to * NZ + z, head)
        )

    def send_wide(to):
        apart = lax.rem(to - x + NX, NX)

        @pl.when(apart != 0)
        def _():
            wide_copy(apart).start()

    g_ring.start(1)
    use(head, True)
    pair_copy(0).wait_recv()
    use(2 * y + 1 - c)
    send_wide(y)
    y_ring.start(1)
    y_ring.wait_others()
    pair_copy(1).start()
    pair_copy(3).start()
    g_ring.start(2)
    for j in (1, 3, 2):
        if j == 2:
            g_ring.start(3)
            y_ring.wait_mains()
            pair_copy(2).start()
        came = y_ring.line.off(j)
        use(2 * came + c)
        pair_copy(j).wait_recv()
        use(2 * came + 1 - c)
        send_wide(came)
    mixed[...] = acc[...].astype(BF)
    o_ring.wait_sends()
    y_ring.wait_sends()
    for copy in total_copies:
        copy.wait()
    for j in range(NY):
        pair_copy(j).wait_send()
    own_g.wait()
    for apart in range(1, NX):
        wide_copy(apart).wait()

    def add_wide(i, carry):
        rows = pl.ds(pl.multiple_of(i * 128, 128), 128)
        total = wide[x, rows, :].astype(F32)
        for d in range(NX - 1):
            total = total + wide_got[d, rows, :].astype(F32)
        wide_sum[i] = total.astype(BF)
        return carry

    lax.fori_loop(0, NZ, add_wide, 0)
    g_ring.finish()


def collect(o, lse, g, cot, w):
    def vm(*shape):
        return pltpu.VMEM(shape, BF)

    def sems(n):
        return pltpu.SemaphoreType.DMA((2, n))

    any_spec = pl.BlockSpec(memory_space=pl.ANY)
    vmem = pl.BlockSpec(memory_space=pltpu.VMEM)
    return pl.pallas_call(
        collect_kernel,
        out_shape=(
            jax.ShapeDtypeStruct((ROWS, WIDTH), BF),
            jax.ShapeDtypeStruct((NZ, 512, WIDTH - WIDE), BF),
            jax.ShapeDtypeStruct((NZ, 128, WIDE), BF),
            jax.ShapeDtypeStruct((NZ, ROWS, WIDTH), BF),
            jax.ShapeDtypeStruct((NZ, 4, 8, 128), F32),
        ),
        in_specs=[vmem] * 4 + [any_spec],
        out_specs=(vmem, vmem, vmem, any_spec, vmem),
        scratch_shapes=[
            vm(8 * WIDTH, WIDTH), vm(NX, 1024, WIDE), vm(NX - 1, 1024, WIDE),
            vm(2, 2, 4, ROWS, 256), pltpu.VMEM((2, 2, 4, 8, 128), F32),
            vm(2, 2, 4, ROWS, 256), pltpu.VMEM((2, 2, 4, 8, 128), F32),
            pltpu.VMEM((ROWS, 256), F32), vm(ROWS + SPAN, WIDTH), vm(8, ROWS, WIDTH),
            pltpu.VMEM((ROWS, WIDTH), F32), pltpu.VMEM((4, 8, 128), F32),
            pltpu.SemaphoreType.DMA((2,)), sems(16), sems(16), sems(14), sems(1), sems(4),
            sems(6), sems(7), sems(3),
        ],
        compiler_params=pltpu.CompilerParams(
            collective_id=2, has_side_effects=True, vmem_limit_bytes=VMEM_BYTES
        ),
        name="collect",
    )(o, lse, g, cot, w)


def finish_kernel(
    wide_sum, tall, keys, values,
    weight_grad, key_grad, value_grad,
    k_v, v_v, k_got, k_sums, v_got, v_sums,
    wide_z, tall_got, tall_sums, tall_sum, tall_x,
    local, k_sems, v_sems, wide_z_sems, tall_sems, tall_x_sems,
):
    seq, head, x, z, y, c = place()
    z_peers = [(x * NZ + lax.rem(z + d, NZ), head) for d in range(1, NZ)]
    x_peers = [(lax.rem(x + d, NX) * NZ + z, head) for d in range(1, NX)]
    own_k = pltpu.make_async_copy(keys, k_v, local.at[0])
    own_v = pltpu.make_async_copy(values, v_v, local.at[1])
    own_k.start()
    own_v.start()
    meet(z_peers + x_peers)
    tall_ring = RingSum("z", tall, 512, tall_got, tall_sums, tall_sems)
    tall_ring.start(0)

    own_k.wait()
    own_v.wait()
    k_ring = RingSum("x", k_v, 512, k_got, k_sums, k_sems)
    v_ring = RingSum("x", v_v, 512, v_got, v_sums, v_sems)
    k_ring.start(0)
    v_ring.start(0)
    tall_ring.start(1)
    tall_ring.start(2)
    k_ring.start(1)
    wide_z_copies = [
        remote(wide_sum.at[lax.rem(z + d + 1, NZ)], wide_z.at[d], wide_z_sems, d, z_peers[d])
        for d in range(NZ - 1)
    ]
    for copy in wide_z_copies:
        copy.start()
    tall_ring.start(3)
    v_ring.start(1)
    tall_ring.wait_last()

    def put_tall(rows, total):
        tall_sum[rows, :] = total.astype(BF)

    tall_ring.total(put_tall, lambda rows: tall[z, rows, :], 32)

    def x_rows(to):
        return pl.ds(pl.multiple_of(to * 128, 128), 128)

    tall_x_copies = [
        remote(
            tall_sum.at[x_rows(lax.rem(x + d + 1, NX))],
            tall_x.at[d], tall_x_sems, d, x_peers[d],
        )
        for d in range(NX - 1)
    ]
    for copy in tall_x_copies:
        copy.start()
    for ring, mine, out in ((k_ring, k_v, key_grad), (v_ring, v_v, value_grad)):
        ring.wait_last()

        def put(rows, total, out=out):
            out[rows, :] = total.astype(BF)

        ring.total(put, lambda rows, mine=mine: mine[x, rows, :], 32)
    for copy in wide_z_copies:
        copy.wait_recv()
    total = wide_sum[z].astype(F32)
    for d in range(NZ - 1):
        total = total + wide_z[d].astype(F32)
    weight_grad[:, :WIDE] = total.astype(BF)
    for copy in tall_x_copies:
        copy.wait_recv()
    total = tall_sum[x_rows(x), :].astype(F32)
    for d in range(NX - 1):
        total = total + tall_x[d].astype(F32)
    weight_grad[:, WIDE:] = total.astype(BF)
    for ring in (k_ring, v_ring, tall_ring):
        ring.wait_sends()
    for copy in wide_z_copies + tall_x_copies:
        copy.wait_send()


def finish(wide, tall_blocks, keys, values):
    def vm(*shape):
        return pltpu.VMEM(shape, BF)

    def sems(n):
        return pltpu.SemaphoreType.DMA((2, n))

    any_spec = pl.BlockSpec(memory_space=pl.ANY)
    vmem = pl.BlockSpec(memory_space=pltpu.VMEM)
    entry = (ENTRIES_HERE * KEYS, WIDTH)
    tall = WIDTH - WIDE
    return pl.pallas_call(
        finish_kernel,
        out_shape=(
            jax.ShapeDtypeStruct((128, WIDTH), BF),
            jax.ShapeDtypeStruct(entry, BF),
            jax.ShapeDtypeStruct(entry, BF),
        ),
        in_specs=[vmem] * 2 + [any_spec] * 2,
        out_specs=(vmem,) * 3,
        scratch_shapes=[
            vm(NX, *entry), vm(NX, *entry),
            vm(2, 2, 2, 256, WIDTH), vm(2, 2, 2, 256, WIDTH),
            vm(2, 2, 2, 256, WIDTH), vm(2, 2, 2, 256, WIDTH),
            vm(NZ - 1, 128, WIDE), vm(2, 2, 4, 256, tall), vm(2, 2, 4, 256, tall),
            vm(512, tall), vm(NX - 1, 128, tall),
            pltpu.SemaphoreType.DMA((2,)), sems(8), sems(8),
            sems(7), sems(16), sems(3),
        ],
        compiler_params=pltpu.CompilerParams(
            collective_id=3, has_side_effects=True, vmem_limit_bytes=VMEM_BYTES
        ),
        name="finish",
    )(wide, tall_blocks, keys, values)


def publish_kernel(*refs):
    for i in range(4):
        refs[4 + i][...] = refs[i][...]


def publish(*arrays):
    vmem = pl.BlockSpec(memory_space=pltpu.VMEM)
    return pl.pallas_call(
        publish_kernel,
        out_shape=tuple(jax.ShapeDtypeStruct(a.shape, a.dtype) for a in arrays),
        in_specs=[vmem] * 4,
        out_specs=(vmem,) * 4,
        name="publish",
    )(*arrays)


def body(queries, cache_keys, cache_values, owners, slots, out_weight, cotangent):
    codes = (owners * ENTRIES_HERE + slots).reshape(1, PAIRS)
    codes = jnp.pad(codes, ((0, 7), (0, 128 - PAIRS)))
    q, g, k, v, codes = gather_all(
        queries, cache_keys, cache_values, codes, cotangent, out_weight
    )
    q = q.reshape(NZ * SPANS_HERE, SPAN, WIDTH)
    k = k.reshape(NX * ENTRIES_HERE, KEYS, WIDTH)
    v = v.reshape(NX * ENTRIES_HERE, KEYS, WIDTH)
    out, lse = local_attention(codes, q, k, v)
    mixed, tall, wide, g_all, totals = collect(out, lse, g, cotangent, out_weight)
    key_terms, value_terms = local_grads(codes, q, k, v, g_all, totals)
    entries = (NX, ENTRIES_HERE * KEYS, WIDTH)
    weight_grad, key_grad, value_grad = finish(
        wide, tall, key_terms.reshape(entries), value_terms.reshape(entries)
    )
    mixed, weight_grad, key_grad, value_grad = publish(
        mixed, weight_grad, key_grad, value_grad
    )
    shape = (ENTRIES_HERE, KEYS, WIDTH)
    return mixed, weight_grad, key_grad.reshape(shape), value_grad.reshape(shape)


def solution(mesh):
    placed = (
        P("seq", "head"),
        P("seq", None, "head"),
        P("seq", None, "head"),
        P("seq", None),
        P("seq", None),
        P(None, "head"),
        P("seq", "head"),
    )
    return jax.shard_map(
        body,
        mesh=mesh,
        in_specs=placed,
        out_specs=(
            P("seq", "head"),
            P("seq", "head"),
            P("seq", None, "head"),
            P("seq", None, "head"),
        ),
        check_vma=False,
    )
```
